32 devices in a mesh: grp: 2 (over y), ex: 4 (over z), lay: 2 (over x), sub: 2 (over core).
Axes of the slice: x: 2, y: 2, z: 4, core: 2. Of those that a mesh axis runs over, the one named last changes fastest.
Arguments:
- layer_inputs: bfloat16 [2, 2048, 4096], P('lay', ('grp', 'ex'), 'sub'), parts along dimension 1, may hold values from -6 to 6
- output_grads: bfloat16 [2, 2048, 4096], P('lay', ('grp', 'ex'), 'sub'), parts along dimension 1, may hold values from -0.59765625 to 0.59765625
- basis_in: bfloat16 [2, 32, 4096], P('lay', None, 'sub'), may hold values from -0.09375 to 0.09375
- basis_out: bfloat16 [2, 32, 4096], P('lay', None, 'sub'), may hold values from -0.09375 to 0.09375
- queries: bfloat16 [2, 64, 1024], P('lay', 'ex', 'sub'), may hold values from -0.1875 to 0.1875
Outputs:
- gram: float32 [4, 1024, 1024], P(('grp', 'lay'), 'ex', 'sub'), parts along dimension 0
- scores: float32 [32, 64], P(('grp', 'ex'), ('lay', 'sub')), parts along dimension 0
The draws below stay inside these ranges and needn't reach their ends.
There are 2 independent parts, one for each index of `grp`. The reference program is written for one: setup_inputs(seed, part) draws one part's arguments, and reference() takes and returns one part's arrays. A program takes and returns all parts, laid end to end along the dimension named above; an argument that names none is the same for every part. Nothing has to cross between parts.
All inputs are finite; a program needn't handle non-finite values.
Results may differ from the reference program's by a relative error of at most 0.0003.
Values may be sent and summed in bfloat16 or wider, within the bound.
No kernel may reach another device: no remote copies, remote signals or barrier semaphores. Data moves between devices by JAX's collectives and lax.ppermute only.
A program may use at most 64 MiB of HBM per device.

```python
import jax
import jax.numpy as jnp
from jax import lax

D = 4096
RANK = 32
PROJ = 1024
LEN = 64
LAYERS = 2
EXAMPLES = 16
TOKENS = 1024
NQ = 64


def shard_levels(key, extent, cuts, least, top_value):
    factor_of, own = 1.0, jax.random.fold_in(key, 6)
    for axis_at, blocks in cuts:
        heights = jnp.exp(jax.random.uniform(jax.random.fold_in(own, axis_at), (blocks,), jnp.float32, least / len(cuts), top_value / len(cuts)))
        factor_of = factor_of * jnp.repeat(heights, extent[axis_at] // blocks).reshape([-1 if axis == axis_at else 1 for axis in range(len(extent))])
    return factor_of


def normal_values(own_key, shape, scale, reach, cuts=(), dtype=jnp.bfloat16):
    gain = shard_levels(own_key, shape, cuts, -0.22, 0.18) if cuts else 1.0
    result = jax.random.normal(own_key, shape, jnp.float32) * scale * gain
    return jnp.minimum(jnp.maximum(result, -reach), reach).astype(dtype)


def setup_inputs(seed: int = 0, part: int = 0) -> dict:
    arg_keys = jax.random.split(jax.random.key(seed), 6)
    part_splits = jax.random.split(jax.random.fold_in(arg_keys[5], part), 6)
    layer_inputs = normal_values(part_splits[0], (LAYERS, TOKENS, D), 1.0, 6.0, ((0, 2), (1, 4), (2, 2)))
    output_grads = normal_values(part_splits[1], (LAYERS, TOKENS, D), 0.1, 0.59765625, ((0, 2), (1, 4), (2, 2)))
    basis_in = normal_values(arg_keys[2], (LAYERS, RANK, D), D ** -0.5, 0.09375, ((0, 2), (2, 2)))
    basis_out = normal_values(arg_keys[3], (LAYERS, RANK, D), D ** -0.5, 0.09375, ((0, 2), (2, 2)))
    queries = normal_values(arg_keys[4], (LAYERS, NQ, PROJ), PROJ ** -0.5, 0.1875, ((0, 2), (1, 4), (2, 2)))
    return {"layer_inputs": layer_inputs, "output_grads": output_grads, "basis_in": basis_in, "basis_out": basis_out, "queries": queries}


def reference(layer_inputs, output_grads, basis_in, basis_out, queries):
    contract = (((1,), (1,)), ((), ()))
    gram_list = []
    scores = jnp.zeros((EXAMPLES, NQ), jnp.float32)
    for layer_index in range(LAYERS):
        proj_x = lax.dot_general(basis_in[layer_index], layer_inputs[layer_index], contract, preferred_element_type=jnp.float32)
        proj_g = lax.dot_general(basis_out[layer_index], output_grads[layer_index], contract, preferred_element_type=jnp.float32)
        grads = jnp.einsum("ael,bel->eab", proj_g.reshape(RANK, EXAMPLES, LEN), proj_x.reshape(RANK, EXAMPLES, LEN), precision=lax.Precision.HIGHEST).reshape(EXAMPLES, PROJ)
        gram_list.append(jnp.dot(grads.T, grads, precision=lax.Precision.HIGHEST) / EXAMPLES)
        scores = scores + jnp.dot(grads, queries[layer_index].astype(jnp.float32).T, precision=lax.Precision.HIGHEST)
    return jnp.stack(gram_list), scores
```

```python
import jax
import jax.numpy as jnp
from jax import lax
from jax.sharding import PartitionSpec as P

LEN = 64
HIGHEST = lax.Precision.HIGHEST


def solution(mesh):
    n_ex, n_lay, n_sub = mesh.shape["ex"], mesh.shape["lay"], mesh.shape["sub"]
    n_blk = n_lay * n_sub
    per_blk = n_ex // n_blk

    def flat(ex, lay, sub):
        return (ex * n_lay + lay) * n_sub + sub

    def query_round(k):
        pairs = []
        for ex in range(n_ex):
            at = (ex + k) % n_ex
            for blk in range(n_blk):
                source = flat(blk * per_blk + at // n_blk, (at % n_blk) // n_sub, at % n_sub)
                pairs.append((source, flat(ex, blk // n_sub, blk % n_sub)))
        return pairs

    def rotate(value, axis, size, k):
        return lax.ppermute(value, axis, [((i + k) % size, i) for i in range(size)])

    def body(layer_inputs, output_grads, basis_in, basis_out, queries):
        ex, lay, sub = lax.axis_index("ex"), lax.axis_index("lay"), lax.axis_index("sub")
        got = jnp.stack([lax.ppermute(queries[0], ("ex", "lay", "sub"), query_round(k)) for k in range(n_ex)])
        got = jnp.roll(got, ex, axis=0)
        rows, half = queries.shape[1:]
        got = got.reshape(per_blk, n_lay, n_sub, rows, half).transpose(1, 0, 3, 2, 4)
        got = got.reshape(n_lay, per_blk * rows, n_sub * half).astype(jnp.float32)

        contract = (((1,), (1,)), ((), ()))
        proj_x = lax.dot_general(basis_in[0], layer_inputs[0], contract, preferred_element_type=jnp.float32)
        proj_g = lax.dot_general(basis_out[0], output_grads[0], contract, preferred_element_type=jnp.float32)
        proj = jnp.stack([proj_x, proj_g])
        total = proj
        for k in range(1, n_sub):
            total = total + rotate(proj, "sub", n_sub, k)
        basis = basis_in.shape[1]
        own = layer_inputs.shape[1] // LEN
        width = basis * basis
        total = total.reshape(2, basis, own, LEN)
        grads = jnp.einsum("ael,bel->eab", total[1], total[0], precision=HIGHEST).reshape(own, width)

        gathered = jnp.concatenate([grads] + [rotate(grads, "ex", n_ex, k) for k in range(1, n_ex)])
        scores = 0.0
        for k in range(n_lay):
            other = rotate(grads, "lay", n_lay, k) if k else grads
            here = lax.dynamic_index_in_dim(got, (lay + k) % n_lay, 0, keepdims=False)
            scores = scores + jnp.dot(other, here.T, precision=HIGHEST)
        n_rows, n_cols = width // n_ex, width // n_sub
        left = lax.dynamic_slice_in_dim(gathered, ex * n_rows, n_rows, 1)
        right = lax.dynamic_slice_in_dim(gathered, sub * n_cols, n_cols, 1)
        gram = jnp.dot(left.T, right, precision=HIGHEST) / (own * n_ex)
        return gram[None], scores

    in_specs = (
        P("lay", ("grp", "ex"), "sub"),
        P("lay", ("grp", "ex"), "sub"),
        P("lay", None, "sub"),
        P("lay", None, "sub"),
        P("lay", "ex", "sub"),
    )
    out_specs = (P(("grp", "lay"), "ex", "sub"), P(("grp", "ex"), ("lay", "sub")))
    return jax.shard_map(body, mesh=mesh, in_specs=in_specs, out_specs=out_specs, check_vma=False)
```

```python
import jax
import jax.numpy as jnp
from jax import lax
from jax.sharding import PartitionSpec as P

LEN = 64
HIGHEST = lax.Precision.HIGHEST


def solution(mesh):
    n_ex, n_lay, n_sub = mesh.shape["ex"], mesh.shape["lay"], mesh.shape["sub"]

    def to_all(value, axes):
        return lax.all_to_all(value, axes, 0, 0, tiled=False)

    def body(layer_inputs, output_grads, basis_in, basis_out, queries):
        ex, sub = lax.axis_index("ex"), lax.axis_index("sub")
        contract = (((1,), (1,)), ((), ()))
        proj_x = lax.dot_general(basis_in[0], layer_inputs[0], contract, preferred_element_type=jnp.float32)
        proj_g = lax.dot_general(basis_out[0], output_grads[0], contract, preferred_element_type=jnp.float32)
        proj = jnp.stack([proj_x, proj_g])
        total = proj
        for k in range(1, n_sub):
            total = total + lax.ppermute(proj, "sub", [((i + k) % n_sub, i) for i in range(n_sub)])
        basis = basis_in.shape[1]
        own = layer_inputs.shape[1] // LEN
        width = basis * basis
        n_rows, n_cols = width // n_ex, width // n_sub
        total = total.reshape(2, basis, own, LEN)
        grads = jnp.einsum("ael,bel->eab", total[1], total[0], precision=HIGHEST).reshape(own, width)
        rounded = lax.reduce_precision(grads, 8, 7)
        high = rounded.astype(jnp.bfloat16)
        low = (grads - rounded).astype(jnp.bfloat16)

        rows = queries.shape[1]
        sent = jnp.concatenate([high, low, queries[0].reshape(-1, width)])
        got = to_all(jnp.broadcast_to(sent, (n_ex, *sent.shape)), "ex")
        all_queries = got[:, 2 * own :].reshape(n_ex * rows, n_cols)
        own_cols = lax.dynamic_slice_in_dim(grads, sub * n_cols, n_cols, 1)
        partial = jnp.dot(own_cols, all_queries.astype(jnp.float32).T, precision=HIGHEST)
        partial = partial.reshape(own, n_lay * n_sub, -1).swapaxes(0, 1)
        scores = to_all(partial, ("lay", "sub")).sum(0)

        high = got[:, :own].reshape(-1, width)
        low = got[:, own : 2 * own].reshape(-1, width)
        left = lax.dynamic_slice_in_dim(jnp.concatenate([high, low, high]), ex * n_rows, n_rows, 1)
        right = lax.dynamic_slice_in_dim(jnp.concatenate([high, high, low]), sub * n_cols, n_cols, 1)
        gram = jnp.dot(left.T, right, preferred_element_type=jnp.float32) / (own * n_ex)
        return gram[None], scores

    in_specs = (
        P("lay", ("grp", "ex"), "sub"),
        P("lay", ("grp", "ex"), "sub"),
        P("lay", None, "sub"),
        P("lay", None, "sub"),
        P("lay", "ex", "sub"),
    )
    out_specs = (P(("grp", "lay"), "ex", "sub"), P(("grp", "ex"), ("lay", "sub")))
    return jax.shard_map(body, mesh=mesh, in_specs=in_specs, out_specs=out_specs, check_vma=False)
```

```python
import functools

import jax
import jax.numpy as jnp
from jax import lax
from jax.experimental import pallas as pl
from jax.experimental.pallas import tpu as pltpu
from jax.sharding import PartitionSpec as P

LEN = 64
CHUNKS = 4
F32, BF16 = jnp.float32, jnp.bfloat16
VMEM = pl.BlockSpec(memory_space=pltpu.VMEM)
ANY = pl.BlockSpec(memory_space=pl.ANY)
LAST = (((1,), (1,)), ((), ()))
FIRST = (((0,), (0,)), ((), ()))


def project_kernel(x_ref, g_ref, bi_ref, bo_ref, out_ref, x_buf, g_buf, bi_buf, bo_buf, sems):
    step = x_buf.shape[2]
    copies = [
        pltpu.make_async_copy(bi_ref.at[0], bi_buf, sems.at[0]),
        pltpu.make_async_copy(bo_ref.at[0], bo_buf, sems.at[1]),
    ]
    for k in range(CHUNKS):
        cols = pl.ds(k * step, step)
        copies.append(pltpu.make_async_copy(x_ref.at[0, :, cols], x_buf.at[k], sems.at[2 + 2 * k]))
        copies.append(pltpu.make_async_copy(g_ref.at[0, :, cols], g_buf.at[k], sems.at[3 + 2 * k]))
    for copy in copies:
        copy.start()
    copies[0].wait()
    copies[1].wait()
    total = None
    for k in range(CHUNKS):
        cols = pl.ds(k * step, step)
        bi, bo = bi_buf[:, cols], bo_buf[:, cols]
        none = jnp.zeros_like(bi)
        copies[2 + 2 * k].wait()
        part = lax.dot_general(x_buf[k], jnp.concatenate([bi, none, bi, none]), LAST, preferred_element_type=F32)
        total = part if total is None else total + part
        copies[3 + 2 * k].wait()
        total += lax.dot_general(g_buf[k], jnp.concatenate([none, bo, none, bo]), LAST, preferred_element_type=F32)
    out_ref[...] = total


def grads_kernel(basis, n_sub, *refs):
    parts, q_ref, out_ref, own_ref = refs[:n_sub], refs[n_sub], refs[n_sub + 1], refs[n_sub + 2]
    total = parts[0][...]
    for part in parts[1:]:
        total += part[...]
    tokens, lanes = total.shape
    pair = 2 * basis
    high = total.astype(BF16).astype(F32)
    rest = total - high
    mid = rest.astype(BF16).astype(F32)
    low = rest - mid
    first = lax.broadcasted_iota(jnp.int32, (tokens, lanes), 1) < pair
    pieces = jnp.concatenate([jnp.where(first, high, mid), jnp.where(first, low, 0.0)], axis=1).astype(BF16)

    row = lax.broadcasted_iota(jnp.int32, (2 * lanes, lanes), 0) % pair
    col = lax.broadcasted_iota(jnp.int32, (2 * lanes, lanes), 1)
    pick_x = jnp.where(row == col % basis, 1.0, 0.0).astype(BF16)
    tiled_x = jnp.dot(pieces, pick_x, preferred_element_type=F32)
    gap = row - basis - col // basis
    own = tokens // LEN
    tiles = []
    for j in range(basis * basis // lanes):
        pick_g = jnp.where(gap == j * (lanes // basis), 1.0, 0.0).astype(BF16)
        product = jnp.dot(pieces, pick_g, preferred_element_type=F32) * tiled_x
        tiles.append(product.reshape(own, LEN, lanes).sum(axis=1))
    grads = jnp.concatenate(tiles, axis=1)
    high = grads.astype(BF16).astype(F32)
    low = grads - high
    half = grads.shape[1] // n_sub
    rows = []
    for h in range(n_sub):
        cols = slice(h * half, (h + 1) * half)
        rows += [high[:, cols], low[:, cols]]
    packed = jnp.concatenate(rows, axis=0).astype(BF16)
    own_ref[...] = packed
    out_ref[0, : packed.shape[0], :] = packed
    out_ref[0, packed.shape[0] :, :] = q_ref[...]


def final_kernel(n_ex, n_lay, n_sub, own, order, *refs):
    others, gots = refs[: n_lay - 1], refs[n_lay - 1 : -2]
    gram_ref, scores_ref = refs[-2:]
    ex, lay, sub = lax.axis_index("ex"), lax.axis_index("lay"), lax.axis_index("sub")
    n_blk = n_lay * n_sub
    per_blk = n_ex // n_blk
    used = 2 * own * n_sub
    half = gots[0].shape[2]
    n_rows, per_half = half * n_sub // n_ex, n_ex // n_sub
    places = [(got, at) for got in gots for at in range(got.shape[0])]

    def halves_of(pieces):
        pieces = pieces.astype(F32)
        return [pieces[h * 2 * own : (h + 1) * 2 * own] for h in range(n_sub)]

    layers = [halves_of(gots[0][0, :used, :])] + [halves_of(other[...]) for other in others]
    blocks = [0.0] * per_blk
    for (got, at), slot in zip(places, order):
        source = slot ^ ex
        l, h = source % n_blk // n_sub, source % n_sub
        grads = layers[0][0]
        for k in range(n_lay):
            for i in range(n_sub):
                grads = jnp.where(((lay + k) % n_lay == l) & (h == i), layers[k][i], grads)
        part = lax.dot_general(grads.astype(BF16), got[at, used:, :], LAST, preferred_element_type=F32)
        part = part[:own] + part[own:]
        for j in range(per_blk):
            blocks[j] += part if per_blk == 1 else jnp.where(source // n_blk == j, part, 0.0)
    scores_ref[...] = blocks[0] if per_blk == 1 else jnp.concatenate(blocks, axis=1)

    lefts, rights = [], []
    for got, at in places:
        halves = halves_of(got[at, :used, :])
        right = halves[0]
        for h in range(1, n_sub):
            right = jnp.where(sub == h, halves[h], right)
        left = None
        for e in range(n_ex):
            piece = halves[e // per_half][:, (e % per_half) * n_rows : (e % per_half + 1) * n_rows]
            left = piece if left is None else jnp.where(ex == e, piece, left)
        lefts += [left, pltpu.roll(left, own, 0)]
        rights += [right, right]
    left = jnp.concatenate(lefts, axis=0).astype(BF16)
    right = jnp.concatenate(rights, axis=0).astype(BF16)
    gram = lax.dot_general(left, right, FIRST, preferred_element_type=F32)
    gram_ref[0] = gram * (1.0 / (own * n_ex))


def solution(mesh):
    n_ex, n_lay, n_sub = mesh.shape["ex"], mesh.shape["lay"], mesh.shape["sub"]
    n_blk = n_lay * n_sub
    per_blk = n_ex // n_blk

    def flat(ex, lay, sub):
        return (ex * n_lay + lay) * n_sub + sub

    query_pairs = [
        (flat(blk * per_blk + ex // n_blk, ex % n_blk // n_sub, ex % n_sub), flat(ex, blk // n_sub, blk % n_sub))
        for ex in range(n_ex)
        for blk in range(n_blk)
    ]

    def rotate(value, axis, size, k):
        return lax.ppermute(value, axis, [((i + k) % size, i) for i in range(size)])

    def body(layer_inputs, output_grads, basis_in, basis_out, queries):
        _, tokens, depth = layer_inputs.shape
        basis = basis_in.shape[1]
        own = tokens // LEN
        width = basis * basis
        rows, half = queries.shape[1:]
        used = 2 * own * n_sub
        chunk = lax.ppermute(queries[0], ("ex", "lay", "sub"), query_pairs)

        proj = pl.pallas_call(
            project_kernel,
            out_shape=jax.ShapeDtypeStruct((tokens, 4 * basis), F32),
            in_specs=[ANY] * 4,
            out_specs=VMEM,
            scratch_shapes=[
                pltpu.VMEM((CHUNKS, tokens, depth // CHUNKS), BF16),
                pltpu.VMEM((CHUNKS, tokens, depth // CHUNKS), BF16),
                pltpu.VMEM((basis, depth), BF16),
                pltpu.VMEM((basis, depth), BF16),
                pltpu.SemaphoreType.DMA((2 + 2 * CHUNKS,)),
            ],
            compiler_params=pltpu.CompilerParams(vmem_limit_bytes=60 * 1024 * 1024),
            name="project",
        )(layer_inputs, output_grads, basis_in, basis_out)
        parts = [proj] + [rotate(proj, "sub", n_sub, k) for k in range(1, n_sub)]

        got, grads = pl.pallas_call(
            functools.partial(grads_kernel, basis, n_sub),
            out_shape=(
                jax.ShapeDtypeStruct((1, used + rows, half), BF16),
                jax.ShapeDtypeStruct((used, half), BF16),
            ),
            in_specs=[VMEM] * (n_sub + 1),
            out_specs=(VMEM, VMEM),
            compiler_params=pltpu.CompilerParams(vmem_limit_bytes=16 * 1024 * 1024),
            name="grads",
        )(*parts, chunk)

        others = [rotate(grads, "lay", n_lay, k) for k in range(1, n_lay)]
        gots, order, far = [got], [0], n_ex // 2
        while far:
            sent = gots[0] if len(gots) == 1 else jnp.concatenate(gots)
            gots.append(lax.ppermute(sent, "ex", [(i, i ^ far) for i in range(n_ex)]))
            order += [k ^ far for k in order]
            far //= 2

        gram, scores = pl.pallas_call(
            functools.partial(final_kernel, n_ex, n_lay, n_sub, own, order),
            out_shape=(
                jax.ShapeDtypeStruct((1, width // n_ex, half), F32),
                jax.ShapeDtypeStruct((own, rows * per_blk), F32),
            ),
            in_specs=[VMEM] * (len(others) + len(gots)),
            out_specs=(VMEM, VMEM),
            compiler_params=pltpu.CompilerParams(vmem_limit_bytes=16 * 1024 * 1024),
            name="gram_and_scores",
        )(*others, *gots)
        return gram, scores

    in_specs = (
        P("lay", ("grp", "ex"), "sub"),
        P("lay", ("grp", "ex"), "sub"),
        P("lay", None, "sub"),
        P("lay", None, "sub"),
        P("lay", "ex", "sub"),
    )
    out_specs = (P(("grp", "lay"), "ex", "sub"), P(("grp", "ex"), ("lay", "sub")))
    return jax.shard_map(body, mesh=mesh, in_specs=in_specs, out_specs=out_specs, check_vma=False)
```

```python
import functools

import jax
import jax.numpy as jnp
from jax import lax
from jax.experimental import pallas as pl
from jax.experimental.pallas import tpu as pltpu
from jax.sharding import PartitionSpec as P

LEN = 64
F32, BF16 = jnp.float32, jnp.bfloat16
VMEM = pl.BlockSpec(memory_space=pltpu.VMEM)
LAST = (((1,), (1,)), ((), ()))
FIRST = (((0,), (0,)), ((), ()))


def project_kernel(x_ref, g_ref, bi_ref, bo_ref, out_ref):
    bi, bo = bi_ref[0], bo_ref[0]
    none = jnp.zeros_like(bi)
    half = out_ref.shape[0]
    total = None
    for at, (values, basis) in enumerate([(x_ref, bi), (g_ref, bo)] * 2):
        rows = pl.ds(at // 2 * half, half)
        weights = jnp.concatenate([basis if i == at else none for i in range(4)])
        part = lax.dot_general(values[0, rows, :], weights, LAST, preferred_element_type=F32)
        total = part if total is None else total + part
    out_ref[...] = total


def prepare_kernel(basis, q_ref, chunk_ref, pick_x_ref, pick_g_ref):
    chunk_ref[...] = q_ref[...]
    rows, width = pick_g_ref.shape
    lanes, pair = pick_x_ref.shape[1], 2 * basis
    row = lax.broadcasted_iota(jnp.int32, (rows, lanes), 0) % pair
    col = lax.broadcasted_iota(jnp.int32, (rows, lanes), 1)
    pick_x_ref[...] = jnp.where(row == col % basis, 1.0, 0.0).astype(BF16)
    gap = row - basis - col // basis
    for j in range(width // lanes):
        pick_g_ref[:, j * lanes : (j + 1) * lanes] = jnp.where(gap == j * (lanes // basis), 1.0, 0.0).astype(BF16)


def grads_kernel(basis, n_sub, *refs):
    parts, (q_ref, pick_x_ref, pick_g_ref, out_ref, own_ref) = refs[:n_sub], refs[n_sub:]
    total = parts[0][...]
    for part in parts[1:]:
        total += part[...]
    lanes = total.shape[1]
    pair = 2 * basis
    high = total.astype(BF16).astype(F32)
    rest = total - high
    mid = rest.astype(BF16).astype(F32)
    low = rest - mid
    first = lax.broadcasted_iota(jnp.int32, total.shape, 1) < pair
    top = [jnp.where(first, high, pltpu.roll(mid, pair, 1)), jnp.where(first, low, 0.0)]
    bottom = [jnp.where(first, pltpu.roll(high, pair, 1), mid), jnp.where(first, pltpu.roll(low, pair, 1), 0.0)]
    pieces = jnp.concatenate([jnp.concatenate(top, axis=1), jnp.concatenate(bottom, axis=1)]).astype(BF16)
    tokens = pieces.shape[0]

    tiled_x = jnp.dot(pieces, pick_x_ref[...], preferred_element_type=F32)
    own = tokens // LEN
    tiles = []
    for j in range(basis * basis // lanes):
        pick_g = pick_g_ref[:, j * lanes : (j + 1) * lanes]
        product = jnp.dot(pieces, pick_g, preferred_element_type=F32) * tiled_x
        tiles.append(product.reshape(own, LEN, lanes).sum(axis=1))
    grads = jnp.concatenate(tiles, axis=1)
    high = grads.astype(BF16).astype(F32)
    low = grads - high
    half = grads.shape[1] // n_sub
    rows = []
    for h in range(n_sub):
        cols = slice(h * half, (h + 1) * half)
        rows += [high[:, cols], low[:, cols]]
    packed = jnp.concatenate(rows, axis=0).astype(BF16)
    own_ref[...] = packed
    out_ref[0, : packed.shape[0], :] = packed
    out_ref[0, packed.shape[0] :, :] = q_ref[...]


def final_kernel(n_ex, n_lay, n_sub, own, turn, order, *refs):
    others, gots = refs[: n_lay - 1], refs[n_lay - 1 : -2]
    gram_ref, scores_ref = refs[-2:]
    ex, lay, sub = lax.axis_index("ex"), lax.axis_index("lay"), lax.axis_index("sub")
    n_blk = n_lay * n_sub
    per_blk = n_ex // n_blk
    used = 2 * own * n_sub
    half = gots[0].shape[2]
    n_rows, per_half = half * n_sub // n_ex, n_ex // n_sub
    places = [(got, at) for got in gots for at in range(got.shape[0])]

    def halves_of(pieces):
        pieces = pieces.astype(F32)
        return [pieces[h * 2 * own : (h + 1) * 2 * own] for h in range(n_sub)]

    layers = [halves_of(gots[0][0, :used, :])] + [halves_of(other[...]) for other in others]
    blocks = [0.0] * per_blk
    for (got, at), slot in zip(places, order):
        source = slot ^ turn ^ ex
        l, h = source % n_blk // n_sub, source % n_sub
        grads = layers[0][0]
        for k in range(n_lay):
            for i in range(n_sub):
                grads = jnp.where(((lay + k) % n_lay == l) & (h == i), layers[k][i], grads)
        part = lax.dot_general(grads.astype(BF16), got[at, used:, :], LAST, preferred_element_type=F32)
        part = part[:own] + part[own:]
        for j in range(per_blk):
            blocks[j] += part if per_blk == 1 else jnp.where(source // n_blk == j, part, 0.0)
    scores_ref[...] = blocks[0] if per_blk == 1 else jnp.concatenate(blocks, axis=1)

    lefts, rights = [], []
    for got, at in places:
        halves = halves_of(got[at, :used, :])
        right = halves[0]
        for h in range(1, n_sub):
            right = jnp.where(sub == h, halves[h], right)
        left = None
        for e in range(n_ex):
            piece = halves[e // per_half][:, (e % per_half) * n_rows : (e % per_half + 1) * n_rows]
            left = piece if left is None else jnp.where(ex == e, piece, left)
        lefts += [left, pltpu.roll(left, own, 0)]
        rights += [right, right]
    left = jnp.concatenate(lefts, axis=0).astype(BF16)
    right = jnp.concatenate(rights, axis=0).astype(BF16)
    gram = lax.dot_general(left, right, FIRST, preferred_element_type=F32)
    gram_ref[0] = gram * (1.0 / (own * n_ex))


def solution(mesh):
    n_ex, n_lay, n_sub = mesh.shape["ex"], mesh.shape["lay"], mesh.shape["sub"]
    n_blk = n_lay * n_sub
    per_blk = n_ex // n_blk

    def flat(ex, lay, sub):
        return (ex * n_lay + lay) * n_sub + sub

    turn = 2

    def query_source(ex, blk):
        at = ex ^ turn
        return flat(blk * per_blk + at // n_blk, at % n_blk // n_sub, at % n_sub)

    query_pairs = [
        (query_source(ex, blk), flat(ex, blk // n_sub, blk % n_sub)) for ex in range(n_ex) for blk in range(n_blk)
    ]

    def rotate(value, axis, size, k):
        return lax.ppermute(value, axis, [((i + k) % size, i) for i in range(size)])

    def body(layer_inputs, output_grads, basis_in, basis_out, queries):
        _, tokens, depth = layer_inputs.shape
        basis = basis_in.shape[1]
        own = tokens // LEN
        width = basis * basis
        rows, half = queries.shape[1:]
        used = 2 * own * n_sub
        chunk = lax.ppermute(queries[0], ("ex", "lay", "sub"), query_pairs)

        proj = pl.pallas_call(
            project_kernel,
            out_shape=jax.ShapeDtypeStruct((tokens // 2, 4 * basis), F32),
            in_specs=[VMEM] * 4,
            out_specs=VMEM,
            compiler_params=pltpu.CompilerParams(vmem_limit_bytes=16 * 1024 * 1024),
            cost_estimate=pl.CostEstimate(flops=10**11, bytes_accessed=10**9, transcendentals=0),
            name="project",
        )(layer_inputs, output_grads, basis_in, basis_out)
        parts = [proj] + [rotate(proj, "sub", n_sub, k) for k in range(1, n_sub)]

        prepared = pl.pallas_call(
            functools.partial(prepare_kernel, basis),
            out_shape=(
                jax.ShapeDtypeStruct((rows, half), BF16),
                jax.ShapeDtypeStruct((8 * basis, 4 * basis), BF16),
                jax.ShapeDtypeStruct((8 * basis, width), BF16),
            ),
            in_specs=[VMEM],
            out_specs=(VMEM,) * 3,
            compiler_params=pltpu.CompilerParams(vmem_limit_bytes=16 * 1024 * 1024),
            cost_estimate=pl.CostEstimate(flops=10**11, bytes_accessed=10**9, transcendentals=0),
            name="prepare",
        )(chunk)

        got, grads = pl.pallas_call(
            functools.partial(grads_kernel, basis, n_sub),
            out_shape=(
                jax.ShapeDtypeStruct((1, used + rows, half), BF16),
                jax.ShapeDtypeStruct((used, half), BF16),
            ),
            in_specs=[VMEM] * (n_sub + 3),
            out_specs=(VMEM, VMEM),
            compiler_params=pltpu.CompilerParams(vmem_limit_bytes=16 * 1024 * 1024),
            name="grads",
        )(*parts, *prepared)

        others = [rotate(grads, "lay", n_lay, k) for k in range(1, n_lay)]
        gots, order, far = [got], [0], n_ex // 2
        while far:
            sent = gots[0] if len(gots) == 1 else jnp.concatenate(gots)
            back = lax.ppermute(sent, "ex", [(i, i ^ far) for i in range(n_ex)])
            if len(gots) == 1:
                back, others = lax.optimization_barrier((back, others))
            gots.append(back)
            order += [k ^ far for k in order]
            far //= 2

        gram, scores = pl.pallas_call(
            functools.partial(final_kernel, n_ex, n_lay, n_sub, own, turn, order),
            out_shape=(
                jax.ShapeDtypeStruct((1, width // n_ex, half), F32),
                jax.ShapeDtypeStruct((own, rows * per_blk), F32),
            ),
            in_specs=[VMEM] * (len(others) + len(gots)),
            out_specs=(VMEM, VMEM),
            compiler_params=pltpu.CompilerParams(vmem_limit_bytes=16 * 1024 * 1024),
            name="gram_and_scores",
        )(*others, *gots)
        return gram, scores

    in_specs = (
        P("lay", ("grp", "ex"), "sub"),
        P("lay", ("grp", "ex"), "sub"),
        P("lay", None, "sub"),
        P("lay", None, "sub"),
        P("lay", "ex", "sub"),
    )
    out_specs = (P(("grp", "lay"), "ex", "sub"), P(("grp", "ex"), ("lay", "sub")))
    return jax.shard_map(body, mesh=mesh, in_specs=in_specs, out_specs=out_specs, check_vma=False)
```

```python
import functools

import jax
import jax.numpy as jnp
from jax import lax
from jax.experimental import pallas as pl
from jax.experimental.pallas import tpu as pltpu
from jax.sharding import PartitionSpec as P

LEN = 64
AXES = ("ex", "lay", "sub")
F32, BF16 = jnp.float32, jnp.bfloat16
VMEM = pl.BlockSpec(memory_space=pltpu.VMEM)
LAST = (((1,), (1,)), ((), ()))
FIRST = (((0,), (0,)), ((), ()))
PARAMS = pltpu.CompilerParams(vmem_limit_bytes=16 * 1024 * 1024)


def prepare_kernel(basis, q_ref, chunk_ref, pick_x_ref, pick_g_ref):
    chunk_ref[...] = q_ref[...]
    rows, width = pick_g_ref.shape
    lanes, pair = pick_x_ref.shape[1], 2 * basis
    row = lax.broadcasted_iota(jnp.int32, (rows, lanes), 0) % pair
    col = lax.broadcasted_iota(jnp.int32, (rows, lanes), 1)
    pick_x_ref[...] = jnp.where(row == col % basis, 1.0, 0.0).astype(BF16)
    gap = row - basis - col // basis
    for j in range(width // lanes):
        pick_g_ref[:, j * lanes : (j + 1) * lanes] = jnp.where(gap == j * (lanes // basis), 1.0, 0.0).astype(BF16)


def grads_kernel(n_sub, *refs):
    parts, (pick_x_ref, pick_g_ref, out_ref) = refs[:n_sub], refs[n_sub:]
    total = parts[0][...]
    for part in parts[1:]:
        total += part[...]
    high = total.astype(BF16).astype(F32)
    rest = total - high
    mid = rest.astype(BF16).astype(F32)
    pieces = jnp.concatenate([high, mid, rest - mid]).astype(BF16)
    own = pieces.shape[1] // LEN
    lanes, width = pick_x_ref.shape[1], pick_g_ref.shape[1]
    tiled_x = lax.dot_general(pieces, pick_x_ref[...], FIRST, preferred_element_type=F32)
    tiles = []
    for j in range(width // lanes):
        pick_g = pick_g_ref[:, j * lanes : (j + 1) * lanes]
        product = lax.dot_general(pieces, pick_g, FIRST, preferred_element_type=F32) * tiled_x
        tiles.append(product.reshape(own, LEN, lanes).sum(axis=1))
    grads = jnp.concatenate(tiles, axis=1)
    high = grads.astype(BF16).astype(F32)
    low = grads - high
    half = width // n_sub
    rows = []
    for h in range(n_sub):
        cols = slice(h * half, (h + 1) * half)
        rows += [high[:, cols], low[:, cols]]
    out_ref[...] = jnp.concatenate(rows, axis=0).astype(BF16)


def final_kernel(n_ex, n_lay, n_sub, own, moves, mine_ref, got_ref, gram_ref, scores_ref):
    ex, lay, sub = lax.axis_index("ex"), lax.axis_index("lay"), lax.axis_index("sub")
    rounds = got_ref.shape[0] // n_sub
    group, per_blk = n_ex // n_lay, n_ex // (n_lay * n_sub)
    used, half = 2 * own * n_sub, got_ref.shape[2]
    rows = (got_ref.shape[1] - used) // n_sub
    n_rows, per_half = half * n_sub // n_ex, n_ex // n_sub

    def halves_of(pieces):
        pieces = pieces[:used].astype(F32)
        return [pieces[h * 2 * own : (h + 1) * 2 * own] for h in range(n_sub)]

    def choose(values, index):
        if isinstance(index, int):
            return values[index]
        result = values[0]
        for i in range(1, len(values)):
            result = jnp.where(index == i, values[i], result)
        return result

    mine = mine_ref[0]
    layers, slots = [halves_of(mine)], [(mine, sub, ex)]
    for at, (axis, k) in enumerate(moves):
        core = at % n_sub
        piece = got_ref[lax.rem(core - sub + n_sub, n_sub) * rounds + at // n_sub]
        if axis == "ex":
            slots.append((piece, core, ex ^ k))
        else:
            layers.append(halves_of(piece))

    blocks = [0.0] * per_blk
    for piece, core, source in slots:
        layer = lax.rem(source // group + n_lay - 1, n_lay)
        behind = lax.rem(layer - lay + n_lay, n_lay)
        grads = [choose([halves[h] for halves in layers], behind) for h in range(n_sub)]
        part = 0.0
        for k in range(n_sub):
            part += lax.dot_general(
                choose(grads, (core + k) % n_sub).astype(BF16),
                piece[used + k * rows : used + (k + 1) * rows],
                LAST,
                preferred_element_type=F32,
            )
        part = part[:own] + part[own:]
        for j in range(per_blk):
            blocks[j] += jnp.where(lax.rem(source, group) == sub * per_blk + j, part, 0.0)
    scores_ref[...] = blocks[0] if per_blk == 1 else jnp.concatenate(blocks, axis=1)

    lefts, rights = [], []
    for piece, _, _ in slots:
        halves = halves_of(piece)
        cuts = [halves[e // per_half][:, e % per_half * n_rows : (e % per_half + 1) * n_rows] for e in range(n_ex)]
        left, right = choose(cuts, ex), choose(halves, sub)
        lefts += [left, pltpu.roll(left, own, 0)]
        rights += [right, right]
    left = jnp.concatenate(lefts, axis=0).astype(BF16)
    right = jnp.concatenate(rights, axis=0).astype(BF16)
    gram = lax.dot_general(left, right, FIRST, preferred_element_type=F32)
    gram_ref[0] = gram * (1.0 / (own * n_ex))


def solution(mesh):
    n_ex, n_lay, n_sub = mesh.shape["ex"], mesh.shape["lay"], mesh.shape["sub"]
    group, per_blk = n_ex // n_lay, n_ex // (n_lay * n_sub)

    def flat(ex, lay, sub):
        return (ex * n_lay + lay) * n_sub + sub

    devices = [(ex, lay, sub) for ex in range(n_ex) for lay in range(n_lay) for sub in range(n_sub)]

    query_pairs = [
        (flat(ex, lay, sub), flat((lay + 1) % n_lay * group + ex % group, ex // group, sub)) for ex, lay, sub in devices
    ]

    far = [("ex", k) for k in range(3, n_ex)]
    across = [("lay", k) for k in range(1, n_lay)]
    moves = [("ex", 1), ("ex", 2)]
    while far or across:
        moves += across[:1] + far[:1]
        across, far = across[1:], far[1:]
    rounds = -(-len(moves) // n_sub)

    def source_of(at, ex, lay, sub):
        axis, k = moves[min(at * n_sub + sub, len(moves) - 1)]
        return flat(ex ^ k, lay, sub) if axis == "ex" else flat(ex, (lay + k) % n_lay, sub)

    def rotate(value, k):
        return lax.ppermute(value, "sub", [((i + k) % n_sub, i) for i in range(n_sub)])

    def body(layer_inputs, output_grads, basis_in, basis_out, queries):
        _, tokens, depth = layer_inputs.shape
        basis = basis_in.shape[1]
        own = tokens // LEN
        width = basis * basis
        rows, half = queries.shape[1:]

        chunk = lax.ppermute(queries[0], AXES, query_pairs)
        proj_x = lax.dot_general(basis_in[0], layer_inputs[0], LAST, preferred_element_type=F32)
        proj_g = lax.dot_general(basis_out[0], output_grads[0], LAST, preferred_element_type=F32)
        proj = jnp.concatenate([proj_x, proj_g])
        parts = [proj] + [rotate(proj, k) for k in range(1, n_sub)]

        chunk, pick_x, pick_g = pl.pallas_call(
            functools.partial(prepare_kernel, basis),
            out_shape=(
                jax.ShapeDtypeStruct((rows, half), BF16),
                jax.ShapeDtypeStruct((6 * basis, 4 * basis), BF16),
                jax.ShapeDtypeStruct((6 * basis, width), BF16),
            ),
            in_specs=[VMEM],
            out_specs=(VMEM,) * 3,
            compiler_params=PARAMS,
            cost_estimate=pl.CostEstimate(flops=10**11, bytes_accessed=10**9, transcendentals=0),
            name="prepare",
        )(chunk)
        chunks = [chunk] + [rotate(chunk, k) for k in range(1, n_sub)]

        grads = pl.pallas_call(
            functools.partial(grads_kernel, n_sub),
            out_shape=jax.ShapeDtypeStruct((2 * own * n_sub, half), BF16),
            in_specs=[VMEM] * (n_sub + 2),
            out_specs=VMEM,
            compiler_params=PARAMS,
            name="grads",
        )(*parts, pick_x, pick_g)

        mine = jnp.concatenate([grads] + chunks)[None]
        received = []
        for at in range(rounds):
            pairs = [(source_of(at, *device), flat(*device)) for device in devices]
            received.append(lax.ppermute(mine, AXES, pairs))
        received = jnp.concatenate(received)
        got = jnp.concatenate([received] + [rotate(received, k) for k in range(1, n_sub)])

        return pl.pallas_call(
            functools.partial(final_kernel, n_ex, n_lay, n_sub, own, moves),
            out_shape=(
                jax.ShapeDtypeStruct((1, width // n_ex, half), F32),
                jax.ShapeDtypeStruct((own, rows * per_blk), F32),
            ),
            in_specs=[VMEM] * 2,
            out_specs=(VMEM, VMEM),
            compiler_params=PARAMS,
            name="gram_and_scores",
        )(mine, got)

    in_specs = (
        P("lay", ("grp", "ex"), "sub"),
        P("lay", ("grp", "ex"), "sub"),
        P("lay", None, "sub"),
        P("lay", None, "sub"),
        P("lay", "ex", "sub"),
    )
    out_specs = (P(("grp", "lay"), "ex", "sub"), P(("grp", "ex"), ("lay", "sub")))
    return jax.shard_map(body, mesh=mesh, in_specs=in_specs, out_specs=out_specs, check_vma=False)
```

```python
import functools

import jax
import jax.numpy as jnp
from jax import lax
from jax.experimental import pallas as pl
from jax.experimental.pallas import tpu as pltpu
from jax.sharding import PartitionSpec as P

LEN = 64
AXES = ("ex", "lay", "sub")
F32, BF16 = jnp.float32, jnp.bfloat16
VMEM = pl.BlockSpec(memory_space=pltpu.VMEM)
LAST = (((1,), (1,)), ((), ()))
FIRST = (((0,), (0,)), ((), ()))
PARAMS = pltpu.CompilerParams(vmem_limit_bytes=16 * 1024 * 1024)


def picks_kernel(basis, pick_x_ref, pick_g_ref):
    rows, width = pick_g_ref.shape
    lanes, pair = pick_x_ref.shape[1], 2 * basis
    row = lax.broadcasted_iota(jnp.int32, (rows, lanes), 0) % pair
    col = lax.broadcasted_iota(jnp.int32, (rows, lanes), 1)
    pick_x_ref[...] = jnp.where(row == col % basis, 1.0, 0.0).astype(BF16)
    gap = row - basis - col // basis
    for j in range(width // lanes):
        pick_g_ref[:, j * lanes : (j + 1) * lanes] = jnp.where(gap == j * (lanes // basis), 1.0, 0.0).astype(BF16)


def grads_kernel(n_sub, *refs):
    parts, (pick_x_ref, pick_g_ref, out_ref) = refs[:n_sub], refs[n_sub:]
    total = parts[0][...]
    for part in parts[1:]:
        total += part[...]
    high = total.astype(BF16).astype(F32)
    rest = total - high
    mid = rest.astype(BF16).astype(F32)
    pieces = jnp.concatenate([high, mid, rest - mid]).astype(BF16)
    own = pieces.shape[1] // LEN
    lanes, width = pick_x_ref.shape[1], pick_g_ref.shape[1]
    tiled_x = lax.dot_general(pieces, pick_x_ref[...], FIRST, preferred_element_type=F32)
    tiles = []
    for j in range(width // lanes):
        pick_g = pick_g_ref[:, j * lanes : (j + 1) * lanes]
        product = lax.dot_general(pieces, pick_g, FIRST, preferred_element_type=F32) * tiled_x
        tiles.append(product.reshape(own, LEN, lanes).sum(axis=1))
    grads = jnp.concatenate(tiles, axis=1)
    high = grads.astype(BF16).astype(F32)
    low = grads - high
    half = width // n_sub
    rows = []
    for h in range(n_sub):
        cols = slice(h * half, (h + 1) * half)
        rows += [high[:, cols], low[:, cols]]
    out_ref[0] = jnp.concatenate(rows, axis=0).astype(BF16)


def halves_of(pieces, n_sub):
    pieces = pieces.astype(F32)
    size = pieces.shape[0] // n_sub
    return [pieces[h * size : (h + 1) * size] for h in range(n_sub)]


def layer_scores(halves, k, units, turns, n_ex, n_lay, n_sub):
    ex, lay = lax.axis_index("ex"), lax.axis_index("lay")
    n_blk = n_lay * n_sub
    own = halves[0].shape[0] // 2
    grads = [half.astype(BF16) for half in halves]
    blocks = [0.0] * (n_ex // n_blk)
    for unit_ref, turn in zip(units, turns):
        source = ex ^ turn
        part = 0.0
        for h in range(n_sub):
            part += lax.dot_general(grads[h], unit_ref[h], LAST, preferred_element_type=F32)
        part = part[:own] + part[own:]
        fits = source % n_blk // n_sub == lax.rem(lay + k, n_lay)
        for j in range(len(blocks)):
            blocks[j] += jnp.where(fits & (source // n_blk == j), part, 0.0)
    return blocks[0] if len(blocks) == 1 else jnp.concatenate(blocks, axis=1)


def own_scores_kernel(n_ex, n_lay, n_sub, turns, mine_ref, *refs):
    units, out_ref = refs[:-1], refs[-1]
    out_ref[...] = layer_scores(halves_of(mine_ref[0], n_sub), 0, units, turns, n_ex, n_lay, n_sub)


def final_kernel(n_ex, n_lay, n_sub, own, moves, turns, mine_ref, got_ref, *refs):
    partials, units, (gram_ref, scores_ref) = refs[: len(turns)], refs[len(turns) : -2], refs[-2:]
    ex, sub = lax.axis_index("ex"), lax.axis_index("sub")
    rounds = got_ref.shape[0] // n_sub
    half = got_ref.shape[2]
    n_rows, per_half = half * n_sub // n_ex, n_ex // n_sub

    def choose(values, index):
        result = values[0]
        for i in range(1, len(values)):
            result = jnp.where(index == i, values[i], result)
        return result

    slots = [halves_of(mine_ref[0], n_sub)]
    layers = slots[:]
    for at, (axis, k) in enumerate(moves):
        piece = halves_of(got_ref[lax.rem(at % n_sub - sub + n_sub, n_sub) * rounds + at // n_sub], n_sub)
        (slots if axis == "ex" else layers).append(piece)

    lefts, rights = [], []
    for halves in slots:
        cuts = [halves[e // per_half][:, e % per_half * n_rows : (e % per_half + 1) * n_rows] for e in range(n_ex)]
        left, right = choose(cuts, ex), choose(halves, sub)
        lefts += [left, pltpu.roll(left, own, 0)]
        rights += [right, right]
    left = jnp.concatenate(lefts, axis=0).astype(BF16)
    right = jnp.concatenate(rights, axis=0).astype(BF16)
    gram = lax.dot_general(left, right, FIRST, preferred_element_type=F32)
    gram_ref[0] = gram * (1.0 / (own * n_ex))

    scores = sum(partial[...] for partial in partials)
    for k in range(1, n_lay):
        scores += layer_scores(layers[k], k, units, turns, n_ex, n_lay, n_sub)
    scores_ref[...] = scores


def solution(mesh):
    n_ex, n_lay, n_sub = mesh.shape["ex"], mesh.shape["lay"], mesh.shape["sub"]
    n_blk = n_lay * n_sub
    per_blk = n_ex // n_blk

    def flat(ex, lay, sub):
        return (ex * n_lay + lay) * n_sub + sub

    devices = [(ex, lay, sub) for ex in range(n_ex) for lay in range(n_lay) for sub in range(n_sub)]

    turns = [max(k * n_sub, 1) for k in range(n_ex // n_sub)]

    def unit_pairs(turn):
        pairs = []
        for ex, lay, sub in devices:
            at, blk = ex ^ turn, lay * n_sub + sub
            pairs.append((flat(blk * per_blk + at // n_blk, at % n_blk // n_sub, at % n_sub), flat(ex, lay, sub)))
        return pairs

    far = [("ex", k) for k in range(3, n_ex)]
    across = [("lay", k) for k in range(1, n_lay)]
    moves = [("ex", 1), ("ex", 2)]
    while far or across:
        moves += across[:1] + far[:1]
        across, far = across[1:], far[1:]
    rounds = -(-len(moves) // n_sub)

    def source_of(at, ex, lay, sub):
        axis, k = moves[min(at * n_sub + sub, len(moves) - 1)]
        return flat(ex ^ k, lay, sub) if axis == "ex" else flat(ex, (lay + k) % n_lay, sub)

    def rotate(value, k):
        return lax.ppermute(value, "sub", [((i + k) % n_sub, i) for i in range(n_sub)])

    def body(layer_inputs, output_grads, basis_in, basis_out, queries):
        _, tokens, depth = layer_inputs.shape
        basis = basis_in.shape[1]
        own = tokens // LEN
        width = basis * basis
        rows, half = queries.shape[1:]

        unit = jnp.stack([queries[0]] + [rotate(queries[0], k) for k in range(1, n_sub)])
        unit = jnp.roll(unit, lax.axis_index("sub"), axis=0)
        pick_x, pick_g = pl.pallas_call(
            functools.partial(picks_kernel, basis),
            out_shape=(
                jax.ShapeDtypeStruct((6 * basis, 4 * basis), BF16),
                jax.ShapeDtypeStruct((6 * basis, width), BF16),
            ),
            out_specs=(VMEM,) * 2,
            compiler_params=PARAMS,
            cost_estimate=pl.CostEstimate(flops=10**11, bytes_accessed=10**9, transcendentals=0),
            name="picks",
        )()

        proj_x = lax.dot_general(basis_in[0], layer_inputs[0], LAST, preferred_element_type=F32)
        proj_g = lax.dot_general(basis_out[0], output_grads[0], LAST, preferred_element_type=F32)
        proj = jnp.concatenate([proj_x, proj_g])
        proj, unit = lax.optimization_barrier((proj, unit))
        units = [lax.ppermute(unit, AXES, unit_pairs(turn)) for turn in turns]
        parts = [proj] + [rotate(proj, k) for k in range(1, n_sub)]

        mine = pl.pallas_call(
            functools.partial(grads_kernel, n_sub),
            out_shape=jax.ShapeDtypeStruct((1, 2 * own * n_sub, half), BF16),
            in_specs=[VMEM] * (n_sub + 2),
            out_specs=VMEM,
            compiler_params=PARAMS,
            cost_estimate=pl.CostEstimate(flops=10**11, bytes_accessed=10**9, transcendentals=0),
            name="grads",
        )(*parts, pick_x, pick_g)

        received = []
        for at in range(rounds):
            pairs = [(source_of(at, *device), flat(*device)) for device in devices]
            received.append(lax.ppermute(mine, AXES, pairs))
        partials = [
            pl.pallas_call(
                functools.partial(own_scores_kernel, n_ex, n_lay, n_sub, [turn]),
                out_shape=jax.ShapeDtypeStruct((own, rows * per_blk), F32),
                in_specs=[VMEM] * 2,
                out_specs=VMEM,
                compiler_params=PARAMS,
                cost_estimate=pl.CostEstimate(flops=10**11, bytes_accessed=10**9, transcendentals=0),
                name="own_scores",
            )(mine, unit)
            for unit, turn in zip(units, turns)
        ]
        early = len(units) // 2
        received, *partials[:early] = lax.optimization_barrier((jnp.concatenate(received), *partials[:early]))
        got = jnp.concatenate([received] + [rotate(received, k) for k in range(1, n_sub)])

        return pl.pallas_call(
            functools.partial(final_kernel, n_ex, n_lay, n_sub, own, moves, turns),
            out_shape=(
                jax.ShapeDtypeStruct((1, width // n_ex, half), F32),
                jax.ShapeDtypeStruct((own, rows * per_blk), F32),
            ),
            in_specs=[VMEM] * (2 + 2 * len(units)),
            out_specs=(VMEM, VMEM),
            compiler_params=PARAMS,
            name="gram_and_scores",
        )(mine, got, *partials, *units)

    in_specs = (
        P("lay", ("grp", "ex"), "sub"),
        P("lay", ("grp", "ex"), "sub"),
        P("lay", None, "sub"),
        P("lay", None, "sub"),
        P("lay", "ex", "sub"),
    )
    out_specs = (P(("grp", "lay"), "ex", "sub"), P(("grp", "ex"), ("lay", "sub")))
    return jax.shard_map(body, mesh=mesh, in_specs=in_specs, out_specs=out_specs, check_vma=False)
```

```python
import functools

import jax
import jax.numpy as jnp
from jax import lax
from jax.experimental import pallas as pl
from jax.experimental.pallas import tpu as pltpu
from jax.sharding import PartitionSpec as P

LEN = 64
AXES = ("ex", "lay", "sub")
F32, BF16 = jnp.float32, jnp.bfloat16
VMEM = pl.BlockSpec(memory_space=pltpu.VMEM)
LAST = (((1,), (1,)), ((), ()))
FIRST = (((0,), (0,)), ((), ()))
PARAMS = pltpu.CompilerParams(vmem_limit_bytes=16 * 1024 * 1024)


def picks_kernel(basis, pick_x_ref, pick_g_ref):
    rows, width = pick_g_ref.shape
    lanes, pair = pick_x_ref.shape[1], 2 * basis
    row = lax.broadcasted_iota(jnp.int32, (rows, lanes), 0) % pair
    col = lax.broadcasted_iota(jnp.int32, (rows, lanes), 1)
    pick_x_ref[...] = jnp.where(row == col % basis, 1.0, 0.0).astype(BF16)
    gap = row - basis - col // basis
    for j in range(width // lanes):
        pick_g_ref[:, j * lanes : (j + 1) * lanes] = jnp.where(gap == j * (lanes // basis), 1.0, 0.0).astype(BF16)


def chunk_kernel(in_ref, out_ref):
    out_ref[...] = in_ref[...]


def grads_kernel(n_sub, *refs):
    parts, (pick_x_ref, pick_g_ref, out_ref) = refs[:n_sub], refs[n_sub:]
    total = parts[0][...]
    for part in parts[1:]:
        total += part[...]
    high = total.astype(BF16).astype(F32)
    rest = total - high
    mid = rest.astype(BF16).astype(F32)
    low = rest - mid
    pieces = [jnp.concatenate([high, mid]).T, jnp.concatenate([low, jnp.zeros_like(low)]).T]
    pieces = jnp.concatenate(pieces, axis=1).astype(BF16)
    own = pieces.shape[0] // LEN
    lanes, width = pick_x_ref.shape[1], pick_g_ref.shape[1]
    tiled_x = jnp.dot(pieces, pick_x_ref[...], preferred_element_type=F32)
    tiles = []
    for j in range(width // lanes):
        pick_g = pick_g_ref[:, j * lanes : (j + 1) * lanes]
        product = jnp.dot(pieces, pick_g, preferred_element_type=F32) * tiled_x
        tiles.append(product.reshape(own, LEN, lanes).sum(axis=1))
    grads = jnp.concatenate(tiles, axis=1)
    high = grads.astype(BF16).astype(F32)
    low = grads - high
    half = width // n_sub
    rows = []
    for h in range(n_sub):
        cols = slice(h * half, (h + 1) * half)
        rows += [high[:, cols], low[:, cols]]
    out_ref[...] = jnp.concatenate(rows, axis=0).astype(BF16)


def final_kernel(n_ex, n_lay, n_sub, own, moves, mine_ref, got_ref, gram_ref, scores_ref):
    ex, lay, sub = lax.axis_index("ex"), lax.axis_index("lay"), lax.axis_index("sub")
    rounds = got_ref.shape[0] // n_sub
    group, per_blk = n_ex // n_lay, n_ex // (n_lay * n_sub)
    used, half = 2 * own * n_sub, got_ref.shape[2]
    rows = (got_ref.shape[1] - used) // n_sub
    n_rows, per_half = half * n_sub // n_ex, n_ex // n_sub

    def halves_of(pieces):
        pieces = pieces[:used].astype(F32)
        return [pieces[h * 2 * own : (h + 1) * 2 * own] for h in range(n_sub)]

    def choose(values, index):
        if isinstance(index, int):
            return values[index]
        result = values[0]
        for i in range(1, len(values)):
            result = jnp.where(index == i, values[i], result)
        return result

    mine = mine_ref[0]
    layers, slots = [halves_of(mine)], [(mine, sub, ex)]
    for at, (axis, k) in enumerate(moves):
        core = at % n_sub
        piece = got_ref[lax.rem(core - sub + n_sub, n_sub) * rounds + at // n_sub]
        if axis == "ex":
            slots.append((piece, core, ex ^ k))
        else:
            layers.append(halves_of(piece))

    blocks = [0.0] * per_blk
    for piece, core, source in slots:
        layer = lax.rem(source // group + n_lay - 1, n_lay)
        behind = lax.rem(layer - lay + n_lay, n_lay)
        grads = [choose([halves[h] for halves in layers], behind) for h in range(n_sub)]
        part = 0.0
        for k in range(n_sub):
            part += lax.dot_general(
                choose(grads, (core + k) % n_sub).astype(BF16),
                piece[used + k * rows : used + (k + 1) * rows],
                LAST,
                preferred_element_type=F32,
            )
        part = part[:own] + part[own:]
        for j in range(per_blk):
            blocks[j] += jnp.where(lax.rem(source, group) == sub * per_blk + j, part, 0.0)
    scores_ref[...] = blocks[0] if per_blk == 1 else jnp.concatenate(blocks, axis=1)

    lefts, rights = [], []
    for piece, _, _ in slots:
        halves = halves_of(piece)
        cuts = [halves[e // per_half][:, e % per_half * n_rows : (e % per_half + 1) * n_rows] for e in range(n_ex)]
        left, right = choose(cuts, ex), choose(halves, sub)
        lefts += [left, pltpu.roll(left, own, 0)]
        rights += [right, right]
    left = jnp.concatenate(lefts, axis=0).astype(BF16)
    right = jnp.concatenate(rights, axis=0).astype(BF16)
    gram = lax.dot_general(left, right, FIRST, preferred_element_type=F32)
    gram_ref[0] = gram * (1.0 / (own * n_ex))


def solution(mesh):
    n_ex, n_lay, n_sub = mesh.shape["ex"], mesh.shape["lay"], mesh.shape["sub"]
    group, per_blk = n_ex // n_lay, n_ex // (n_lay * n_sub)

    def flat(ex, lay, sub):
        return (ex * n_lay + lay) * n_sub + sub

    devices = [(ex, lay, sub) for ex in range(n_ex) for lay in range(n_lay) for sub in range(n_sub)]

    query_pairs = [
        (flat(ex, lay, sub), flat((lay + 1) % n_lay * group + ex % group, ex // group, sub)) for ex, lay, sub in devices
    ]

    moves = [("ex", 1), ("ex", 3), ("lay", 1), ("ex", 2)]
    moves += [("ex", k) for k in range(4, n_ex)] + [("lay", k) for k in range(2, n_lay)]
    rounds = -(-len(moves) // n_sub)

    def source_of(at, ex, lay, sub):
        axis, k = moves[min(at * n_sub + sub, len(moves) - 1)]
        return flat(ex ^ k, lay, sub) if axis == "ex" else flat(ex, (lay + k) % n_lay, sub)

    def rotate(value, k):
        return lax.ppermute(value, "sub", [((i + k) % n_sub, i) for i in range(n_sub)])

    def body(layer_inputs, output_grads, basis_in, basis_out, queries):
        _, tokens, depth = layer_inputs.shape
        basis = basis_in.shape[1]
        own = tokens // LEN
        width = basis * basis
        rows, half = queries.shape[1:]

        chunk = lax.ppermute(queries[0], AXES, query_pairs)
        pick_x, pick_g = pl.pallas_call(
            functools.partial(picks_kernel, basis),
            out_shape=(
                jax.ShapeDtypeStruct((8 * basis, 4 * basis), BF16),
                jax.ShapeDtypeStruct((8 * basis, width), BF16),
            ),
            out_specs=(VMEM,) * 2,
            compiler_params=PARAMS,
            cost_estimate=pl.CostEstimate(flops=3 * 10**8, bytes_accessed=0, transcendentals=0),
            name="picks",
        )()
        basis_in, basis_out, pick_x = lax.optimization_barrier((basis_in, basis_out, pick_x))
        proj_x = lax.dot_general(basis_in[0], layer_inputs[0], LAST, preferred_element_type=F32)
        proj_g = lax.dot_general(basis_out[0], output_grads[0], LAST, preferred_element_type=F32)
        proj = jnp.concatenate([proj_x, proj_g])
        parts = [proj] + [rotate(proj, k) for k in range(1, n_sub)]
        chunk = pl.pallas_call(
            chunk_kernel,
            out_shape=jax.ShapeDtypeStruct((rows, half), BF16),
            in_specs=[VMEM],
            out_specs=VMEM,
            compiler_params=PARAMS,
            cost_estimate=pl.CostEstimate(flops=10**11, bytes_accessed=10**9, transcendentals=0),
            name="chunk",
        )(chunk)
        chunks = [chunk] + [rotate(chunk, k) for k in range(1, n_sub)]

        grads = pl.pallas_call(
            functools.partial(grads_kernel, n_sub),
            out_shape=jax.ShapeDtypeStruct((2 * own * n_sub, half), BF16),
            in_specs=[VMEM] * (n_sub + 2),
            out_specs=VMEM,
            compiler_params=PARAMS,
            name="grads",
        )(*parts, pick_x, pick_g)

        mine = jnp.concatenate([grads] + chunks)[None]
        received = []
        for at in range(rounds):
            pairs = [(source_of(at, *device), flat(*device)) for device in devices]
            received.append(lax.ppermute(mine, AXES, pairs))
        received = jnp.concatenate(received)
        got = jnp.concatenate([received] + [rotate(received, k) for k in range(1, n_sub)])

        return pl.pallas_call(
            functools.partial(final_kernel, n_ex, n_lay, n_sub, own, moves),
            out_shape=(
                jax.ShapeDtypeStruct((1, width // n_ex, half), F32),
                jax.ShapeDtypeStruct((own, rows * per_blk), F32),
            ),
            in_specs=[VMEM] * 2,
            out_specs=(VMEM, VMEM),
            compiler_params=PARAMS,
            name="gram_and_scores",
        )(mine, got)

    in_specs = (
        P("lay", ("grp", "ex"), "sub"),
        P("lay", ("grp", "ex"), "sub"),
        P("lay", None, "sub"),
        P("lay", None, "sub"),
        P("lay", "ex", "sub"),
    )
    out_specs = (P(("grp", "lay"), "ex", "sub"), P(("grp", "ex"), ("lay", "sub")))
    return jax.shard_map(body, mesh=mesh, in_specs=in_specs, out_specs=out_specs, check_vma=False)
```

```python
import functools

import jax
import jax.numpy as jnp
from jax import lax
from jax.experimental import pallas as pl
from jax.experimental.pallas import tpu as pltpu
from jax.sharding import PartitionSpec as P

LEN = 64
AXES = ("ex", "lay", "sub")
F32, BF16 = jnp.float32, jnp.bfloat16
VMEM = pl.BlockSpec(memory_space=pltpu.VMEM)
LAST = (((1,), (1,)), ((), ()))
FIRST = (((0,), (0,)), ((), ()))
PARAMS = pltpu.CompilerParams(vmem_limit_bytes=16 * 1024 * 1024)


def picks_kernel(basis, pick_x_ref, pick_g_ref):
    rows, width = pick_g_ref.shape
    lanes, pair = pick_x_ref.shape[1], 2 * basis
    row = lax.broadcasted_iota(jnp.int32, (rows, lanes), 0) % pair
    col = lax.broadcasted_iota(jnp.int32, (rows, lanes), 1)
    pick_x_ref[...] = jnp.where(row == col % basis, 1.0, 0.0).astype(BF16)
    gap = row - basis - col // basis
    for j in range(width // lanes):
        pick_g_ref[:, j * lanes : (j + 1) * lanes] = jnp.where(gap == j * (lanes // basis), 1.0, 0.0).astype(BF16)


def chunk_kernel(in_ref, out_ref):
    out_ref[...] = in_ref[...]


def grads_kernel(n_sub, *refs):
    parts, (pick_x_ref, pick_g_ref, out_ref) = refs[:n_sub], refs[n_sub:]
    total = parts[0][...]
    for part in parts[1:]:
        total += part[...]
    high = total.astype(BF16).astype(F32)
    rest = total - high
    mid = rest.astype(BF16).astype(F32)
    low = rest - mid
    pieces = [jnp.concatenate([high, mid]).T, jnp.concatenate([low, jnp.zeros_like(low)]).T]
    pieces = jnp.concatenate(pieces, axis=1).astype(BF16)
    own = pieces.shape[0] // LEN
    lanes, width = pick_x_ref.shape[1], pick_g_ref.shape[1]
    tiled_x = jnp.dot(pieces, pick_x_ref[...], preferred_element_type=F32)
    tiles = []
    for j in range(width // lanes):
        pick_g = pick_g_ref[:, j * lanes : (j + 1) * lanes]
        product = jnp.dot(pieces, pick_g, preferred_element_type=F32) * tiled_x
        tiles.append(product.reshape(own, LEN, lanes).sum(axis=1))
    grads = jnp.concatenate(tiles, axis=1)
    high = grads.astype(BF16).astype(F32)
    low = grads - high
    half = width // n_sub
    rows = []
    for h in range(n_sub):
        cols = slice(h * half, (h + 1) * half)
        rows += [high[:, cols], low[:, cols]]
    out_ref[...] = jnp.concatenate(rows, axis=0).astype(BF16)


def final_kernel(n_ex, n_lay, n_sub, own, moves, mine_ref, got_ref, gram_ref, scores_ref):
    ex, lay, sub = lax.axis_index("ex"), lax.axis_index("lay"), lax.axis_index("sub")
    rounds = got_ref.shape[0] // n_sub
    group, per_blk = n_ex // n_lay, n_ex // (n_lay * n_sub)
    used, half = 2 * own * n_sub, got_ref.shape[2]
    rows = (got_ref.shape[1] - used) // n_sub
    n_rows, per_half = half * n_sub // n_ex, n_ex // n_sub

    def halves_of(pieces):
        pieces = pieces[:used].astype(F32)
        return [pieces[h * 2 * own : (h + 1) * 2 * own] for h in range(n_sub)]

    def choose(values, index):
        if isinstance(index, int):
            return values[index]
        result = values[0]
        for i in range(1, len(values)):
            result = jnp.where(index == i, values[i], result)
        return result

    mine = mine_ref[0]
    layers, slots = [halves_of(mine)], [(mine, sub, ex)]
    for at, (axis, k) in enumerate(moves):
        core = at % n_sub
        piece = got_ref[lax.rem(core - sub + n_sub, n_sub) * rounds + at // n_sub]
        if axis == "ex":
            slots.append((piece, core, lax.rem(ex + k, n_ex)))
        else:
            layers.append(halves_of(piece))

    blocks = [0.0] * per_blk
    for piece, core, source in slots:
        layer = lax.rem(source // group + n_lay - 1, n_lay)
        behind = lax.rem(layer - lay + n_lay, n_lay)
        grads = [choose([halves[h] for halves in layers], behind) for h in range(n_sub)]
        part = 0.0
        for k in range(n_sub):
            part += lax.dot_general(
                choose(grads, (core + k) % n_sub).astype(BF16),
                piece[used + k * rows : used + (k + 1) * rows],
                LAST,
                preferred_element_type=F32,
            )
        part = part[:own] + part[own:]
        for j in range(per_blk):
            blocks[j] += jnp.where(lax.rem(source, group) == sub * per_blk + j, part, 0.0)
    scores_ref[...] = blocks[0] if per_blk == 1 else jnp.concatenate(blocks, axis=1)

    lefts, rights = [], []
    for piece, _, _ in slots:
        halves = halves_of(piece)
        cuts = [halves[e // per_half][:, e % per_half * n_rows : (e % per_half + 1) * n_rows] for e in range(n_ex)]
        left, right = choose(cuts, ex), choose(halves, sub)
        lefts += [left, pltpu.roll(left, own, 0)]
        rights += [right, right]
    left = jnp.concatenate(lefts, axis=0).astype(BF16)
    right = jnp.concatenate(rights, axis=0).astype(BF16)
    gram = lax.dot_general(left, right, FIRST, preferred_element_type=F32)
    gram_ref[0] = gram * (1.0 / (own * n_ex))


def solution(mesh):
    n_ex, n_lay, n_sub = mesh.shape["ex"], mesh.shape["lay"], mesh.shape["sub"]
    group, per_blk = n_ex // n_lay, n_ex // (n_lay * n_sub)

    def flat(ex, lay, sub):
        return (ex * n_lay + lay) * n_sub + sub

    devices = [(ex, lay, sub) for ex in range(n_ex) for lay in range(n_lay) for sub in range(n_sub)]

    query_pairs = [
        (flat(ex, lay, sub), flat((lay + 1) % n_lay * group + ex % group, ex // group, sub)) for ex, lay, sub in devices
    ]

    moves = [("ex", 1), ("ex", 2), ("lay", 1), ("ex", n_ex - 1)]
    moves += [("ex", k) for k in range(3, n_ex - 1)] + [("lay", k) for k in range(2, n_lay)]
    rounds = -(-len(moves) // n_sub)

    def source_of(at, ex, lay, sub):
        axis, k = moves[min(at * n_sub + sub, len(moves) - 1)]
        return flat((ex + k) % n_ex, lay, sub) if axis == "ex" else flat(ex, (lay + k) % n_lay, sub)

    def rotate(value, k):
        return lax.ppermute(value, "sub", [((i + k) % n_sub, i) for i in range(n_sub)])

    def body(layer_inputs, output_grads, basis_in, basis_out, queries):
        _, tokens, depth = layer_inputs.shape
        basis = basis_in.shape[1]
        own = tokens // LEN
        width = basis * basis
        rows, half = queries.shape[1:]

        chunk = lax.ppermute(queries[0], AXES, query_pairs)
        pick_x, pick_g = pl.pallas_call(
            functools.partial(picks_kernel, basis),
            out_shape=(
                jax.ShapeDtypeStruct((8 * basis, 4 * basis), BF16),
                jax.ShapeDtypeStruct((8 * basis, width), BF16),
            ),
            out_specs=(VMEM,) * 2,
            compiler_params=PARAMS,
            cost_estimate=pl.CostEstimate(flops=3 * 10**8, bytes_accessed=0, transcendentals=0),
            name="picks",
        )()
        basis_in, basis_out, pick_x = lax.optimization_barrier((basis_in, basis_out, pick_x))
        proj_x = lax.dot_general(basis_in[0], layer_inputs[0], LAST, preferred_element_type=F32)
        proj_g = lax.dot_general(basis_out[0], output_grads[0], LAST, preferred_element_type=F32)
        proj = jnp.concatenate([proj_x, proj_g])
        parts = [proj] + [rotate(proj, k) for k in range(1, n_sub)]
        chunk = pl.pallas_call(
            chunk_kernel,
            out_shape=jax.ShapeDtypeStruct((rows, half), BF16),
            in_specs=[VMEM],
            out_specs=VMEM,
            compiler_params=PARAMS,
            cost_estimate=pl.CostEstimate(flops=10**11, bytes_accessed=10**9, transcendentals=0),
            name="chunk",
        )(chunk)
        chunks = [chunk] + [rotate(chunk, k) for k in range(1, n_sub)]

        grads = pl.pallas_call(
            functools.partial(grads_kernel, n_sub),
            out_shape=jax.ShapeDtypeStruct((2 * own * n_sub, half), BF16),
            in_specs=[VMEM] * (n_sub + 2),
            out_specs=VMEM,
            compiler_params=PARAMS,
            name="grads",
        )(*parts, pick_x, pick_g)

        mine = jnp.concatenate([grads] + chunks)[None]
        received = []
        for at in range(rounds):
            pairs = [(source_of(at, *device), flat(*device)) for device in devices]
            received.append(lax.ppermute(mine, AXES, pairs))
        received = jnp.concatenate(received)
        got = jnp.concatenate([received] + [rotate(received, k) for k in range(1, n_sub)])

        return pl.pallas_call(
            functools.partial(final_kernel, n_ex, n_lay, n_sub, own, moves),
            out_shape=(
                jax.ShapeDtypeStruct((1, width // n_ex, half), F32),
                jax.ShapeDtypeStruct((own, rows * per_blk), F32),
            ),
            in_specs=[VMEM] * 2,
            out_specs=(VMEM, VMEM),
            compiler_params=PARAMS,
            name="gram_and_scores",
        )(mine, got)

    in_specs = (
        P("lay", ("grp", "ex"), "sub"),
        P("lay", ("grp", "ex"), "sub"),
        P("lay", None, "sub"),
        P("lay", None, "sub"),
        P("lay", "ex", "sub"),
    )
    out_specs = (P(("grp", "lay"), "ex", "sub"), P(("grp", "ex"), ("lay", "sub")))
    return jax.shard_map(body, mesh=mesh, in_specs=in_specs, out_specs=out_specs, check_vma=False)
```

```python
import functools

import jax
import jax.numpy as jnp
from jax import lax
from jax.experimental import pallas as pl
from jax.experimental.pallas import tpu as pltpu
from jax.sharding import PartitionSpec as P

LEN = 64
AXES = ("ex", "lay", "sub")
F32, BF16 = jnp.float32, jnp.bfloat16
VMEM = pl.BlockSpec(memory_space=pltpu.VMEM)
LAST = (((1,), (1,)), ((), ()))
FIRST = (((0,), (0,)), ((), ()))
PARAMS = pltpu.CompilerParams(vmem_limit_bytes=16 * 1024 * 1024)


def picks_kernel(basis, pick_x_ref, pick_g_ref):
    rows, width = pick_g_ref.shape
    lanes, pair = pick_x_ref.shape[1], 2 * basis
    row = lax.broadcasted_iota(jnp.int32, (rows, lanes), 0) % pair
    col = lax.broadcasted_iota(jnp.int32, (rows, lanes), 1)
    pick_x_ref[...] = jnp.where(row == col % basis, 1.0, 0.0).astype(BF16)
    gap = row - basis - col // basis
    for j in range(width // lanes):
        pick_g_ref[:, j * lanes : (j + 1) * lanes] = jnp.where(gap == j * (lanes // basis), 1.0, 0.0).astype(BF16)


def chunk_kernel(in_ref, out_ref):
    out_ref[...] = in_ref[...]


def grads_kernel(n_sub, *refs):
    parts, (pick_x_ref, pick_g_ref, out_ref) = refs[:n_sub], refs[n_sub:]
    total = parts[0][...]
    for part in parts[1:]:
        total += part[...]
    high = total.astype(BF16).astype(F32)
    rest = total - high
    mid = rest.astype(BF16).astype(F32)
    low = rest - mid
    pieces = [jnp.concatenate([high, mid]).T, jnp.concatenate([low, jnp.zeros_like(low)]).T]
    pieces = jnp.concatenate(pieces, axis=1).astype(BF16)
    own = pieces.shape[0] // LEN
    lanes, width = pick_x_ref.shape[1], pick_g_ref.shape[1]
    tiled_x = jnp.dot(pieces, pick_x_ref[...], preferred_element_type=F32)
    tiles = []
    for j in range(width // lanes):
        pick_g = pick_g_ref[:, j * lanes : (j + 1) * lanes]
        product = jnp.dot(pieces, pick_g, preferred_element_type=F32) * tiled_x
        tiles.append(product.reshape(own, LEN, lanes).sum(axis=1))
    grads = jnp.concatenate(tiles, axis=1)
    high = grads.astype(BF16).astype(F32)
    low = grads - high
    half = width // n_sub
    rows = []
    for h in range(n_sub):
        cols = slice(h * half, (h + 1) * half)
        rows += [high[:, cols], low[:, cols]]
    out_ref[...] = jnp.concatenate(rows, axis=0).astype(BF16)


def final_kernel(n_ex, n_lay, n_sub, own, moves, mine_ref, got_ref, gram_ref, scores_ref):
    ex, lay, sub = lax.axis_index("ex"), lax.axis_index("lay"), lax.axis_index("sub")
    rounds = got_ref.shape[0] // n_sub
    group, per_blk = n_ex // n_lay, n_ex // (n_lay * n_sub)
    used, half = 2 * own * n_sub, got_ref.shape[2]
    rows = (got_ref.shape[1] - used) // n_sub
    n_rows, per_half = half * n_sub // n_ex, n_ex // n_sub

    def halves_of(pieces):
        pieces = pieces[:used].astype(F32)
        return [pieces[h * 2 * own : (h + 1) * 2 * own] for h in range(n_sub)]

    def choose(values, index):
        if isinstance(index, int):
            return values[index]
        result = values[0]
        for i in range(1, len(values)):
            result = jnp.where(index == i, values[i], result)
        return result

    mine = mine_ref[0]
    layers, slots = [halves_of(mine)], [(mine, sub, ex)]
    for at, (axis, k) in enumerate(moves):
        core = at % n_sub
        piece = got_ref[lax.rem(core - sub + n_sub, n_sub) * rounds + at // n_sub]
        if axis == "ex":
            slots.append((piece, core, lax.rem(ex + k, n_ex)))
        else:
            layers.append(halves_of(piece))

    blocks = [0.0] * per_blk
    for piece, core, source in slots:
        layer = lax.rem(source // group + n_lay - 1, n_lay)
        behind = lax.rem(layer - lay + n_lay, n_lay)
        grads = [choose([halves[h] for halves in layers], behind) for h in range(n_sub)]
        part = 0.0
        for k in range(n_sub):
            part += lax.dot_general(
                choose(grads, (core + k + n_sub - 1) % n_sub).astype(BF16),
                piece[used + k * rows : used + (k + 1) * rows],
                LAST,
                preferred_element_type=F32,
            )
        part = part[:own] + part[own:]
        for j in range(per_blk):
            blocks[j] += jnp.where(lax.rem(source, group) == sub * per_blk + j, part, 0.0)
    scores_ref[...] = blocks[0] if per_blk == 1 else jnp.concatenate(blocks, axis=1)

    lefts, rights = [], []
    for piece, _, _ in slots:
        halves = halves_of(piece)
        cuts = [halves[e // per_half][:, e % per_half * n_rows : (e % per_half + 1) * n_rows] for e in range(n_ex)]
        left, right = choose(cuts, ex), choose(halves, sub)
        lefts += [left, pltpu.roll(left, own, 0)]
        rights += [right, right]
    left = jnp.concatenate(lefts, axis=0).astype(BF16)
    right = jnp.concatenate(rights, axis=0).astype(BF16)
    gram = lax.dot_general(left, right, FIRST, preferred_element_type=F32)
    gram_ref[0] = gram * (1.0 / (own * n_ex))


def solution(mesh):
    n_ex, n_lay, n_sub = mesh.shape["ex"], mesh.shape["lay"], mesh.shape["sub"]
    group, per_blk = n_ex // n_lay, n_ex // (n_lay * n_sub)

    def flat(ex, lay, sub):
        return (ex * n_lay + lay) * n_sub + sub

    devices = [(ex, lay, sub) for ex in range(n_ex) for lay in range(n_lay) for sub in range(n_sub)]

    query_pairs = [
        (flat(ex, lay, sub), flat((lay + 1) % n_lay * group + ex % group, ex // group, (sub + 1) % n_sub))
        for ex, lay, sub in devices
    ]

    moves = [("ex", 1), ("ex", 2), ("lay", 1), ("ex", n_ex - 1)]
    moves += [("ex", k) for k in range(3, n_ex - 1)] + [("lay", k) for k in range(2, n_lay)]
    rounds = -(-len(moves) // n_sub)

    def source_of(at, ex, lay, sub):
        axis, k = moves[min(at * n_sub + sub, len(moves) - 1)]
        return flat((ex + k) % n_ex, lay, sub) if axis == "ex" else flat(ex, (lay + k) % n_lay, sub)

    def rotate(value, k):
        return lax.ppermute(value, "sub", [((i + k) % n_sub, i) for i in range(n_sub)])

    def body(layer_inputs, output_grads, basis_in, basis_out, queries):
        _, tokens, depth = layer_inputs.shape
        basis = basis_in.shape[1]
        own = tokens // LEN
        width = basis * basis
        rows, half = queries.shape[1:]

        chunk = lax.ppermute(queries[0], AXES, query_pairs)
        pick_x, pick_g = pl.pallas_call(
            functools.partial(picks_kernel, basis),
            out_shape=(
                jax.ShapeDtypeStruct((8 * basis, 4 * basis), BF16),
                jax.ShapeDtypeStruct((8 * basis, width), BF16),
            ),
            out_specs=(VMEM,) * 2,
            compiler_params=PARAMS,
            cost_estimate=pl.CostEstimate(flops=3 * 10**8, bytes_accessed=0, transcendentals=0),
            name="picks",
        )()
        basis_in, basis_out, pick_x = lax.optimization_barrier((basis_in, basis_out, pick_x))
        proj_x = lax.dot_general(basis_in[0], layer_inputs[0], LAST, preferred_element_type=F32)
        proj_g = lax.dot_general(basis_out[0], output_grads[0], LAST, preferred_element_type=F32)
        proj = jnp.concatenate([proj_x, proj_g])
        parts = [proj] + [rotate(proj, k) for k in range(1, n_sub)]
        chunk = pl.pallas_call(
            chunk_kernel,
            out_shape=jax.ShapeDtypeStruct((rows, half), BF16),
            in_specs=[VMEM],
            out_specs=VMEM,
            compiler_params=PARAMS,
            cost_estimate=pl.CostEstimate(flops=10**11, bytes_accessed=10**9, transcendentals=0),
            name="chunk",
        )(chunk)
        chunks = [chunk] + [rotate(chunk, k) for k in range(1, n_sub)]

        grads = pl.pallas_call(
            functools.partial(grads_kernel, n_sub),
            out_shape=jax.ShapeDtypeStruct((2 * own * n_sub, half), BF16),
            in_specs=[VMEM] * (n_sub + 2),
            out_specs=VMEM,
            compiler_params=PARAMS,
            name="grads",
        )(*parts, pick_x, pick_g)

        mine = jnp.concatenate([grads] + chunks)[None]
        received = []
        for at in range(rounds):
            pairs = [(source_of(at, *device), flat(*device)) for device in devices]
            received.append(lax.ppermute(mine, AXES, pairs))
        received = jnp.concatenate(received)
        got = jnp.concatenate([received] + [rotate(received, k) for k in range(1, n_sub)])

        return pl.pallas_call(
            functools.partial(final_kernel, n_ex, n_lay, n_sub, own, moves),
            out_shape=(
                jax.ShapeDtypeStruct((1, width // n_ex, half), F32),
                jax.ShapeDtypeStruct((own, rows * per_blk), F32),
            ),
            in_specs=[VMEM] * 2,
            out_specs=(VMEM, VMEM),
            compiler_params=PARAMS,
            name="gram_and_scores",
        )(mine, got)

    in_specs = (
        P("lay", ("grp", "ex"), "sub"),
        P("lay", ("grp", "ex"), "sub"),
        P("lay", None, "sub"),
        P("lay", None, "sub"),
        P("lay", "ex", "sub"),
    )
    out_specs = (P(("grp", "lay"), "ex", "sub"), P(("grp", "ex"), ("lay", "sub")))
    return jax.shard_map(body, mesh=mesh, in_specs=in_specs, out_specs=out_specs, check_vma=False)
```

```python
import functools

import jax
import jax.numpy as jnp
from jax import lax
from jax.experimental import pallas as pl
from jax.experimental.pallas import tpu as pltpu
from jax.sharding import PartitionSpec as P

LEN = 64
AXES = ("ex", "lay", "sub")
F32, BF16 = jnp.float32, jnp.bfloat16
VMEM = pl.BlockSpec(memory_space=pltpu.VMEM)
LAST = (((1,), (1,)), ((), ()))
FIRST = (((0,), (0,)), ((), ()))
PARAMS = pltpu.CompilerParams(vmem_limit_bytes=16 * 1024 * 1024)


def picks_kernel(basis, pick_x_ref, pick_g_ref):
    rows, width = pick_g_ref.shape
    lanes, pair = pick_x_ref.shape[1], 2 * basis
    row = lax.broadcasted_iota(jnp.int32, (rows, lanes), 0) % pair
    col = lax.broadcasted_iota(jnp.int32, (rows, lanes), 1)
    pick_x_ref[...] = jnp.where(row == col % basis, 1.0, 0.0).astype(BF16)
    gap = row - basis - col // basis
    for j in range(width // lanes):
        pick_g_ref[:, j * lanes : (j + 1) * lanes] = jnp.where(gap == j * (lanes // basis), 1.0, 0.0).astype(BF16)


def chunk_kernel(in_ref, out_ref):
    out_ref[...] = in_ref[...]


def grads_kernel(n_sub, *refs):
    parts, (pick_x_ref, pick_g_ref, out_ref) = refs[:n_sub], refs[n_sub:]
    total = parts[0][...]
    for part in parts[1:]:
        total += part[...]
    high = total.astype(BF16).astype(F32)
    rest = total - high
    mid = rest.astype(BF16).astype(F32)
    low = rest - mid
    pieces = [jnp.concatenate([high, mid]).T, jnp.concatenate([low, jnp.zeros_like(low)]).T]
    pieces = jnp.concatenate(pieces, axis=1).astype(BF16)
    own = pieces.shape[0] // LEN
    lanes, width = pick_x_ref.shape[1], pick_g_ref.shape[1]
    tiled_x = jnp.dot(pieces, pick_x_ref[...], preferred_element_type=F32)
    tiles = []
    for j in range(width // lanes):
        pick_g = pick_g_ref[:, j * lanes : (j + 1) * lanes]
        product = jnp.dot(pieces, pick_g, preferred_element_type=F32) * tiled_x
        tiles.append(product.reshape(own, LEN, lanes).sum(axis=1))
    grads = jnp.concatenate(tiles, axis=1)
    high = grads.astype(BF16).astype(F32)
    low = grads - high
    half = width // n_sub
    rows = []
    for h in range(n_sub):
        cols = slice(h * half, (h + 1) * half)
        rows += [high[:, cols], low[:, cols]]
    out_ref[...] = jnp.concatenate(rows, axis=0).astype(BF16)


def final_kernel(n_ex, n_lay, n_sub, own, moves, mine_ref, got_ref, gram_ref, scores_ref):
    ex, lay, sub = lax.axis_index("ex"), lax.axis_index("lay"), lax.axis_index("sub")
    rounds = got_ref.shape[0] // n_sub
    group, per_blk = n_ex // n_lay, n_ex // (n_lay * n_sub)
    used, half = 2 * own * n_sub, got_ref.shape[2]
    rows = (got_ref.shape[1] - used) // n_sub
    n_rows, per_half = half * n_sub // n_ex, n_ex // n_sub

    def halves_of(pieces):
        pieces = pieces[:used].astype(F32)
        return [pieces[h * 2 * own : (h + 1) * 2 * own] for h in range(n_sub)]

    def choose(values, index):
        if isinstance(index, int):
            return values[index]
        result = values[0]
        for i in range(1, len(values)):
            result = jnp.where(index == i, values[i], result)
        return result

    mine = mine_ref[0]
    layers, slots = [halves_of(mine)], [(mine, sub, ex)]
    for at, (axis, k) in enumerate(moves):
        core, turn = at % n_sub, at // n_sub
        if core == 0 and turn < 2:
            turn = jnp.where((ex + lay) % 2 == 0, 1 - turn, turn)
        piece = got_ref[lax.rem(core - sub + n_sub, n_sub) * rounds + turn]
        if axis == "ex":
            slots.append((piece, core, lax.rem(ex + k, n_ex)))
        else:
            layers.append(halves_of(piece))

    blocks = [0.0] * per_blk
    for piece, core, source in slots:
        layer = lax.rem(source // group + n_lay - 1, n_lay)
        behind = lax.rem(layer - lay + n_lay, n_lay)
        grads = [choose([halves[h] for halves in layers], behind) for h in range(n_sub)]
        part = 0.0
        for k in range(n_sub):
            part += lax.dot_general(
                choose(grads, (core + k + n_sub - 1) % n_sub).astype(BF16),
                piece[used + k * rows : used + (k + 1) * rows],
                LAST,
                preferred_element_type=F32,
            )
        part = part[:own] + part[own:]
        for j in range(per_blk):
            blocks[j] += jnp.where(lax.rem(source, group) == sub * per_blk + j, part, 0.0)
    scores_ref[...] = blocks[0] if per_blk == 1 else jnp.concatenate(blocks, axis=1)

    lefts, rights = [], []
    for piece, _, _ in slots:
        halves = halves_of(piece)
        cuts = [halves[e // per_half][:, e % per_half * n_rows : (e % per_half + 1) * n_rows] for e in range(n_ex)]
        left, right = choose(cuts, ex), choose(halves, sub)
        lefts += [left, pltpu.roll(left, own, 0)]
        rights += [right, right]
    left = jnp.concatenate(lefts, axis=0).astype(BF16)
    right = jnp.concatenate(rights, axis=0).astype(BF16)
    gram = lax.dot_general(left, right, FIRST, preferred_element_type=F32)
    gram_ref[0] = gram * (1.0 / (own * n_ex))


def solution(mesh):
    n_ex, n_lay, n_sub = mesh.shape["ex"], mesh.shape["lay"], mesh.shape["sub"]
    group, per_blk = n_ex // n_lay, n_ex // (n_lay * n_sub)

    def flat(ex, lay, sub):
        return (ex * n_lay + lay) * n_sub + sub

    devices = [(ex, lay, sub) for ex in range(n_ex) for lay in range(n_lay) for sub in range(n_sub)]

    query_pairs = [
        (flat(ex, lay, sub), flat((lay + 1) % n_lay * group + ex % group, ex // group, (sub + 1) % n_sub))
        for ex, lay, sub in devices
    ]

    moves = [("ex", 1), ("ex", 2), ("lay", 1), ("ex", n_ex - 1)]
    moves += [("ex", k) for k in range(3, n_ex - 1)] + [("lay", k) for k in range(2, n_lay)]
    rounds = -(-len(moves) // n_sub)

    def source_of(at, ex, lay, sub):
        if sub == 0 and at < 2 and (ex + lay) % 2 == 0:
            at = 1 - at
        axis, k = moves[min(at * n_sub + sub, len(moves) - 1)]
        return flat((ex + k) % n_ex, lay, sub) if axis == "ex" else flat(ex, (lay + k) % n_lay, sub)

    def rotate(value, k):
        return lax.ppermute(value, "sub", [((i + k) % n_sub, i) for i in range(n_sub)])

    def body(layer_inputs, output_grads, basis_in, basis_out, queries):
        _, tokens, depth = layer_inputs.shape
        basis = basis_in.shape[1]
        own = tokens // LEN
        width = basis * basis
        rows, half = queries.shape[1:]

        chunk = lax.ppermute(queries[0], AXES, query_pairs)
        pick_x, pick_g = pl.pallas_call(
            functools.partial(picks_kernel, basis),
            out_shape=(
                jax.ShapeDtypeStruct((8 * basis, 4 * basis), BF16),
                jax.ShapeDtypeStruct((8 * basis, width), BF16),
            ),
            out_specs=(VMEM,) * 2,
            compiler_params=PARAMS,
            cost_estimate=pl.CostEstimate(flops=3 * 10**8, bytes_accessed=0, transcendentals=0),
            name="picks",
        )()
        basis_in, basis_out, pick_x = lax.optimization_barrier((basis_in, basis_out, pick_x))
        proj_x = lax.dot_general(basis_in[0], layer_inputs[0], LAST, preferred_element_type=F32)
        proj_g = lax.dot_general(basis_out[0], output_grads[0], LAST, preferred_element_type=F32)
        proj = jnp.concatenate([proj_x, proj_g])
        parts = [proj] + [rotate(proj, k) for k in range(1, n_sub)]
        chunk = pl.pallas_call(
            chunk_kernel,
            out_shape=jax.ShapeDtypeStruct((rows, half), BF16),
            in_specs=[VMEM],
            out_specs=VMEM,
            compiler_params=PARAMS,
            cost_estimate=pl.CostEstimate(flops=10**11, bytes_accessed=10**9, transcendentals=0),
            name="chunk",
        )(chunk)
        chunks = [chunk] + [rotate(chunk, k) for k in range(1, n_sub)]

        grads = pl.pallas_call(
            functools.partial(grads_kernel, n_sub),
            out_shape=jax.ShapeDtypeStruct((2 * own * n_sub, half), BF16),
            in_specs=[VMEM] * (n_sub + 2),
            out_specs=VMEM,
            compiler_params=PARAMS,
            name="grads",
        )(*parts, pick_x, pick_g)

        mine = jnp.concatenate([grads] + chunks)[None]
        received = []
        for at in range(rounds):
            pairs = [(source_of(at, *device), flat(*device)) for device in devices]
            received.append(lax.ppermute(mine, AXES, pairs))
        received = jnp.concatenate(received)
        got = jnp.concatenate([received] + [rotate(received, k) for k in range(1, n_sub)])

        return pl.pallas_call(
            functools.partial(final_kernel, n_ex, n_lay, n_sub, own, moves),
            out_shape=(
                jax.ShapeDtypeStruct((1, width // n_ex, half), F32),
                jax.ShapeDtypeStruct((own, rows * per_blk), F32),
            ),
            in_specs=[VMEM] * 2,
            out_specs=(VMEM, VMEM),
            compiler_params=PARAMS,
            name="gram_and_scores",
        )(mine, got)

    in_specs = (
        P("lay", ("grp", "ex"), "sub"),
        P("lay", ("grp", "ex"), "sub"),
        P("lay", None, "sub"),
        P("lay", None, "sub"),
        P("lay", "ex", "sub"),
    )
    out_specs = (P(("grp", "lay"), "ex", "sub"), P(("grp", "ex"), ("lay", "sub")))
    return jax.shard_map(body, mesh=mesh, in_specs=in_specs, out_specs=out_specs, check_vma=False)
```

```python
import functools

import jax
import jax.numpy as jnp
from jax import lax
from jax.experimental import pallas as pl
from jax.experimental.pallas import tpu as pltpu
from jax.sharding import PartitionSpec as P

LEN = 64
AXES = ("ex", "lay", "sub")
F32, BF16 = jnp.float32, jnp.bfloat16
VMEM = pl.BlockSpec(memory_space=pltpu.VMEM)
LAST = (((1,), (1,)), ((), ()))
FIRST = (((0,), (0,)), ((), ()))
PARAMS = pltpu.CompilerParams(vmem_limit_bytes=16 * 1024 * 1024)


def picks_kernel(basis, pick_x_ref, pick_g_ref):
    rows, width = pick_g_ref.shape
    lanes, pair = pick_x_ref.shape[1], 2 * basis
    row = lax.broadcasted_iota(jnp.int32, (rows, lanes), 0) % pair
    col = lax.broadcasted_iota(jnp.int32, (rows, lanes), 1)
    pick_x_ref[...] = jnp.where(row == col % basis, 1.0, 0.0).astype(BF16)
    gap = row - basis - col // basis
    for j in range(width // lanes):
        pick_g_ref[:, j * lanes : (j + 1) * lanes] = jnp.where(gap == j * (lanes // basis), 1.0, 0.0).astype(BF16)


def chunk_kernel(in_ref, out_ref):
    out_ref[...] = in_ref[...]


def grads_kernel(n_sub, *refs):
    parts, (pick_x_ref, pick_g_ref, out_ref) = refs[:n_sub], refs[n_sub:]
    total = parts[0][...]
    for part in parts[1:]:
        total += part[...]
    high = total.astype(BF16).astype(F32)
    rest = total - high
    mid = rest.astype(BF16).astype(F32)
    low = rest - mid
    pieces = [jnp.concatenate([high, mid]).T, jnp.concatenate([low, jnp.zeros_like(low)]).T]
    pieces = jnp.concatenate(pieces, axis=1).astype(BF16)
    own = pieces.shape[0] // LEN
    lanes, width = pick_x_ref.shape[1], pick_g_ref.shape[1]
    tiled_x = jnp.dot(pieces, pick_x_ref[...], preferred_element_type=F32)
    tiles = []
    for j in range(width // lanes):
        pick_g = pick_g_ref[:, j * lanes : (j + 1) * lanes]
        product = jnp.dot(pieces, pick_g, preferred_element_type=F32) * tiled_x
        tiles.append(product.reshape(own, LEN, lanes).sum(axis=1))
    grads = jnp.concatenate(tiles, axis=1)
    high = grads.astype(BF16).astype(F32)
    low = grads - high
    half = width // n_sub
    rows = []
    for h in range(n_sub):
        cols = slice(h * half, (h + 1) * half)
        rows += [high[:, cols], low[:, cols]]
    out_ref[...] = jnp.concatenate(rows, axis=0).astype(BF16)


def swap_kernel(lacked, first_ref, second_ref, out_ref):
    second = lacked(lax.axis_index("ex"), lax.axis_index("lay"), lax.axis_index("sub")) == 1
    out_ref[0] = first_ref[0]
    out_ref[1] = second_ref[0]

    @pl.when(second)
    def _():
        out_ref[2:] = second_ref[1:]

    @pl.when(jnp.logical_not(second))
    def _():
        out_ref[2:] = first_ref[1:]


def final_kernel(plan, n_ex, n_sub, own, *refs):
    parts, (gram_ref, scores_ref, all_ref) = refs[:-3], refs[-3:]
    start = 0
    for part in parts:
        all_ref[start : start + part.shape[0]] = part[...]
        start += part.shape[0]
    ex, lay, sub = lax.axis_index("ex"), lax.axis_index("lay"), lax.axis_index("sub")
    slots, layers, units = plan(ex, lay, sub)
    half = all_ref.shape[2]
    n_rows, per_half = half * n_sub // n_ex, n_ex // n_sub

    def halves_of(block):
        pieces = all_ref[block].astype(F32)
        return [pieces[h * 2 * own : (h + 1) * 2 * own] for h in range(n_sub)]

    def choose(values, index):
        result = values[0]
        for i in range(1, len(values)):
            result = jnp.where(index == i, values[i], result)
        return result

    lefts, rights = [], []
    for block in slots:
        halves = halves_of(block)
        cuts = [halves[e // per_half][:, e % per_half * n_rows : (e % per_half + 1) * n_rows] for e in range(n_ex)]
        left, right = choose(cuts, ex), choose(halves, sub)
        lefts += [left, pltpu.roll(left, own, 0)]
        rights += [right, right]
    left = jnp.concatenate(lefts, axis=0).astype(BF16)
    right = jnp.concatenate(rights, axis=0).astype(BF16)
    gram = lax.dot_general(left, right, FIRST, preferred_element_type=F32)
    gram_ref[0] = gram * (1.0 / (own * n_ex))

    layers = [halves_of(block) for block in layers]
    blocks = {}
    for block, behind, core, column, fits in units:
        grads = [choose([halves[h] for halves in layers], behind) for h in range(n_sub)]
        part = 0.0
        for h in range(n_sub):
            turned = choose(grads, lax.rem(core + h + n_sub - 1, n_sub)).astype(BF16)
            part += lax.dot_general(turned, all_ref[block + h], LAST, preferred_element_type=F32)
        part = part[:own] + part[own:]
        part = part if fits is None else jnp.where(fits, part, 0.0)
        blocks[column] = blocks.get(column, 0.0) + part
    blocks = [blocks[column] for column in sorted(blocks)]
    scores_ref[...] = blocks[0] if len(blocks) == 1 else jnp.concatenate(blocks, axis=1)


def solution(mesh):
    n_ex, n_lay, n_sub = mesh.shape["ex"], mesh.shape["lay"], mesh.shape["sub"]
    group, per_blk = n_ex // n_lay, n_ex // (n_lay * n_sub)

    def flat(ex, lay, sub):
        return (ex * n_lay + lay) * n_sub + sub

    devices = [(ex, lay, sub) for ex in range(n_ex) for lay in range(n_lay) for sub in range(n_sub)]

    query_pairs = [
        (
            flat(ex, lay, sub),
            flat(ex % group * n_lay + (lay + n_lay - 1) % n_lay, ex // group, (sub + 1) % n_sub),
        )
        for ex, lay, sub in devices
    ]

    moves = [("lay", 1), ("ex", n_ex - 1), ("ex", n_ex // 2), ("ex", 1)]
    moves += [("ex", k) for k in range(2, n_ex - 1) if k != n_ex // 2] + [("lay", k) for k in range(2, n_lay)]
    rounds = -(-len(moves) // n_sub)

    def turned(ex, lay):
        return (ex // (n_ex // 2) + lay) % 2 == 0

    def source_of(at, ex, lay, sub):
        if sub == 0 and at < 2 and turned(ex, lay):
            at = 1 - at
        axis, k = moves[min(at * n_sub + sub, len(moves) - 1)]
        return flat((ex + k) % n_ex, lay, sub) if axis == "ex" else flat(ex, (lay + k) % n_lay, sub)

    compact = (n_ex, n_lay, n_sub) == (4, 2, 2)

    def lacked(ex, lay, sub):
        return jnp.where(sub == 0, jnp.where(turned(ex, lay), 0, 1), 1 - (ex + ex // 2) % 2)

    def compact_plan(ex, lay, sub):
        across = lacked(ex, lay, 0)
        beside = lacked(ex, lay, 1)

        def grads_at(core, turn):
            return jnp.where(sub == core, 3 + 3 * turn, 9 + turn)

        slots = [0, grads_at(0, across), grads_at(1, 0), grads_at(1, 1)]
        layers = [0, grads_at(0, 1 - across)]
        same = jnp.where(ex // 2 == sub, 1, jnp.where(sub == 0, 4 + 3 * across, 11))
        other = jnp.where(sub == 0, 11, 4 + 3 * (1 - beside))
        near = jnp.where((sub == 1) & (ex // 2 == 0), 0, sub)
        units = [(same, (ex + 1 + lay) % 2, near, 0, None), (other, (ex + lay) % 2, 1, 0, None)]
        return slots, layers, units

    def general_plan(ex, lay, sub):
        size = 1 + n_sub
        slots, layers, sources = [0], [0], [(ex, sub)]
        for at, (axis, k) in enumerate(moves):
            core, turn = at % n_sub, at // n_sub
            if core == 0 and turn < 2:
                turn = jnp.where(turned(ex, lay), 1 - turn, turn)
            block = (1 + (core - sub + n_sub) % n_sub * rounds + turn) * size
            if axis == "ex":
                slots.append(block)
                sources.append(((ex + k) % n_ex, core))
            else:
                layers.append(block)
        units = []
        for block, (source, core) in zip(slots, sources):
            behind, row = (source % n_lay + 1 - lay + n_lay) % n_lay, source // n_lay
            for column in range(per_blk):
                units.append((block + 1, behind, core, column, row == sub * per_blk + column))
        return slots, layers, units

    def rotate(value, k):
        return lax.ppermute(value, "sub", [((i + k) % n_sub, i) for i in range(n_sub)])

    def body(layer_inputs, output_grads, basis_in, basis_out, queries):
        _, tokens, depth = layer_inputs.shape
        basis = basis_in.shape[1]
        own = tokens // LEN
        width = basis * basis
        rows, half = queries.shape[1:]

        chunk = lax.ppermute(queries[0], AXES, query_pairs)
        pick_x, pick_g = pl.pallas_call(
            functools.partial(picks_kernel, basis),
            out_shape=(
                jax.ShapeDtypeStruct((8 * basis, 4 * basis), BF16),
                jax.ShapeDtypeStruct((8 * basis, width), BF16),
            ),
            out_specs=(VMEM,) * 2,
            compiler_params=PARAMS,
            cost_estimate=pl.CostEstimate(flops=3 * 10**8, bytes_accessed=0, transcendentals=0),
            name="picks",
        )()
        basis_in, basis_out, pick_x = lax.optimization_barrier((basis_in, basis_out, pick_x))
        proj_x = lax.dot_general(basis_in[0], layer_inputs[0], LAST, preferred_element_type=F32)
        proj_g = lax.dot_general(basis_out[0], output_grads[0], LAST, preferred_element_type=F32)
        proj = jnp.concatenate([proj_x, proj_g])
        parts = [proj] + [rotate(proj, k) for k in range(1, n_sub)]
        chunk = pl.pallas_call(
            chunk_kernel,
            out_shape=jax.ShapeDtypeStruct((rows, half), BF16),
            in_specs=[VMEM],
            out_specs=VMEM,
            compiler_params=PARAMS,
            cost_estimate=pl.CostEstimate(flops=10**11, bytes_accessed=10**9, transcendentals=0),
            name="chunk",
        )(chunk)
        chunks = [chunk] + [rotate(chunk, k) for k in range(1, n_sub)]

        grads = pl.pallas_call(
            functools.partial(grads_kernel, n_sub),
            out_shape=jax.ShapeDtypeStruct((2 * own * n_sub, half), BF16),
            in_specs=[VMEM] * (n_sub + 2),
            out_specs=VMEM,
            compiler_params=PARAMS,
            name="grads",
        )(*parts, pick_x, pick_g)

        mine = jnp.stack([grads] + chunks)
        received = []
        for at in range(rounds):
            pairs = [(source_of(at, *device), flat(*device)) for device in devices]
            received.append(lax.ppermute(mine, AXES, pairs))
        if compact:
            swapped = pl.pallas_call(
                functools.partial(swap_kernel, lacked),
                out_shape=jax.ShapeDtypeStruct((4, rows, half), BF16),
                in_specs=[VMEM] * 2,
                out_specs=VMEM,
                compiler_params=PARAMS,
                name="swap",
            )(*received)
            blocks = [mine] + received + [rotate(swapped, 1)]
        else:
            both = jnp.concatenate(received)
            blocks = [mine, both] + [rotate(both, k) for k in range(1, n_sub)]

        return pl.pallas_call(
            functools.partial(final_kernel, compact_plan if compact else general_plan, n_ex, n_sub, own),
            out_shape=(
                jax.ShapeDtypeStruct((1, width // n_ex, half), F32),
                jax.ShapeDtypeStruct((own, rows * per_blk), F32),
            ),
            in_specs=[VMEM] * len(blocks),
            out_specs=(VMEM, VMEM),
            scratch_shapes=[pltpu.VMEM((sum(block.shape[0] for block in blocks), rows, half), BF16)],
            compiler_params=PARAMS,
            name="gram_and_scores",
        )(*blocks)

    in_specs = (
        P("lay", ("grp", "ex"), "sub"),
        P("lay", ("grp", "ex"), "sub"),
        P("lay", None, "sub"),
        P("lay", None, "sub"),
        P("lay", "ex", "sub"),
    )
    out_specs = (P(("grp", "lay"), "ex", "sub"), P(("grp", "ex"), ("lay", "sub")))
    return jax.shard_map(body, mesh=mesh, in_specs=in_specs, out_specs=out_specs, check_vma=False)
```

```python
import functools

import jax
import jax.numpy as jnp
from jax import lax
from jax.experimental import pallas as pl
from jax.experimental.pallas import tpu as pltpu
from jax.sharding import PartitionSpec as P

LEN = 64
AXES = ("ex", "lay", "sub")
F32, BF16 = jnp.float32, jnp.bfloat16
VMEM = pl.BlockSpec(memory_space=pltpu.VMEM)
LAST = (((1,), (1,)), ((), ()))
FIRST = (((0,), (0,)), ((), ()))
PARAMS = pltpu.CompilerParams(vmem_limit_bytes=16 * 1024 * 1024)


def picks_kernel(basis, pick_x_ref, pick_g_ref):
    rows, width = pick_g_ref.shape
    lanes, pair = pick_x_ref.shape[1], 2 * basis
    row = lax.broadcasted_iota(jnp.int32, (rows, lanes), 0) % pair
    col = lax.broadcasted_iota(jnp.int32, (rows, lanes), 1)
    pick_x_ref[...] = jnp.where(row == col % basis, 1.0, 0.0).astype(BF16)
    gap = row - basis - col // basis
    for j in range(width // lanes):
        pick_g_ref[:, j * lanes : (j + 1) * lanes] = jnp.where(gap == j * (lanes // basis), 1.0, 0.0).astype(BF16)


def take_kernel(in_ref, out_ref):
    out_ref[...] = in_ref[...]


def grads_kernel(n_sub, *refs):
    parts, (pick_x_ref, pick_g_ref, out_ref) = refs[:n_sub], refs[n_sub:]
    total = parts[0][...]
    for part in parts[1:]:
        total += part[...]
    high = total.astype(BF16).astype(F32)
    rest = total - high
    mid = rest.astype(BF16).astype(F32)
    low = rest - mid
    pieces = [jnp.concatenate([high, mid]).T, jnp.concatenate([low, jnp.zeros_like(low)]).T]
    pieces = jnp.concatenate(pieces, axis=1).astype(BF16)
    own = pieces.shape[0] // LEN
    lanes, width = pick_x_ref.shape[1], pick_g_ref.shape[1]
    tiled_x = jnp.dot(pieces, pick_x_ref[...], preferred_element_type=F32)
    tiles = []
    for j in range(width // lanes):
        pick_g = pick_g_ref[:, j * lanes : (j + 1) * lanes]
        product = jnp.dot(pieces, pick_g, preferred_element_type=F32) * tiled_x
        tiles.append(product.reshape(own, LEN, lanes).sum(axis=1))
    grads = jnp.concatenate(tiles, axis=1)
    high = grads.astype(BF16).astype(F32)
    low = grads - high
    half = width // n_sub
    rows = []
    for h in range(n_sub):
        cols = slice(h * half, (h + 1) * half)
        rows += [high[:, cols], low[:, cols]]
    out_ref[...] = jnp.concatenate(rows, axis=0).astype(BF16)


def swap_kernel(lacked, across_ref, first_ref, second_ref, out_ref):
    sub = lax.axis_index("sub")
    second = (sub != 0) & lacked(lax.axis_index("ex"))
    out_ref[0] = first_ref[0]

    @pl.when(sub == 0)
    def _():
        out_ref[1] = across_ref[0]

    @pl.when(sub != 0)
    def _():
        out_ref[1] = second_ref[0]

    @pl.when(second)
    def _():
        out_ref[2:] = second_ref[1:]

    @pl.when(jnp.logical_not(second))
    def _():
        out_ref[2:] = first_ref[1:]


def final_kernel(plan, n_ex, n_sub, own, *refs):
    parts, (gram_ref, scores_ref, all_ref) = refs[:-3], refs[-3:]
    start = 0
    for part in parts:
        all_ref[start : start + part.shape[0]] = part[...]
        start += part.shape[0]
    ex, lay, sub = lax.axis_index("ex"), lax.axis_index("lay"), lax.axis_index("sub")
    slots, layers, units = plan(ex, lay, sub)
    half = all_ref.shape[2]
    n_rows, per_half = half * n_sub // n_ex, n_ex // n_sub

    def halves_of(block):
        pieces = all_ref[block].astype(F32)
        return [pieces[h * 2 * own : (h + 1) * 2 * own] for h in range(n_sub)]

    def choose(values, index):
        result = values[0]
        for i in range(1, len(values)):
            result = jnp.where(index == i, values[i], result)
        return result

    lefts, rights = [], []
    for block in slots:
        halves = halves_of(block)
        cuts = [halves[e // per_half][:, e % per_half * n_rows : (e % per_half + 1) * n_rows] for e in range(n_ex)]
        left, right = choose(cuts, ex), choose(halves, sub)
        lefts += [left, pltpu.roll(left, own, 0)]
        rights += [right, right]
    left = jnp.concatenate(lefts, axis=0).astype(BF16)
    right = jnp.concatenate(rights, axis=0).astype(BF16)
    gram = lax.dot_general(left, right, FIRST, preferred_element_type=F32)
    gram_ref[0] = gram * (1.0 / (own * n_ex))

    layers = [halves_of(block) for block in layers]
    blocks = {}
    for block, behind, core, column, fits in units:
        grads = [choose([halves[h] for halves in layers], behind) for h in range(n_sub)]
        part = 0.0
        for h in range(n_sub):
            turned = choose(grads, lax.rem(core + h + n_sub - 1, n_sub)).astype(BF16)
            part += lax.dot_general(turned, all_ref[block + h], LAST, preferred_element_type=F32)
        part = part[:own] + part[own:]
        part = part if fits is None else jnp.where(fits, part, 0.0)
        blocks[column] = blocks.get(column, 0.0) + part
    blocks = [blocks[column] for column in sorted(blocks)]
    scores_ref[...] = blocks[0] if len(blocks) == 1 else jnp.concatenate(blocks, axis=1)


def solution(mesh):
    n_ex, n_lay, n_sub = mesh.shape["ex"], mesh.shape["lay"], mesh.shape["sub"]
    group, per_blk = n_ex // n_lay, n_ex // (n_lay * n_sub)

    def flat(ex, lay, sub):
        return (ex * n_lay + lay) * n_sub + sub

    devices = [(ex, lay, sub) for ex in range(n_ex) for lay in range(n_lay) for sub in range(n_sub)]

    query_pairs = [
        (
            flat(ex, lay, sub),
            flat(ex % group * n_lay + (lay + n_lay - 1) % n_lay, ex // group, (sub + 1) % n_sub),
        )
        for ex, lay, sub in devices
    ]

    rest = [k for k in range(2, n_ex - 1) if k != n_ex // 2]
    moves = [(n_ex // 2, n_ex - 1), ((rest + [None])[0], 1)]
    rest = rest[1:]
    while rest:
        moves.append((rest[0], (rest + [None])[1]))
        rest = rest[2:]

    def ex_pairs(move):
        return [
            (flat((ex + move[sub]) % n_ex, lay, sub), flat(ex, lay, sub))
            for ex, lay, sub in devices
            if move[sub] is not None
        ]

    def lay_pairs(k):
        core = (k - 1) % n_sub
        return [(flat(ex, (lay + k) % n_lay, core), flat(ex, lay, core)) for ex, lay, sub in devices if sub == core]

    compact = (n_ex, n_lay, n_sub) == (4, 2, 2)

    def lacked(ex):
        return (ex + ex // 2) % 2 == 0

    def compact_plan(ex, lay, sub):
        slots = [0, jnp.where(sub == 0, 3, 10), jnp.where(sub == 1, 3, 10), jnp.where(sub == 1, 6, 11)]
        layers = [0, jnp.where(sub == 0, 9, 11)]
        same = jnp.where(ex // 2 == sub, 1, jnp.where(sub == 0, 4, 12))
        other = jnp.where(sub == 0, 12, jnp.where(lacked(ex), 4, 7))
        core = jnp.where((sub == 1) & (ex // 2 == 0), 0, sub)
        units = [(same, (ex + 1 + lay) % 2, core, 0, None), (other, (ex + lay) % 2, 1, 0, None)]
        return slots, layers, units

    def general_plan(ex, lay, sub):
        size = 1 + n_sub
        per_core = len(moves) * size + n_lay - 1
        slots, layers, sources = [0], [0], [(ex, sub)]
        for core in range(n_sub):
            start = size + (core - sub + n_sub) % n_sub * per_core
            for at, move in enumerate(moves):
                if move[core] is not None:
                    slots.append(start + at * size)
                    sources.append(((ex + move[core]) % n_ex, core))
        for k in range(1, n_lay):
            start = size + ((k - 1) % n_sub - sub + n_sub) % n_sub * per_core
            layers.append(start + len(moves) * size + k - 1)
        units = []
        for block, (source, core) in zip(slots, sources):
            behind, row = (source % n_lay + 1 - lay + n_lay) % n_lay, source // n_lay
            for column in range(per_blk):
                units.append((block + 1, behind, core, column, row == sub * per_blk + column))
        return slots, layers, units

    def take(value, name):
        return pl.pallas_call(
            take_kernel,
            out_shape=jax.ShapeDtypeStruct(value.shape, value.dtype),
            in_specs=[VMEM],
            out_specs=VMEM,
            compiler_params=PARAMS,
            cost_estimate=pl.CostEstimate(flops=10**11, bytes_accessed=10**9, transcendentals=0),
            name=name,
        )(value)

    def rotate(value, k):
        return lax.ppermute(value, "sub", [((i + k) % n_sub, i) for i in range(n_sub)])

    def body(layer_inputs, output_grads, basis_in, basis_out, queries):
        _, tokens, depth = layer_inputs.shape
        basis = basis_in.shape[1]
        own = tokens // LEN
        width = basis * basis
        rows, half = queries.shape[1:]

        chunk = lax.ppermute(queries[0], AXES, query_pairs)
        pick_x, pick_g = pl.pallas_call(
            functools.partial(picks_kernel, basis),
            out_shape=(
                jax.ShapeDtypeStruct((8 * basis, 4 * basis), BF16),
                jax.ShapeDtypeStruct((8 * basis, width), BF16),
            ),
            out_specs=(VMEM,) * 2,
            compiler_params=PARAMS,
            cost_estimate=pl.CostEstimate(flops=3 * 10**8, bytes_accessed=0, transcendentals=0),
            name="picks",
        )()
        basis_in, basis_out, pick_x = lax.optimization_barrier((basis_in, basis_out, pick_x))
        proj_x = lax.dot_general(basis_in[0], layer_inputs[0], LAST, preferred_element_type=F32)
        proj_g = lax.dot_general(basis_out[0], output_grads[0], LAST, preferred_element_type=F32)
        proj = jnp.concatenate([proj_x, proj_g])
        parts = [proj] + [rotate(proj, k) for k in range(1, n_sub)]
        chunk = take(chunk, "take_chunk")
        chunks = [chunk] + [rotate(chunk, k) for k in range(1, n_sub)]

        grads = pl.pallas_call(
            functools.partial(grads_kernel, n_sub),
            out_shape=jax.ShapeDtypeStruct((2 * own * n_sub, half), BF16),
            in_specs=[VMEM] * (n_sub + 2),
            out_specs=VMEM,
            compiler_params=PARAMS,
            name="grads",
        )(*parts, pick_x, pick_g)

        grads = grads[None]
        across = [take(lax.ppermute(grads, AXES, lay_pairs(k)), "take_across") for k in range(1, n_lay)]
        mine = jnp.concatenate([grads] + [chunk[None] for chunk in chunks])
        received = [lax.ppermute(mine, AXES, ex_pairs(move)) for move in moves]
        if compact:
            swapped = pl.pallas_call(
                functools.partial(swap_kernel, lacked),
                out_shape=jax.ShapeDtypeStruct((4, rows, half), BF16),
                in_specs=[VMEM] * 3,
                out_specs=VMEM,
                compiler_params=PARAMS,
                name="swap",
            )(*across, *received)
            blocks = [mine] + received + across + [rotate(swapped, 1)]
        else:
            both = jnp.concatenate(received + across)
            blocks = [mine, both] + [rotate(both, k) for k in range(1, n_sub)]

        return pl.pallas_call(
            functools.partial(final_kernel, compact_plan if compact else general_plan, n_ex, n_sub, own),
            out_shape=(
                jax.ShapeDtypeStruct((1, width // n_ex, half), F32),
                jax.ShapeDtypeStruct((own, rows * per_blk), F32),
            ),
            in_specs=[VMEM] * len(blocks),
            out_specs=(VMEM, VMEM),
            scratch_shapes=[pltpu.VMEM((sum(block.shape[0] for block in blocks), rows, half), BF16)],
            compiler_params=PARAMS,
            name="gram_and_scores",
        )(*blocks)

    in_specs = (
        P("lay", ("grp", "ex"), "sub"),
        P("lay", ("grp", "ex"), "sub"),
        P("lay", None, "sub"),
        P("lay", None, "sub"),
        P("lay", "ex", "sub"),
    )
    out_specs = (P(("grp", "lay"), "ex", "sub"), P(("grp", "ex"), ("lay", "sub")))
    return jax.shard_map(body, mesh=mesh, in_specs=in_specs, out_specs=out_specs, check_vma=False)
```

```python
import functools

import jax
import jax.numpy as jnp
from jax import lax
from jax.experimental import pallas as pl
from jax.experimental.pallas import tpu as pltpu
from jax.sharding import PartitionSpec as P

LEN = 64
AXES = ("ex", "lay", "sub")
F32, BF16 = jnp.float32, jnp.bfloat16
VMEM = pl.BlockSpec(memory_space=pltpu.VMEM)
LAST = (((1,), (1,)), ((), ()))
FIRST = (((0,), (0,)), ((), ()))
PARAMS = pltpu.CompilerParams(vmem_limit_bytes=16 * 1024 * 1024)


def picks_kernel(basis, pick_x_ref, pick_g_ref):
    rows, width = pick_g_ref.shape
    lanes, pair = pick_x_ref.shape[1], 2 * basis
    row = lax.broadcasted_iota(jnp.int32, (rows, lanes), 0) % pair
    col = lax.broadcasted_iota(jnp.int32, (rows, lanes), 1)
    pick_x_ref[...] = jnp.where(row == col % basis, 1.0, 0.0).astype(BF16)
    gap = row - basis - col // basis
    for j in range(width // lanes):
        pick_g_ref[:, j * lanes : (j + 1) * lanes] = jnp.where(gap == j * (lanes // basis), 1.0, 0.0).astype(BF16)


def chunk_kernel(in_ref, out_ref):
    out_ref[...] = in_ref[...]


def grads_kernel(n_sub, *refs):
    parts, (pick_x_ref, pick_g_ref, out_ref) = refs[:n_sub], refs[n_sub:]
    total = parts[0][...]
    for part in parts[1:]:
        total += part[...]
    high = total.astype(BF16).astype(F32)
    rest = total - high
    mid = rest.astype(BF16).astype(F32)
    low = rest - mid
    pieces = [jnp.concatenate([high, mid]).T, jnp.concatenate([low, jnp.zeros_like(low)]).T]
    pieces = jnp.concatenate(pieces, axis=1).astype(BF16)
    own = pieces.shape[0] // LEN
    lanes, width = pick_x_ref.shape[1], pick_g_ref.shape[1]
    tiled_x = jnp.dot(pieces, pick_x_ref[...], preferred_element_type=F32)
    tiles = []
    for j in range(width // lanes):
        pick_g = pick_g_ref[:, j * lanes : (j + 1) * lanes]
        product = jnp.dot(pieces, pick_g, preferred_element_type=F32) * tiled_x
        tiles.append(product.reshape(own, LEN, lanes).sum(axis=1))
    grads = jnp.concatenate(tiles, axis=1)
    high = grads.astype(BF16).astype(F32)
    low = grads - high
    half = width // n_sub
    rows = []
    for h in range(n_sub):
        cols = slice(h * half, (h + 1) * half)
        rows += [high[:, cols], low[:, cols]]
    out_ref[...] = jnp.concatenate(rows, axis=0).astype(BF16)


def swap_kernel(lacked, first_ref, second_ref, out_ref):
    second = lacked(lax.axis_index("ex"), lax.axis_index("lay"), lax.axis_index("sub")) == 1
    out_ref[0] = first_ref[0]
    out_ref[1] = second_ref[0]

    @pl.when(second)
    def _():
        out_ref[2:] = second_ref[1:]

    @pl.when(jnp.logical_not(second))
    def _():
        out_ref[2:] = first_ref[1:]


def final_kernel(plan, n_ex, n_sub, own, *refs):
    parts, (gram_ref, scores_ref, all_ref) = refs[:-3], refs[-3:]
    start = 0
    for part in parts:
        all_ref[start : start + part.shape[0]] = part[...]
        start += part.shape[0]
    ex, lay, sub = lax.axis_index("ex"), lax.axis_index("lay"), lax.axis_index("sub")
    slots, layers, units = plan(ex, lay, sub)
    half = all_ref.shape[2]
    n_rows, per_half = half * n_sub // n_ex, n_ex // n_sub

    def halves_of(block):
        pieces = all_ref[block].astype(F32)
        return [pieces[h * 2 * own : (h + 1) * 2 * own] for h in range(n_sub)]

    def choose(values, index):
        result = values[0]
        for i in range(1, len(values)):
            result = jnp.where(index == i, values[i], result)
        return result

    lefts, rights = [], []
    for block in slots:
        halves = halves_of(block)
        cuts = [halves[e // per_half][:, e % per_half * n_rows : (e % per_half + 1) * n_rows] for e in range(n_ex)]
        left, right = choose(cuts, ex), choose(halves, sub)
        lefts += [left, pltpu.roll(left, own, 0)]
        rights += [right, right]
    left = jnp.concatenate(lefts, axis=0).astype(BF16)
    right = jnp.concatenate(rights, axis=0).astype(BF16)
    gram = lax.dot_general(left, right, FIRST, preferred_element_type=F32)
    gram_ref[0] = gram * (1.0 / (own * n_ex))

    layers = [halves_of(block) for block in layers]
    blocks = {}
    for block, behind, core, column, fits in units:
        grads = [choose([halves[h] for halves in layers], behind) for h in range(n_sub)]
        part = 0.0
        for h in range(n_sub):
            turned = choose(grads, lax.rem(core + h + n_sub - 1, n_sub)).astype(BF16)
            part += lax.dot_general(turned, all_ref[block + h], LAST, preferred_element_type=F32)
        part = part[:own] + part[own:]
        part = part if fits is None else jnp.where(fits, part, 0.0)
        blocks[column] = blocks.get(column, 0.0) + part
    blocks = [blocks[column] for column in sorted(blocks)]
    scores_ref[...] = blocks[0] if len(blocks) == 1 else jnp.concatenate(blocks, axis=1)


def solution(mesh):
    n_ex, n_lay, n_sub = mesh.shape["ex"], mesh.shape["lay"], mesh.shape["sub"]
    group, per_blk = n_ex // n_lay, n_ex // (n_lay * n_sub)

    def flat(ex, lay, sub):
        return (ex * n_lay + lay) * n_sub + sub

    devices = [(ex, lay, sub) for ex in range(n_ex) for lay in range(n_lay) for sub in range(n_sub)]

    query_pairs = [
        (
            flat(ex, lay, sub),
            flat(ex % group * n_lay + (lay + n_lay - 1) % n_lay, ex // group, (sub + 1) % n_sub),
        )
        for ex, lay, sub in devices
    ]

    moves = [("lay", 1), ("ex", n_ex - 1), ("ex", n_ex // 2), ("ex", 1)]
    moves += [("ex", k) for k in range(2, n_ex - 1) if k != n_ex // 2] + [("lay", k) for k in range(2, n_lay)]
    rounds = -(-len(moves) // n_sub)

    def turned(ex, lay):
        return (ex // (n_ex // 2) + lay) % 2 == 0

    def source_of(at, ex, lay, sub):
        if sub == 0 and at < 2 and turned(ex, lay):
            at = 1 - at
        axis, k = moves[min(at * n_sub + sub, len(moves) - 1)]
        sender = (sub + 1) % n_sub
        return flat((ex + k) % n_ex, lay, sender) if axis == "ex" else flat(ex, (lay + k) % n_lay, sender)

    compact = (n_ex, n_lay, n_sub) == (4, 2, 2)

    def lacked(ex, lay, sub):
        return jnp.where(sub == 0, jnp.where(turned(ex, lay), 0, 1), 1 - (ex + ex // 2) % 2)

    def compact_plan(ex, lay, sub):
        across = lacked(ex, lay, 0)
        beside = lacked(ex, lay, 1)

        def grads_at(core, turn):
            return jnp.where(sub == core, 3 + 3 * turn, 9 + turn)

        slots = [0, grads_at(0, across), grads_at(1, 0), grads_at(1, 1)]
        layers = [0, grads_at(0, 1 - across)]
        same = jnp.where(ex // 2 == sub, 1, jnp.where(sub == 0, 4 + 3 * across, 11))
        other = jnp.where(sub == 0, 11, 4 + 3 * (1 - beside))
        near = jnp.where(ex // 2 == sub, sub, 1)
        units = [(same, (ex + 1 + lay) % 2, near, 0, None), (other, (ex + lay) % 2, 0, 0, None)]
        return slots, layers, units

    def general_plan(ex, lay, sub):
        size = 1 + n_sub
        slots, layers, sources = [0], [0], [(ex, sub)]
        for at, (axis, k) in enumerate(moves):
            core, turn = at % n_sub, at // n_sub
            if core == 0 and turn < 2:
                turn = jnp.where(turned(ex, lay), 1 - turn, turn)
            block = (1 + (core - sub + n_sub) % n_sub * rounds + turn) * size
            if axis == "ex":
                slots.append(block)
                sources.append(((ex + k) % n_ex, (core + 1) % n_sub))
            else:
                layers.append(block)
        units = []
        for block, (source, core) in zip(slots, sources):
            behind, row = (source % n_lay + 1 - lay + n_lay) % n_lay, source // n_lay
            for column in range(per_blk):
                units.append((block + 1, behind, core, column, row == sub * per_blk + column))
        return slots, layers, units

    def rotate(value, k):
        return lax.ppermute(value, "sub", [((i + k) % n_sub, i) for i in range(n_sub)])

    def body(layer_inputs, output_grads, basis_in, basis_out, queries):
        _, tokens, depth = layer_inputs.shape
        basis = basis_in.shape[1]
        own = tokens // LEN
        width = basis * basis
        rows, half = queries.shape[1:]

        chunk = lax.ppermute(queries[0], AXES, query_pairs)
        pick_x, pick_g = pl.pallas_call(
            functools.partial(picks_kernel, basis),
            out_shape=(
                jax.ShapeDtypeStruct((8 * basis, 4 * basis), BF16),
                jax.ShapeDtypeStruct((8 * basis, width), BF16),
            ),
            out_specs=(VMEM,) * 2,
            compiler_params=PARAMS,
            cost_estimate=pl.CostEstimate(flops=3 * 10**8, bytes_accessed=0, transcendentals=0),
            name="picks",
        )()
        basis_in, basis_out, pick_x = lax.optimization_barrier((basis_in, basis_out, pick_x))
        proj_x = lax.dot_general(basis_in[0], layer_inputs[0], LAST, preferred_element_type=F32)
        proj_g = lax.dot_general(basis_out[0], output_grads[0], LAST, preferred_element_type=F32)
        proj = jnp.concatenate([proj_x, proj_g])
        parts = [proj] + [rotate(proj, k) for k in range(1, n_sub)]
        chunk = pl.pallas_call(
            chunk_kernel,
            out_shape=jax.ShapeDtypeStruct((rows, half), BF16),
            in_specs=[VMEM],
            out_specs=VMEM,
            compiler_params=PARAMS,
            cost_estimate=pl.CostEstimate(flops=10**11, bytes_accessed=10**9, transcendentals=0),
            name="chunk",
        )(chunk)
        chunks = [chunk] + [rotate(chunk, k) for k in range(1, n_sub)]

        grads = pl.pallas_call(
            functools.partial(grads_kernel, n_sub),
            out_shape=jax.ShapeDtypeStruct((2 * own * n_sub, half), BF16),
            in_specs=[VMEM] * (n_sub + 2),
            out_specs=VMEM,
            compiler_params=PARAMS,
            name="grads",
        )(*parts, pick_x, pick_g)

        mine = jnp.stack([grads] + chunks)
        received = []
        for at in range(rounds):
            pairs = [(source_of(at, *device), flat(*device)) for device in devices]
            received.append(lax.ppermute(mine, AXES, pairs))
        if compact:
            swapped = pl.pallas_call(
                functools.partial(swap_kernel, lacked),
                out_shape=jax.ShapeDtypeStruct((4, rows, half), BF16),
                in_specs=[VMEM] * 2,
                out_specs=VMEM,
                compiler_params=PARAMS,
                name="swap",
            )(*received)
            blocks = [mine] + received + [rotate(swapped, 1)]
        else:
            both = jnp.concatenate(received)
            blocks = [mine, both] + [rotate(both, k) for k in range(1, n_sub)]

        return pl.pallas_call(
            functools.partial(final_kernel, compact_plan if compact else general_plan, n_ex, n_sub, own),
            out_shape=(
                jax.ShapeDtypeStruct((1, width // n_ex, half), F32),
                jax.ShapeDtypeStruct((own, rows * per_blk), F32),
            ),
            in_specs=[VMEM] * len(blocks),
            out_specs=(VMEM, VMEM),
            scratch_shapes=[pltpu.VMEM((sum(block.shape[0] for block in blocks), rows, half), BF16)],
            compiler_params=PARAMS,
            name="gram_and_scores",
        )(*blocks)

    in_specs = (
        P("lay", ("grp", "ex"), "sub"),
        P("lay", ("grp", "ex"), "sub"),
        P("lay", None, "sub"),
        P("lay", None, "sub"),
        P("lay", "ex", "sub"),
    )
    out_specs = (P(("grp", "lay"), "ex", "sub"), P(("grp", "ex"), ("lay", "sub")))
    return jax.shard_map(body, mesh=mesh, in_specs=in_specs, out_specs=out_specs, check_vma=False)
```

```python
import functools

import jax
import jax.numpy as jnp
from jax import lax
from jax.experimental import pallas as pl
from jax.experimental.pallas import tpu as pltpu
from jax.sharding import PartitionSpec as P

LEN = 64
AXES = ("ex", "lay", "sub")
F32, BF16 = jnp.float32, jnp.bfloat16
VMEM = pl.BlockSpec(memory_space=pltpu.VMEM)
LAST = (((1,), (1,)), ((), ()))
FIRST = (((0,), (0,)), ((), ()))
PARAMS = pltpu.CompilerParams(vmem_limit_bytes=16 * 1024 * 1024)


def picks_kernel(basis, pick_x_ref, pick_g_ref):
    rows, width = pick_g_ref.shape
    lanes, pair = pick_x_ref.shape[1], 2 * basis
    row = lax.broadcasted_iota(jnp.int32, (rows, lanes), 0) % pair
    col = lax.broadcasted_iota(jnp.int32, (rows, lanes), 1)
    pick_x_ref[...] = jnp.where(row == col % basis, 1.0, 0.0).astype(BF16)
    gap = row - basis - col // basis
    for j in range(width // lanes):
        pick_g_ref[:, j * lanes : (j + 1) * lanes] = jnp.where(gap == j * (lanes // basis), 1.0, 0.0).astype(BF16)


def chunk_kernel(in_ref, out_ref):
    out_ref[...] = in_ref[...]


def grads_kernel(n_sub, *refs):
    parts, (pick_x_ref, pick_g_ref, out_ref) = refs[:n_sub], refs[n_sub:]
    total = parts[0][...]
    for part in parts[1:]:
        total += part[...]
    high = total.astype(BF16).astype(F32)
    rest = total - high
    mid = rest.astype(BF16).astype(F32)
    low = rest - mid
    pieces = [jnp.concatenate([high, mid]).T, jnp.concatenate([low, jnp.zeros_like(low)]).T]
    pieces = jnp.concatenate(pieces, axis=1).astype(BF16)
    own = pieces.shape[0] // LEN
    lanes, width = pick_x_ref.shape[1], pick_g_ref.shape[1]
    tiled_x = jnp.dot(pieces, pick_x_ref[...], preferred_element_type=F32)
    tiles = []
    for j in range(width // lanes):
        pick_g = pick_g_ref[:, j * lanes : (j + 1) * lanes]
        product = jnp.dot(pieces, pick_g, preferred_element_type=F32) * tiled_x
        tiles.append(product.reshape(own, LEN, lanes).sum(axis=1))
    grads = jnp.concatenate(tiles, axis=1)
    high = grads.astype(BF16).astype(F32)
    low = grads - high
    half = width // n_sub
    rows = []
    for h in range(n_sub):
        cols = slice(h * half, (h + 1) * half)
        rows += [high[:, cols], low[:, cols]]
    out_ref[...] = jnp.concatenate(rows, axis=0).astype(BF16)


def swap_kernel(lacked, first_ref, second_ref, out_ref):
    second = lacked(lax.axis_index("ex"), lax.axis_index("lay"), lax.axis_index("sub")) == 1
    out_ref[0] = first_ref[0]
    out_ref[1] = second_ref[0]

    @pl.when(second)
    def _():
        out_ref[2:] = second_ref[1:]

    @pl.when(jnp.logical_not(second))
    def _():
        out_ref[2:] = first_ref[1:]


def final_kernel(plan, n_ex, n_sub, own, *refs):
    parts, (gram_ref, scores_ref, all_ref) = refs[:-3], refs[-3:]
    start = 0
    for part in parts:
        all_ref[start : start + part.shape[0]] = part[...]
        start += part.shape[0]
    ex, lay, sub = lax.axis_index("ex"), lax.axis_index("lay"), lax.axis_index("sub")
    slots, layers, units = plan(ex, lay, sub)
    half = all_ref.shape[2]
    n_rows, per_half = half * n_sub // n_ex, n_ex // n_sub

    def halves_of(block):
        pieces = all_ref[block].astype(F32)
        return [pieces[h * 2 * own : (h + 1) * 2 * own] for h in range(n_sub)]

    def choose(values, index):
        result = values[0]
        for i in range(1, len(values)):
            result = jnp.where(index == i, values[i], result)
        return result

    lefts, rights = [], []
    for block in slots:
        halves = halves_of(block)
        cuts = [halves[e // per_half][:, e % per_half * n_rows : (e % per_half + 1) * n_rows] for e in range(n_ex)]
        left, right = choose(cuts, ex), choose(halves, sub)
        lefts += [left, pltpu.roll(left, own, 0)]
        rights += [right, right]
    left = jnp.concatenate(lefts, axis=0).astype(BF16)
    right = jnp.concatenate(rights, axis=0).astype(BF16)
    gram = lax.dot_general(left, right, FIRST, preferred_element_type=F32)
    gram_ref[0] = gram * (1.0 / (own * n_ex))

    layers = [halves_of(block) for block in layers]
    blocks = {}
    for block, behind, core, column, fits in units:
        grads = [choose([halves[h] for halves in layers], behind) for h in range(n_sub)]
        part = 0.0
        for h in range(n_sub):
            turned = choose(grads, lax.rem(core + h + n_sub - 1, n_sub)).astype(BF16)
            part += lax.dot_general(turned, all_ref[block + h], LAST, preferred_element_type=F32)
        part = part[:own] + part[own:]
        part = part if fits is None else jnp.where(fits, part, 0.0)
        blocks[column] = blocks.get(column, 0.0) + part
    blocks = [blocks[column] for column in sorted(blocks)]
    scores_ref[...] = blocks[0] if len(blocks) == 1 else jnp.concatenate(blocks, axis=1)


def solution(mesh):
    n_ex, n_lay, n_sub = mesh.shape["ex"], mesh.shape["lay"], mesh.shape["sub"]
    group, per_blk = n_ex // n_lay, n_ex // (n_lay * n_sub)

    def flat(ex, lay, sub):
        return (ex * n_lay + lay) * n_sub + sub

    devices = [(ex, lay, sub) for ex in range(n_ex) for lay in range(n_lay) for sub in range(n_sub)]

    query_pairs = [
        (
            flat(ex, lay, sub),
            flat(ex % group * n_lay + (lay + n_lay - 1) % n_lay, ex // group, (sub + 1) % n_sub),
        )
        for ex, lay, sub in devices
    ]

    moves = [("lay", 1), ("ex", n_ex - 1), ("ex", n_ex // 2), ("ex", 1)]
    moves += [("ex", k) for k in range(2, n_ex - 1) if k != n_ex // 2] + [("lay", k) for k in range(2, n_lay)]
    rounds = -(-len(moves) // n_sub)

    def sender_of(at, sub):
        return (sub + (at == 1)) % n_sub

    def turned(ex, lay):
        return (ex // (n_ex // 2) + lay) % 2 == 0

    def source_of(at, ex, lay, sub):
        sender = sender_of(at, sub)
        if sub == 0 and at < 2 and turned(ex, lay):
            at = 1 - at
        axis, k = moves[min(at * n_sub + sub, len(moves) - 1)]
        return flat((ex + k) % n_ex, lay, sender) if axis == "ex" else flat(ex, (lay + k) % n_lay, sender)

    compact = (n_ex, n_lay, n_sub) == (4, 2, 2)

    def lacked(ex, lay, sub):
        return jnp.where(sub == 0, jnp.where(turned(ex, lay), 0, 1), 1 - (ex + ex // 2) % 2)

    def compact_plan(ex, lay, sub):
        across = lacked(ex, lay, 0)
        beside = lacked(ex, lay, 1)

        def grads_at(core, turn):
            return jnp.where(sub == core, 3 + 3 * turn, 9 + turn)

        slots = [0, grads_at(0, across), grads_at(1, 0), grads_at(1, 1)]
        layers = [0, grads_at(0, 1 - across)]
        same = jnp.where(ex // 2 == sub, 1, jnp.where(sub == 0, 4 + 3 * across, 11))
        other = jnp.where(sub == 0, 11, 4 + 3 * (1 - beside))
        near = jnp.where(ex // 2 == sub, sub, across)
        far = jnp.where(sub == 0, 1 - beside, beside)
        units = [(same, (ex + 1 + lay) % 2, near, 0, None), (other, (ex + lay) % 2, far, 0, None)]
        return slots, layers, units

    def general_plan(ex, lay, sub):
        size = 1 + n_sub
        slots, layers, sources = [0], [0], [(ex, sub)]
        for at, (axis, k) in enumerate(moves):
            core, turn = at % n_sub, at // n_sub
            if core == 0 and turn < 2:
                turn = jnp.where(turned(ex, lay), 1 - turn, turn)
            block = (1 + (core - sub + n_sub) % n_sub * rounds + turn) * size
            if axis == "ex":
                slots.append(block)
                sources.append(((ex + k) % n_ex, sender_of(turn, core)))
            else:
                layers.append(block)
        units = []
        for block, (source, core) in zip(slots, sources):
            behind, row = (source % n_lay + 1 - lay + n_lay) % n_lay, source // n_lay
            for column in range(per_blk):
                units.append((block + 1, behind, core, column, row == sub * per_blk + column))
        return slots, layers, units

    def rotate(value, k):
        return lax.ppermute(value, "sub", [((i + k) % n_sub, i) for i in range(n_sub)])

    def body(layer_inputs, output_grads, basis_in, basis_out, queries):
        _, tokens, depth = layer_inputs.shape
        basis = basis_in.shape[1]
        own = tokens // LEN
        width = basis * basis
        rows, half = queries.shape[1:]

        chunk = lax.ppermute(queries[0], AXES, query_pairs)
        pick_x, pick_g = pl.pallas_call(
            functools.partial(picks_kernel, basis),
            out_shape=(
                jax.ShapeDtypeStruct((8 * basis, 4 * basis), BF16),
                jax.ShapeDtypeStruct((8 * basis, width), BF16),
            ),
            out_specs=(VMEM,) * 2,
            compiler_params=PARAMS,
            cost_estimate=pl.CostEstimate(flops=3 * 10**8, bytes_accessed=0, transcendentals=0),
            name="picks",
        )()
        basis_in, basis_out, pick_x = lax.optimization_barrier((basis_in, basis_out, pick_x))
        proj_x = lax.dot_general(basis_in[0], layer_inputs[0], LAST, preferred_element_type=F32)
        proj_g = lax.dot_general(basis_out[0], output_grads[0], LAST, preferred_element_type=F32)
        proj = jnp.concatenate([proj_x, proj_g])
        parts = [proj] + [rotate(proj, k) for k in range(1, n_sub)]
        chunk = pl.pallas_call(
            chunk_kernel,
            out_shape=jax.ShapeDtypeStruct((rows, half), BF16),
            in_specs=[VMEM],
            out_specs=VMEM,
            compiler_params=PARAMS,
            cost_estimate=pl.CostEstimate(flops=10**11, bytes_accessed=10**9, transcendentals=0),
            name="chunk",
        )(chunk)
        chunks = [chunk] + [rotate(chunk, k) for k in range(1, n_sub)]

        grads = pl.pallas_call(
            functools.partial(grads_kernel, n_sub),
            out_shape=jax.ShapeDtypeStruct((2 * own * n_sub, half), BF16),
            in_specs=[VMEM] * (n_sub + 2),
            out_specs=VMEM,
            compiler_params=PARAMS,
            name="grads",
        )(*parts, pick_x, pick_g)

        mine = jnp.stack([grads] + chunks)
        received = []
        for at in range(rounds):
            pairs = [(source_of(at, *device), flat(*device)) for device in devices]
            received.append(lax.ppermute(mine, AXES, pairs))
        if compact:
            swapped = pl.pallas_call(
                functools.partial(swap_kernel, lacked),
                out_shape=jax.ShapeDtypeStruct((4, rows, half), BF16),
                in_specs=[VMEM] * 2,
                out_specs=VMEM,
                compiler_params=PARAMS,
                name="swap",
            )(*received)
            blocks = [mine] + received + [rotate(swapped, 1)]
        else:
            both = jnp.concatenate(received)
            blocks = [mine, both] + [rotate(both, k) for k in range(1, n_sub)]

        return pl.pallas_call(
            functools.partial(final_kernel, compact_plan if compact else general_plan, n_ex, n_sub, own),
            out_shape=(
                jax.ShapeDtypeStruct((1, width // n_ex, half), F32),
                jax.ShapeDtypeStruct((own, rows * per_blk), F32),
            ),
            in_specs=[VMEM] * len(blocks),
            out_specs=(VMEM, VMEM),
            scratch_shapes=[pltpu.VMEM((sum(block.shape[0] for block in blocks), rows, half), BF16)],
            compiler_params=PARAMS,
            name="gram_and_scores",
        )(*blocks)

    in_specs = (
        P("lay", ("grp", "ex"), "sub"),
        P("lay", ("grp", "ex"), "sub"),
        P("lay", None, "sub"),
        P("lay", None, "sub"),
        P("lay", "ex", "sub"),
    )
    out_specs = (P(("grp", "lay"), "ex", "sub"), P(("grp", "ex"), ("lay", "sub")))
    return jax.shard_map(body, mesh=mesh, in_specs=in_specs, out_specs=out_specs, check_vma=False)
```

```python
import functools

import jax
import jax.numpy as jnp
from jax import lax
from jax.experimental import pallas as pl
from jax.experimental.pallas import tpu as pltpu
from jax.sharding import PartitionSpec as P

LEN = 64
AXES = ("ex", "lay", "sub")
F32, BF16 = jnp.float32, jnp.bfloat16
VMEM = pl.BlockSpec(memory_space=pltpu.VMEM)
ANY = pl.BlockSpec(memory_space=pl.ANY)
LAST = (((1,), (1,)), ((), ()))
FIRST = (((0,), (0,)), ((), ()))
PARAMS = pltpu.CompilerParams(vmem_limit_bytes=16 * 1024 * 1024)


def picks_kernel(basis, pick_x_ref, pick_g_ref):
    rows, width = pick_g_ref.shape
    lanes, pair = pick_x_ref.shape[1], 2 * basis
    row = lax.broadcasted_iota(jnp.int32, (rows, lanes), 0) % pair
    col = lax.broadcasted_iota(jnp.int32, (rows, lanes), 1)
    pick_x_ref[...] = jnp.where(row == col % basis, 1.0, 0.0).astype(BF16)
    gap = row - basis - col // basis
    for j in range(width // lanes):
        pick_g_ref[:, j * lanes : (j + 1) * lanes] = jnp.where(gap == j * (lanes // basis), 1.0, 0.0).astype(BF16)


def chunk_kernel(in_ref, out_ref):
    out_ref[...] = in_ref[...]


def grads_kernel(n_sub, *refs):
    parts, (pick_x_ref, pick_g_ref, out_ref) = refs[:n_sub], refs[n_sub:]
    total = parts[0][...]
    for part in parts[1:]:
        total += part[...]
    high = total.astype(BF16).astype(F32)
    rest = total - high
    mid = rest.astype(BF16).astype(F32)
    low = rest - mid
    pieces = [jnp.concatenate([high, mid]).T, jnp.concatenate([low, jnp.zeros_like(low)]).T]
    pieces = jnp.concatenate(pieces, axis=1).astype(BF16)
    own = pieces.shape[0] // LEN
    lanes, width = pick_x_ref.shape[1], pick_g_ref.shape[1]
    tiled_x = jnp.dot(pieces, pick_x_ref[...], preferred_element_type=F32)
    tiles = []
    for j in range(width // lanes):
        pick_g = pick_g_ref[:, j * lanes : (j + 1) * lanes]
        product = jnp.dot(pieces, pick_g, preferred_element_type=F32) * tiled_x
        tiles.append(product.reshape(own, LEN, lanes).sum(axis=1))
    grads = jnp.concatenate(tiles, axis=1)
    high = grads.astype(BF16).astype(F32)
    low = grads - high
    half = width // n_sub
    rows = []
    for h in range(n_sub):
        cols = slice(h * half, (h + 1) * half)
        rows += [high[:, cols], low[:, cols]]
    out_ref[...] = jnp.concatenate(rows, axis=0).astype(BF16)


def swap_kernel(lacked, first_ref, second_ref, out_ref):
    second = lacked(lax.axis_index("ex"), lax.axis_index("lay"), lax.axis_index("sub")) == 1
    out_ref[0] = first_ref[0]
    out_ref[1] = second_ref[0]

    @pl.when(second)
    def _():
        out_ref[2:] = second_ref[1:]

    @pl.when(jnp.logical_not(second))
    def _():
        out_ref[2:] = first_ref[1:]


def final_kernel(plan, n_ex, n_sub, own, *refs):
    parts, (gram_ref, scores_ref, all_ref, gram_buf, scores_buf, sems) = refs[:-6], refs[-6:]
    start = 0
    for part in parts:
        all_ref[start : start + part.shape[0]] = part[...]
        start += part.shape[0]
    ex, lay, sub = lax.axis_index("ex"), lax.axis_index("lay"), lax.axis_index("sub")
    slots, layers, units = plan(ex, lay, sub)
    half = all_ref.shape[2]
    n_rows, per_half = half * n_sub // n_ex, n_ex // n_sub

    def halves_of(block):
        pieces = all_ref[block].astype(F32)
        return [pieces[h * 2 * own : (h + 1) * 2 * own] for h in range(n_sub)]

    def choose(values, index):
        result = values[0]
        for i in range(1, len(values)):
            result = jnp.where(index == i, values[i], result)
        return result

    lefts, rights = [], []
    for block in slots:
        halves = halves_of(block)
        cuts = [halves[e // per_half][:, e % per_half * n_rows : (e % per_half + 1) * n_rows] for e in range(n_ex)]
        left, right = choose(cuts, ex), choose(halves, sub)
        lefts += [left, pltpu.roll(left, own, 0)]
        rights += [right, right]
    left = jnp.concatenate(lefts, axis=0).astype(BF16)
    right = jnp.concatenate(rights, axis=0).astype(BF16)
    copies = []
    step = n_rows // gram_buf.shape[0]
    for at in range(gram_buf.shape[0]):
        rows = slice(at * step, (at + 1) * step)
        gram = lax.dot_general(left[:, rows], right, FIRST, preferred_element_type=F32)
        gram_buf[at] = gram * (1.0 / (own * n_ex))
        copies.append(pltpu.make_async_copy(gram_buf.at[at], gram_ref.at[0, rows, :], sems.at[at]))
        copies[-1].start()

    layers = [halves_of(block) for block in layers]
    blocks = {}
    for block, behind, core, column, fits in units:
        grads = [choose([halves[h] for halves in layers], behind) for h in range(n_sub)]
        part = 0.0
        for h in range(n_sub):
            turned = choose(grads, lax.rem(core + h + n_sub - 1, n_sub)).astype(BF16)
            part += lax.dot_general(turned, all_ref[block + h], LAST, preferred_element_type=F32)
        part = part[:own] + part[own:]
        part = part if fits is None else jnp.where(fits, part, 0.0)
        blocks[column] = blocks.get(column, 0.0) + part
    blocks = [blocks[column] for column in sorted(blocks)]
    scores_buf[...] = blocks[0] if len(blocks) == 1 else jnp.concatenate(blocks, axis=1)
    copies.append(pltpu.make_async_copy(scores_buf, scores_ref, sems.at[len(copies)]))
    copies[-1].start()
    for copy in copies:
        copy.wait()


def solution(mesh):
    n_ex, n_lay, n_sub = mesh.shape["ex"], mesh.shape["lay"], mesh.shape["sub"]
    group, per_blk = n_ex // n_lay, n_ex // (n_lay * n_sub)

    def flat(ex, lay, sub):
        return (ex * n_lay + lay) * n_sub + sub

    devices = [(ex, lay, sub) for ex in range(n_ex) for lay in range(n_lay) for sub in range(n_sub)]

    query_pairs = [
        (
            flat(ex, lay, sub),
            flat(ex % group * n_lay + (lay + n_lay - 1) % n_lay, ex // group, (sub + 1) % n_sub),
        )
        for ex, lay, sub in devices
    ]

    moves = [("lay", 1), ("ex", n_ex - 1), ("ex", n_ex // 2), ("ex", 1)]
    moves += [("ex", k) for k in range(2, n_ex - 1) if k != n_ex // 2] + [("lay", k) for k in range(2, n_lay)]
    rounds = -(-len(moves) // n_sub)

    def sender_of(at, sub):
        return (sub + (at == 1)) % n_sub

    def turned(ex, lay):
        return (ex // (n_ex // 2) + lay) % 2 == 0

    def source_of(at, ex, lay, sub):
        sender = sender_of(at, sub)
        if sub == 0 and at < 2 and turned(ex, lay):
            at = 1 - at
        axis, k = moves[min(at * n_sub + sub, len(moves) - 1)]
        return flat((ex + k) % n_ex, lay, sender) if axis == "ex" else flat(ex, (lay + k) % n_lay, sender)

    compact = (n_ex, n_lay, n_sub) == (4, 2, 2)

    def lacked(ex, lay, sub):
        return jnp.where(sub == 0, jnp.where(turned(ex, lay), 0, 1), 1 - (ex + ex // 2) % 2)

    def compact_plan(ex, lay, sub):
        across = lacked(ex, lay, 0)
        beside = lacked(ex, lay, 1)

        def grads_at(core, turn):
            return jnp.where(sub == core, 3 + 3 * turn, 9 + turn)

        slots = [0, grads_at(0, across), grads_at(1, 0), grads_at(1, 1)]
        layers = [0, grads_at(0, 1 - across)]
        same = jnp.where(ex // 2 == sub, 1, jnp.where(sub == 0, 4 + 3 * across, 11))
        other = jnp.where(sub == 0, 11, 4 + 3 * (1 - beside))
        near = jnp.where(ex // 2 == sub, sub, across)
        far = jnp.where(sub == 0, 1 - beside, beside)
        units = [(same, (ex + 1 + lay) % 2, near, 0, None), (other, (ex + lay) % 2, far, 0, None)]
        return slots, layers, units

    def general_plan(ex, lay, sub):
        size = 1 + n_sub
        slots, layers, sources = [0], [0], [(ex, sub)]
        for at, (axis, k) in enumerate(moves):
            core, turn = at % n_sub, at // n_sub
            if core == 0 and turn < 2:
                turn = jnp.where(turned(ex, lay), 1 - turn, turn)
            block = (1 + (core - sub + n_sub) % n_sub * rounds + turn) * size
            if axis == "ex":
                slots.append(block)
                sources.append(((ex + k) % n_ex, sender_of(turn, core)))
            else:
                layers.append(block)
        units = []
        for block, (source, core) in zip(slots, sources):
            behind, row = (source % n_lay + 1 - lay + n_lay) % n_lay, source // n_lay
            for column in range(per_blk):
                units.append((block + 1, behind, core, column, row == sub * per_blk + column))
        return slots, layers, units

    def rotate(value, k):
        return lax.ppermute(value, "sub", [((i + k) % n_sub, i) for i in range(n_sub)])

    def body(layer_inputs, output_grads, basis_in, basis_out, queries):
        _, tokens, depth = layer_inputs.shape
        basis = basis_in.shape[1]
        own = tokens // LEN
        width = basis * basis
        rows, half = queries.shape[1:]

        chunk = lax.ppermute(queries[0], AXES, query_pairs)
        pick_x, pick_g = pl.pallas_call(
            functools.partial(picks_kernel, basis),
            out_shape=(
                jax.ShapeDtypeStruct((8 * basis, 4 * basis), BF16),
                jax.ShapeDtypeStruct((8 * basis, width), BF16),
            ),
            out_specs=(VMEM,) * 2,
            compiler_params=PARAMS,
            cost_estimate=pl.CostEstimate(flops=3 * 10**8, bytes_accessed=0, transcendentals=0),
            name="picks",
        )()
        basis_in, basis_out, pick_x = lax.optimization_barrier((basis_in, basis_out, pick_x))
        proj_x = lax.dot_general(basis_in[0], layer_inputs[0], LAST, preferred_element_type=F32)
        proj_g = lax.dot_general(basis_out[0], output_grads[0], LAST, preferred_element_type=F32)
        proj = jnp.concatenate([proj_x, proj_g])
        parts = [proj] + [rotate(proj, k) for k in range(1, n_sub)]
        chunk = pl.pallas_call(
            chunk_kernel,
            out_shape=jax.ShapeDtypeStruct((rows, half), BF16),
            in_specs=[VMEM],
            out_specs=VMEM,
            compiler_params=PARAMS,
            cost_estimate=pl.CostEstimate(flops=10**11, bytes_accessed=10**9, transcendentals=0),
            name="chunk",
        )(chunk)
        chunks = [chunk] + [rotate(chunk, k) for k in range(1, n_sub)]

        grads = pl.pallas_call(
            functools.partial(grads_kernel, n_sub),
            out_shape=jax.ShapeDtypeStruct((2 * own * n_sub, half), BF16),
            in_specs=[VMEM] * (n_sub + 2),
            out_specs=VMEM,
            compiler_params=PARAMS,
            name="grads",
        )(*parts, pick_x, pick_g)

        mine = jnp.stack([grads] + chunks)
        received = []
        for at in range(rounds):
            pairs = [(source_of(at, *device), flat(*device)) for device in devices]
            received.append(lax.ppermute(mine, AXES, pairs))
        if compact:
            swapped = pl.pallas_call(
                functools.partial(swap_kernel, lacked),
                out_shape=jax.ShapeDtypeStruct((4, rows, half), BF16),
                in_specs=[VMEM] * 2,
                out_specs=VMEM,
                compiler_params=PARAMS,
                name="swap",
            )(*received)
            blocks = [mine] + received + [rotate(swapped, 1)]
        else:
            both = jnp.concatenate(received)
            blocks = [mine, both] + [rotate(both, k) for k in range(1, n_sub)]

        pieces = 2 if width // n_ex % 256 == 0 else 1
        return pl.pallas_call(
            functools.partial(final_kernel, compact_plan if compact else general_plan, n_ex, n_sub, own),
            out_shape=(
                jax.ShapeDtypeStruct((1, width // n_ex, half), F32),
                jax.ShapeDtypeStruct((own, rows * per_blk), F32),
            ),
            in_specs=[VMEM] * len(blocks),
            out_specs=(ANY, ANY),
            scratch_shapes=[
                pltpu.VMEM((sum(block.shape[0] for block in blocks), rows, half), BF16),
                pltpu.VMEM((pieces, width // n_ex // pieces, half), F32),
                pltpu.VMEM((own, rows * per_blk), F32),
                pltpu.SemaphoreType.DMA((pieces + 1,)),
            ],
            compiler_params=PARAMS,
            name="gram_and_scores",
        )(*blocks)

    in_specs = (
        P("lay", ("grp", "ex"), "sub"),
        P("lay", ("grp", "ex"), "sub"),
        P("lay", None, "sub"),
        P("lay", None, "sub"),
        P("lay", "ex", "sub"),
    )
    out_specs = (P(("grp", "lay"), "ex", "sub"), P(("grp", "ex"), ("lay", "sub")))
    return jax.shard_map(body, mesh=mesh, in_specs=in_specs, out_specs=out_specs, check_vma=False)
```

```python
import functools

import jax
import jax.numpy as jnp
from jax import lax
from jax.experimental import pallas as pl
from jax.experimental.pallas import tpu as pltpu
from jax.sharding import PartitionSpec as P

LEN = 64
AXES = ("ex", "lay", "sub")
F32, BF16 = jnp.float32, jnp.bfloat16
VMEM = pl.BlockSpec(memory_space=pltpu.VMEM)
ANY = pl.BlockSpec(memory_space=pl.ANY)
LAST = (((1,), (1,)), ((), ()))
FIRST = (((0,), (0,)), ((), ()))
DEAL = (
    (5, 7, 1, 3),
    (2, 5, 7, 1),
    (0, 5, 7, 3),
    (3, 6, 5, 0),
    (2, 4, 6, 0),
    (4, 6, 3, 1),
    (0, 7, 4, 2),
    (2, 6, 4, 1),
)
PARAMS = pltpu.CompilerParams(vmem_limit_bytes=16 * 1024 * 1024)


def picks_kernel(basis, pick_x_ref, pick_g_ref):
    rows, width = pick_g_ref.shape
    lanes, pair = pick_x_ref.shape[1], 2 * basis
    row = lax.broadcasted_iota(jnp.int32, (rows, lanes), 0) % pair
    col = lax.broadcasted_iota(jnp.int32, (rows, lanes), 1)
    pick_x_ref[...] = jnp.where(row == col % basis, 1.0, 0.0).astype(BF16)
    gap = row - basis - col // basis
    for j in range(width // lanes):
        pick_g_ref[:, j * lanes : (j + 1) * lanes] = jnp.where(gap == j * (lanes // basis), 1.0, 0.0).astype(BF16)


def chunk_kernel(in_ref, out_ref):
    out_ref[...] = in_ref[...]


def grads_kernel(n_sub, *refs):
    parts, (pick_x_ref, pick_g_ref, out_ref) = refs[:n_sub], refs[n_sub:]
    total = parts[0][...]
    for part in parts[1:]:
        total += part[...]
    high = total.astype(BF16).astype(F32)
    rest = total - high
    mid = rest.astype(BF16).astype(F32)
    low = rest - mid
    pieces = [jnp.concatenate([high, mid]).T, jnp.concatenate([low, jnp.zeros_like(low)]).T]
    pieces = jnp.concatenate(pieces, axis=1).astype(BF16)
    own = pieces.shape[0] // LEN
    lanes, width = pick_x_ref.shape[1], pick_g_ref.shape[1]
    tiled_x = jnp.dot(pieces, pick_x_ref[...], preferred_element_type=F32)
    tiles = []
    for j in range(width // lanes):
        pick_g = pick_g_ref[:, j * lanes : (j + 1) * lanes]
        product = jnp.dot(pieces, pick_g, preferred_element_type=F32) * tiled_x
        tiles.append(product.reshape(own, LEN, lanes).sum(axis=1))
    grads = jnp.concatenate(tiles, axis=1)
    high = grads.astype(BF16).astype(F32)
    low = grads - high
    half = width // n_sub
    rows = []
    for h in range(n_sub):
        cols = slice(h * half, (h + 1) * half)
        rows += [high[:, cols], low[:, cols]]
    out_ref[...] = jnp.concatenate(rows, axis=0).astype(BF16)


def swap_kernel(lacked, first_ref, second_ref, out_ref):
    second = lacked(lax.axis_index("ex"), lax.axis_index("lay"), lax.axis_index("sub")) == 1
    out_ref[0] = first_ref[0]
    out_ref[1] = second_ref[0]

    @pl.when(second)
    def _():
        out_ref[2:] = second_ref[1:]

    @pl.when(jnp.logical_not(second))
    def _():
        out_ref[2:] = first_ref[1:]


def final_kernel(plan, n_ex, n_sub, own, *refs):
    parts, (gram_ref, scores_ref, all_ref, gram_buf, scores_buf, sems) = refs[:-6], refs[-6:]
    start = 0
    for part in parts:
        all_ref[start : start + part.shape[0]] = part[...]
        start += part.shape[0]
    ex, lay, sub = lax.axis_index("ex"), lax.axis_index("lay"), lax.axis_index("sub")
    slots, layers, units = plan(ex, lay, sub)
    half = all_ref.shape[2]
    n_rows, per_half = half * n_sub // n_ex, n_ex // n_sub

    def halves_of(block):
        pieces = all_ref[block].astype(F32)
        return [pieces[h * 2 * own : (h + 1) * 2 * own] for h in range(n_sub)]

    def choose(values, index):
        result = values[0]
        for i in range(1, len(values)):
            result = jnp.where(index == i, values[i], result)
        return result

    lefts, rights = [], []
    for block in slots:
        halves = halves_of(block)
        cuts = [halves[e // per_half][:, e % per_half * n_rows : (e % per_half + 1) * n_rows] for e in range(n_ex)]
        left, right = choose(cuts, ex), choose(halves, sub)
        lefts += [left, pltpu.roll(left, own, 0)]
        rights += [right, right]
    left = jnp.concatenate(lefts, axis=0).astype(BF16)
    right = jnp.concatenate(rights, axis=0).astype(BF16)
    copies = []
    step = n_rows // gram_buf.shape[0]
    for at in range(gram_buf.shape[0]):
        rows = slice(at * step, (at + 1) * step)
        gram = lax.dot_general(left[:, rows], right, FIRST, preferred_element_type=F32)
        gram_buf[at] = gram * (1.0 / (own * n_ex))
        copies.append(pltpu.make_async_copy(gram_buf.at[at], gram_ref.at[0, rows, :], sems.at[at]))
        copies[-1].start()

    layers = [halves_of(block) for block in layers]
    blocks = {}
    for block, behind, core, column, fits in units:
        grads = [choose([halves[h] for halves in layers], behind) for h in range(n_sub)]
        part = 0.0
        for h in range(n_sub):
            turned = choose(grads, lax.rem(core + h + n_sub - 1, n_sub)).astype(BF16)
            part += lax.dot_general(turned, all_ref[block + h], LAST, preferred_element_type=F32)
        part = part[:own] + part[own:]
        part = part if fits is None else jnp.where(fits, part, 0.0)
        blocks[column] = blocks.get(column, 0.0) + part
    blocks = [blocks[column] for column in sorted(blocks)]
    scores_buf[...] = blocks[0] if len(blocks) == 1 else jnp.concatenate(blocks, axis=1)
    copies.append(pltpu.make_async_copy(scores_buf, scores_ref, sems.at[len(copies)]))
    copies[-1].start()
    for copy in copies:
        copy.wait()


def solution(mesh):
    n_ex, n_lay, n_sub = mesh.shape["ex"], mesh.shape["lay"], mesh.shape["sub"]
    group, per_blk = n_ex // n_lay, n_ex // (n_lay * n_sub)

    def flat(ex, lay, sub):
        return (ex * n_lay + lay) * n_sub + sub

    devices = [(ex, lay, sub) for ex in range(n_ex) for lay in range(n_lay) for sub in range(n_sub)]

    query_pairs = [
        (
            flat(ex, lay, sub),
            flat(ex % group * n_lay + (lay + n_lay - 1) % n_lay, ex // group, (sub + 1) % n_sub),
        )
        for ex, lay, sub in devices
    ]

    compact = (n_ex, n_lay, n_sub) == (4, 2, 2)
    moves = [("ex", k) for k in range(1, n_ex)] + [("lay", k) for k in range(1, n_lay)]
    rounds = -(-len(moves) // n_sub)

    def source_of(at, ex, lay, sub):
        if compact:
            row = DEAL[ex * n_lay + lay]
            kind = [value // 2 for value in row].index(2 * at + sub)
            sender = row[kind] % 2
            (axis, k) = ("ex", kind) if kind else ("lay", 1)
        else:
            sender = sub
            axis, k = moves[min(at * n_sub + sub, len(moves) - 1)]
        return flat((ex + k) % n_ex, lay, sender) if axis == "ex" else flat(ex, (lay + k) % n_lay, sender)

    def dealt(kind, ex, lay):
        values = [row[kind] for row in DEAL]
        result = values[0]
        for chip in range(1, len(values)):
            result = jnp.where(ex * n_lay + lay == chip, values[chip], result)
        return result // 4, result // 2 % 2, result % 2

    def unit_kinds(ex, lay):
        up, down = dealt(1, ex, lay), dealt(3, ex, lay)
        odd = ex % 2 == 1
        beside = [jnp.where(odd, b, a) for a, b in zip(up, down)]
        beyond = [jnp.where(odd, a, b) for a, b in zip(up, down)]
        return beside, dealt(2, ex, lay), beyond

    def lacked(ex, lay, sub):
        beside, across, beyond = unit_kinds(ex, lay)
        later = jnp.where(across[1] == sub, across[0], beyond[0])
        return jnp.where(ex // 2 == sub, later, beside[0])

    def compact_plan(ex, lay, sub):
        def grads_at(kind):
            turn, core, _ = dealt(kind, ex, lay)
            return jnp.where(sub == core, 3 + 3 * turn, 9 + turn)

        def unit_at(kind):
            turn, core, _ = kind
            return jnp.where(sub == core, 4 + 3 * turn, 11)

        slots = [0, grads_at(1), grads_at(2), grads_at(3)]
        layers = [0, grads_at(0)]
        beside, across, beyond = unit_kinds(ex, lay)
        mine = ex // 2 == sub
        first, first_core = jnp.where(mine, 1, unit_at(across)), jnp.where(mine, sub, across[2])
        second = jnp.where(mine, unit_at(beside), unit_at(beyond))
        second_core = jnp.where(mine, beside[2], beyond[2])
        units = [(first, (ex + 1 + lay) % 2, first_core, 0, None), (second, (ex + lay) % 2, second_core, 0, None)]
        return slots, layers, units

    def general_plan(ex, lay, sub):
        size = 1 + n_sub
        slots, layers, sources = [0], [0], [(ex, sub)]
        for at, (axis, k) in enumerate(moves):
            core, turn = at % n_sub, at // n_sub
            block = (1 + (core - sub + n_sub) % n_sub * rounds + turn) * size
            if axis == "ex":
                slots.append(block)
                sources.append(((ex + k) % n_ex, core))
            else:
                layers.append(block)
        units = []
        for block, (source, core) in zip(slots, sources):
            behind, row = (source % n_lay + 1 - lay + n_lay) % n_lay, source // n_lay
            for column in range(per_blk):
                units.append((block + 1, behind, core, column, row == sub * per_blk + column))
        return slots, layers, units

    def rotate(value, k):
        return lax.ppermute(value, "sub", [((i + k) % n_sub, i) for i in range(n_sub)])

    def body(layer_inputs, output_grads, basis_in, basis_out, queries):
        _, tokens, depth = layer_inputs.shape
        basis = basis_in.shape[1]
        own = tokens // LEN
        width = basis * basis
        rows, half = queries.shape[1:]

        chunk = lax.ppermute(queries[0], AXES, query_pairs)
        pick_x, pick_g = pl.pallas_call(
            functools.partial(picks_kernel, basis),
            out_shape=(
                jax.ShapeDtypeStruct((8 * basis, 4 * basis), BF16),
                jax.ShapeDtypeStruct((8 * basis, width), BF16),
            ),
            out_specs=(VMEM,) * 2,
            compiler_params=PARAMS,
            cost_estimate=pl.CostEstimate(flops=3 * 10**8, bytes_accessed=0, transcendentals=0),
            name="picks",
        )()
        basis_in, basis_out, pick_x = lax.optimization_barrier((basis_in, basis_out, pick_x))
        proj_x = lax.dot_general(basis_in[0], layer_inputs[0], LAST, preferred_element_type=F32)
        proj_g = lax.dot_general(basis_out[0], output_grads[0], LAST, preferred_element_type=F32)
        proj = jnp.concatenate([proj_x, proj_g])
        parts = [proj] + [rotate(proj, k) for k in range(1, n_sub)]
        chunk = pl.pallas_call(
            chunk_kernel,
            out_shape=jax.ShapeDtypeStruct((rows, half), BF16),
            in_specs=[VMEM],
            out_specs=VMEM,
            compiler_params=PARAMS,
            cost_estimate=pl.CostEstimate(flops=10**11, bytes_accessed=10**9, transcendentals=0),
            name="chunk",
        )(chunk)
        chunks = [chunk] + [rotate(chunk, k) for k in range(1, n_sub)]

        grads = pl.pallas_call(
            functools.partial(grads_kernel, n_sub),
            out_shape=jax.ShapeDtypeStruct((2 * own * n_sub, half), BF16),
            in_specs=[VMEM] * (n_sub + 2),
            out_specs=VMEM,
            compiler_params=PARAMS,
            name="grads",
        )(*parts, pick_x, pick_g)

        mine = jnp.stack([grads] + chunks)
        received = []
        for at in range(rounds):
            pairs = [(source_of(at, *device), flat(*device)) for device in devices]
            received.append(lax.ppermute(mine, AXES, pairs))
        if compact:
            swapped = pl.pallas_call(
                functools.partial(swap_kernel, lacked),
                out_shape=jax.ShapeDtypeStruct((4, rows, half), BF16),
                in_specs=[VMEM] * 2,
                out_specs=VMEM,
                compiler_params=PARAMS,
                name="swap",
            )(*received)
            blocks = [mine] + received + [rotate(swapped, 1)]
        else:
            both = jnp.concatenate(received)
            blocks = [mine, both] + [rotate(both, k) for k in range(1, n_sub)]

        pieces = 2 if width // n_ex % 256 == 0 else 1
        return pl.pallas_call(
            functools.partial(final_kernel, compact_plan if compact else general_plan, n_ex, n_sub, own),
            out_shape=(
                jax.ShapeDtypeStruct((1, width // n_ex, half), F32),
                jax.ShapeDtypeStruct((own, rows * per_blk), F32),
            ),
            in_specs=[VMEM] * len(blocks),
            out_specs=(ANY, ANY),
            scratch_shapes=[
                pltpu.VMEM((sum(block.shape[0] for block in blocks), rows, half), BF16),
                pltpu.VMEM((pieces, width // n_ex // pieces, half), F32),
                pltpu.VMEM((own, rows * per_blk), F32),
                pltpu.SemaphoreType.DMA((pieces + 1,)),
            ],
            compiler_params=PARAMS,
            name="gram_and_scores",
        )(*blocks)

    in_specs = (
        P("lay", ("grp", "ex"), "sub"),
        P("lay", ("grp", "ex"), "sub"),
        P("lay", None, "sub"),
        P("lay", None, "sub"),
        P("lay", "ex", "sub"),
    )
    out_specs = (P(("grp", "lay"), "ex", "sub"), P(("grp", "ex"), ("lay", "sub")))
    return jax.shard_map(body, mesh=mesh, in_specs=in_specs, out_specs=out_specs, check_vma=False)
```

```python
import functools

import jax
import jax.numpy as jnp
from jax import lax
from jax.experimental import pallas as pl
from jax.experimental.pallas import tpu as pltpu
from jax.sharding import PartitionSpec as P

LEN = 64
AXES = ("ex", "lay", "sub")
F32, BF16 = jnp.float32, jnp.bfloat16
VMEM = pl.BlockSpec(memory_space=pltpu.VMEM)
ANY = pl.BlockSpec(memory_space=pl.ANY)
LAST = (((1,), (1,)), ((), ()))
FIRST = (((0,), (0,)), ((), ()))
DEAL = (
    (5, 7, 0, 3),
    (2, 5, 7, 1),
    (4, 6, 0, 3),
    (1, 4, 7, 2),
    (0, 7, 4, 2),
    (5, 6, 3, 0),
    (2, 5, 6, 1),
    (4, 6, 1, 3),
)
PARAMS = pltpu.CompilerParams(vmem_limit_bytes=16 * 1024 * 1024)


def picks_kernel(basis, pick_x_ref, pick_g_ref):
    rows, width = pick_g_ref.shape
    lanes, pair = pick_x_ref.shape[1], 2 * basis
    row = lax.broadcasted_iota(jnp.int32, (rows, lanes), 0) % pair
    col = lax.broadcasted_iota(jnp.int32, (rows, lanes), 1)
    pick_x_ref[...] = jnp.where(row == col % basis, 1.0, 0.0).astype(BF16)
    gap = row - basis - col // basis
    for j in range(width // lanes):
        pick_g_ref[:, j * lanes : (j + 1) * lanes] = jnp.where(gap == j * (lanes // basis), 1.0, 0.0).astype(BF16)


def chunk_kernel(in_ref, out_ref):
    out_ref[...] = in_ref[...]


def grads_kernel(n_sub, *refs):
    parts, (pick_x_ref, pick_g_ref, out_ref) = refs[:n_sub], refs[n_sub:]
    total = parts[0][...]
    for part in parts[1:]:
        total += part[...]
    high = total.astype(BF16).astype(F32)
    rest = total - high
    mid = rest.astype(BF16).astype(F32)
    low = rest - mid
    pieces = [jnp.concatenate([high, mid]).T, jnp.concatenate([low, jnp.zeros_like(low)]).T]
    pieces = jnp.concatenate(pieces, axis=1).astype(BF16)
    own = pieces.shape[0] // LEN
    lanes, width = pick_x_ref.shape[1], pick_g_ref.shape[1]
    tiled_x = jnp.dot(pieces, pick_x_ref[...], preferred_element_type=F32)
    tiles = []
    for j in range(width // lanes):
        pick_g = pick_g_ref[:, j * lanes : (j + 1) * lanes]
        product = jnp.dot(pieces, pick_g, preferred_element_type=F32) * tiled_x
        tiles.append(product.reshape(own, LEN, lanes).sum(axis=1))
    grads = jnp.concatenate(tiles, axis=1)
    high = grads.astype(BF16).astype(F32)
    low = grads - high
    half = width // n_sub
    rows = []
    for h in range(n_sub):
        cols = slice(h * half, (h + 1) * half)
        rows += [high[:, cols], low[:, cols]]
    out_ref[...] = jnp.concatenate(rows, axis=0).astype(BF16)


def swap_kernel(lacked, first_ref, second_ref, out_ref):
    second = lacked(lax.axis_index("ex"), lax.axis_index("lay"), lax.axis_index("sub")) == 1
    out_ref[0] = first_ref[0]
    out_ref[1] = second_ref[0]

    @pl.when(second)
    def _():
        out_ref[2:] = second_ref[1:]

    @pl.when(jnp.logical_not(second))
    def _():
        out_ref[2:] = first_ref[1:]


def final_kernel(plan, n_ex, n_sub, own, *refs):
    parts, (gram_ref, scores_ref, all_ref, gram_buf, scores_buf, sems) = refs[:-6], refs[-6:]
    start = 0
    for part in parts:
        all_ref[start : start + part.shape[0]] = part[...]
        start += part.shape[0]
    ex, lay, sub = lax.axis_index("ex"), lax.axis_index("lay"), lax.axis_index("sub")
    slots, layers, units = plan(ex, lay, sub)
    half = all_ref.shape[2]
    n_rows, per_half = half * n_sub // n_ex, n_ex // n_sub

    def halves_of(block):
        pieces = all_ref[block].astype(F32)
        return [pieces[h * 2 * own : (h + 1) * 2 * own] for h in range(n_sub)]

    def choose(values, index):
        result = values[0]
        for i in range(1, len(values)):
            result = jnp.where(index == i, values[i], result)
        return result

    lefts, rights = [], []
    for block in slots:
        halves = halves_of(block)
        cuts = [halves[e // per_half][:, e % per_half * n_rows : (e % per_half + 1) * n_rows] for e in range(n_ex)]
        left, right = choose(cuts, ex), choose(halves, sub)
        lefts += [left, pltpu.roll(left, own, 0)]
        rights += [right, right]
    left = jnp.concatenate(lefts, axis=0).astype(BF16)
    right = jnp.concatenate(rights, axis=0).astype(BF16)
    copies = []
    step = n_rows // gram_buf.shape[0]
    for at in range(gram_buf.shape[0]):
        rows = slice(at * step, (at + 1) * step)
        gram = lax.dot_general(left[:, rows], right, FIRST, preferred_element_type=F32)
        gram_buf[at] = gram * (1.0 / (own * n_ex))
        copies.append(pltpu.make_async_copy(gram_buf.at[at], gram_ref.at[0, rows, :], sems.at[at]))
        copies[-1].start()

    layers = [halves_of(block) for block in layers]
    blocks = {}
    for block, behind, core, column, fits in units:
        grads = [choose([halves[h] for halves in layers], behind) for h in range(n_sub)]
        part = 0.0
        for h in range(n_sub):
            turned = choose(grads, lax.rem(core + h + n_sub - 1, n_sub)).astype(BF16)
            part += lax.dot_general(turned, all_ref[block + h], LAST, preferred_element_type=F32)
        part = part[:own] + part[own:]
        part = part if fits is None else jnp.where(fits, part, 0.0)
        blocks[column] = blocks.get(column, 0.0) + part
    blocks = [blocks[column] for column in sorted(blocks)]
    scores_buf[...] = blocks[0] if len(blocks) == 1 else jnp.concatenate(blocks, axis=1)
    copies.append(pltpu.make_async_copy(scores_buf, scores_ref, sems.at[len(copies)]))
    copies[-1].start()
    for copy in copies:
        copy.wait()


def solution(mesh):
    n_ex, n_lay, n_sub = mesh.shape["ex"], mesh.shape["lay"], mesh.shape["sub"]
    group, per_blk = n_ex // n_lay, n_ex // (n_lay * n_sub)

    def flat(ex, lay, sub):
        return (ex * n_lay + lay) * n_sub + sub

    devices = [(ex, lay, sub) for ex in range(n_ex) for lay in range(n_lay) for sub in range(n_sub)]

    query_pairs = [
        (
            flat(ex, lay, sub),
            flat(ex % group * n_lay + (lay + n_lay - 1) % n_lay, ex // group, (sub + 1) % n_sub),
        )
        for ex, lay, sub in devices
    ]

    compact = (n_ex, n_lay, n_sub) == (4, 2, 2)
    moves = [("ex", k) for k in range(1, n_ex)] + [("lay", k) for k in range(1, n_lay)]
    rounds = -(-len(moves) // n_sub)

    def source_of(at, ex, lay, sub):
        if compact:
            row = DEAL[ex * n_lay + lay]
            kind = [value // 2 for value in row].index(2 * at + sub)
            sender = row[kind] % 2
            (axis, k) = ("ex", kind) if kind else ("lay", 1)
        else:
            sender = sub
            axis, k = moves[min(at * n_sub + sub, len(moves) - 1)]
        return flat((ex + k) % n_ex, lay, sender) if axis == "ex" else flat(ex, (lay + k) % n_lay, sender)

    def dealt(kind, ex, lay):
        values = [row[kind] for row in DEAL]
        result = values[0]
        for chip in range(1, len(values)):
            result = jnp.where(ex * n_lay + lay == chip, values[chip], result)
        return result // 4, result // 2 % 2, result % 2

    def unit_kinds(ex, lay):
        up, down = dealt(1, ex, lay), dealt(3, ex, lay)
        odd = ex % 2 == 1
        beside = [jnp.where(odd, b, a) for a, b in zip(up, down)]
        beyond = [jnp.where(odd, a, b) for a, b in zip(up, down)]
        return beside, dealt(2, ex, lay), beyond

    def lacked(ex, lay, sub):
        beside, across, beyond = unit_kinds(ex, lay)
        later = jnp.where(across[1] == sub, across[0], beyond[0])
        return jnp.where(ex // 2 == sub, later, beside[0])

    def compact_plan(ex, lay, sub):
        def grads_at(kind):
            turn, core, _ = dealt(kind, ex, lay)
            return jnp.where(sub == core, 3 + 3 * turn, 9 + turn)

        def unit_at(kind):
            turn, core, _ = kind
            return jnp.where(sub == core, 4 + 3 * turn, 11)

        slots = [0, grads_at(1), grads_at(2), grads_at(3)]
        layers = [0, grads_at(0)]
        beside, across, beyond = unit_kinds(ex, lay)
        mine = ex // 2 == sub
        first, first_core = jnp.where(mine, 1, unit_at(across)), jnp.where(mine, sub, across[2])
        second = jnp.where(mine, unit_at(beside), unit_at(beyond))
        second_core = jnp.where(mine, beside[2], beyond[2])
        units = [(first, (ex + 1 + lay) % 2, first_core, 0, None), (second, (ex + lay) % 2, second_core, 0, None)]
        return slots, layers, units

    def general_plan(ex, lay, sub):
        size = 1 + n_sub
        slots, layers, sources = [0], [0], [(ex, sub)]
        for at, (axis, k) in enumerate(moves):
            core, turn = at % n_sub, at // n_sub
            block = (1 + (core - sub + n_sub) % n_sub * rounds + turn) * size
            if axis == "ex":
                slots.append(block)
                sources.append(((ex + k) % n_ex, core))
            else:
                layers.append(block)
        units = []
        for block, (source, core) in zip(slots, sources):
            behind, row = (source % n_lay + 1 - lay + n_lay) % n_lay, source // n_lay
            for column in range(per_blk):
                units.append((block + 1, behind, core, column, row == sub * per_blk + column))
        return slots, layers, units

    def rotate(value, k):
        return lax.ppermute(value, "sub", [((i + k) % n_sub, i) for i in range(n_sub)])

    def body(layer_inputs, output_grads, basis_in, basis_out, queries):
        _, tokens, depth = layer_inputs.shape
        basis = basis_in.shape[1]
        own = tokens // LEN
        width = basis * basis
        rows, half = queries.shape[1:]

        chunk = lax.ppermute(queries[0], AXES, query_pairs)
        pick_x, pick_g = pl.pallas_call(
            functools.partial(picks_kernel, basis),
            out_shape=(
                jax.ShapeDtypeStruct((8 * basis, 4 * basis), BF16),
                jax.ShapeDtypeStruct((8 * basis, width), BF16),
            ),
            out_specs=(VMEM,) * 2,
            compiler_params=PARAMS,
            cost_estimate=pl.CostEstimate(flops=3 * 10**8, bytes_accessed=0, transcendentals=0),
            name="picks",
        )()
        basis_in, basis_out, pick_x = lax.optimization_barrier((basis_in, basis_out, pick_x))
        proj_x = lax.dot_general(basis_in[0], layer_inputs[0], LAST, preferred_element_type=F32)
        proj_g = lax.dot_general(basis_out[0], output_grads[0], LAST, preferred_element_type=F32)
        proj = jnp.concatenate([proj_x, proj_g])
        parts = [proj] + [rotate(proj, k) for k in range(1, n_sub)]
        chunk = pl.pallas_call(
            chunk_kernel,
            out_shape=jax.ShapeDtypeStruct((rows, half), BF16),
            in_specs=[VMEM],
            out_specs=VMEM,
            compiler_params=PARAMS,
            cost_estimate=pl.CostEstimate(flops=10**11, bytes_accessed=10**9, transcendentals=0),
            name="chunk",
        )(chunk)
        chunks = [chunk] + [rotate(chunk, k) for k in range(1, n_sub)]

        grads = pl.pallas_call(
            functools.partial(grads_kernel, n_sub),
            out_shape=jax.ShapeDtypeStruct((2 * own * n_sub, half), BF16),
            in_specs=[VMEM] * (n_sub + 2),
            out_specs=VMEM,
            compiler_params=PARAMS,
            name="grads",
        )(*parts, pick_x, pick_g)

        mine = jnp.stack([grads] + chunks)
        received = []
        for at in range(rounds):
            pairs = [(source_of(at, *device), flat(*device)) for device in devices]
            received.append(lax.ppermute(mine, AXES, pairs))
        if compact:
            swapped = pl.pallas_call(
                functools.partial(swap_kernel, lacked),
                out_shape=jax.ShapeDtypeStruct((4, rows, half), BF16),
                in_specs=[VMEM] * 2,
                out_specs=VMEM,
                compiler_params=PARAMS,
                name="swap",
            )(*received)
            blocks = [mine] + received + [rotate(swapped, 1)]
        else:
            both = jnp.concatenate(received)
            blocks = [mine, both] + [rotate(both, k) for k in range(1, n_sub)]

        pieces = 2 if width // n_ex % 256 == 0 else 1
        return pl.pallas_call(
            functools.partial(final_kernel, compact_plan if compact else general_plan, n_ex, n_sub, own),
            out_shape=(
                jax.ShapeDtypeStruct((1, width // n_ex, half), F32),
                jax.ShapeDtypeStruct((own, rows * per_blk), F32),
            ),
            in_specs=[VMEM] * len(blocks),
            out_specs=(ANY, ANY),
            scratch_shapes=[
                pltpu.VMEM((sum(block.shape[0] for block in blocks), rows, half), BF16),
                pltpu.VMEM((pieces, width // n_ex // pieces, half), F32),
                pltpu.VMEM((own, rows * per_blk), F32),
                pltpu.SemaphoreType.DMA((pieces + 1,)),
            ],
            compiler_params=PARAMS,
            name="gram_and_scores",
        )(*blocks)

    in_specs = (
        P("lay", ("grp", "ex"), "sub"),
        P("lay", ("grp", "ex"), "sub"),
        P("lay", None, "sub"),
        P("lay", None, "sub"),
        P("lay", "ex", "sub"),
    )
    out_specs = (P(("grp", "lay"), "ex", "sub"), P(("grp", "ex"), ("lay", "sub")))
    return jax.shard_map(body, mesh=mesh, in_specs=in_specs, out_specs=out_specs, check_vma=False)
```

```python
import functools

import jax
import jax.numpy as jnp
from jax import lax
from jax.experimental import pallas as pl
from jax.experimental.pallas import tpu as pltpu
from jax.sharding import PartitionSpec as P

LEN = 64
AXES = ("ex", "lay", "sub")
F32, BF16 = jnp.float32, jnp.bfloat16
VMEM = pl.BlockSpec(memory_space=pltpu.VMEM)
ANY = pl.BlockSpec(memory_space=pl.ANY)
LAST = (((1,), (1,)), ((), ()))
FIRST = (((0,), (0,)), ((), ()))
PARAMS = pltpu.CompilerParams(vmem_limit_bytes=16 * 1024 * 1024)


def picks_kernel(basis, pick_x_ref, pick_g_ref):
    rows, width = pick_g_ref.shape
    lanes, pair = pick_x_ref.shape[1], 2 * basis
    row = lax.broadcasted_iota(jnp.int32, (rows, lanes), 0) % pair
    col = lax.broadcasted_iota(jnp.int32, (rows, lanes), 1)
    pick_x_ref[...] = jnp.where(row == col % basis, 1.0, 0.0).astype(BF16)
    gap = row - basis - col // basis
    for j in range(width // lanes):
        pick_g_ref[:, j * lanes : (j + 1) * lanes] = jnp.where(gap == j * (lanes // basis), 1.0, 0.0).astype(BF16)


def chunk_kernel(in_ref, out_ref):
    out_ref[...] = in_ref[...]


def grads_kernel(n_sub, *refs):
    parts, (pick_x_ref, pick_g_ref, out_ref) = refs[:n_sub], refs[n_sub:]
    total = parts[0][...]
    for part in parts[1:]:
        total += part[...]
    high = total.astype(BF16).astype(F32)
    rest = total - high
    mid = rest.astype(BF16).astype(F32)
    low = rest - mid
    pieces = [jnp.concatenate([high, mid]).T, jnp.concatenate([low, jnp.zeros_like(low)]).T]
    pieces = jnp.concatenate(pieces, axis=1).astype(BF16)
    own = pieces.shape[0] // LEN
    lanes, width = pick_x_ref.shape[1], pick_g_ref.shape[1]
    tiled_x = jnp.dot(pieces, pick_x_ref[...], preferred_element_type=F32)
    tiles = []
    wide = 2 * lanes if width % (2 * lanes) == 0 else lanes
    tiled_x = jnp.concatenate([tiled_x] * (wide // lanes), axis=1)
    for j in range(width // wide):
        pick_g = pick_g_ref[:, j * wide : (j + 1) * wide]
        product = jnp.dot(pieces, pick_g, preferred_element_type=F32) * tiled_x
        tiles.append(product.reshape(own, LEN, wide).sum(axis=1))
    grads = jnp.concatenate(tiles, axis=1)
    high = grads.astype(BF16).astype(F32)
    low = grads - high
    half = width // n_sub
    rows = []
    for h in range(n_sub):
        cols = slice(h * half, (h + 1) * half)
        rows += [high[:, cols], low[:, cols]]
    out_ref[...] = jnp.concatenate(rows, axis=0).astype(BF16)


def swap_kernel(lacked, first_ref, second_ref, out_ref):
    second = lacked(lax.axis_index("ex"), lax.axis_index("lay"), lax.axis_index("sub")) == 1
    out_ref[0] = first_ref[0]
    out_ref[1] = second_ref[0]

    @pl.when(second)
    def _():
        out_ref[2:] = second_ref[1:]

    @pl.when(jnp.logical_not(second))
    def _():
        out_ref[2:] = first_ref[1:]


def final_kernel(plan, n_ex, n_sub, own, *refs):
    parts, (gram_ref, scores_ref, all_ref, gram_buf, scores_buf, sems) = refs[:-6], refs[-6:]
    start = 0
    for part in parts:
        all_ref[start : start + part.shape[0]] = part[...]
        start += part.shape[0]
    ex, lay, sub = lax.axis_index("ex"), lax.axis_index("lay"), lax.axis_index("sub")
    slots, layers, units = plan(ex, lay, sub)
    half = all_ref.shape[2]
    n_rows, per_half = half * n_sub // n_ex, n_ex // n_sub

    def halves_of(block):
        pieces = all_ref[block].astype(F32)
        return [pieces[h * 2 * own : (h + 1) * 2 * own] for h in range(n_sub)]

    def choose(values, index):
        result = values[0]
        for i in range(1, len(values)):
            result = jnp.where(index == i, values[i], result)
        return result

    lefts, rights = [], []
    for block in slots:
        halves = halves_of(block)
        cuts = [halves[e // per_half][:, e % per_half * n_rows : (e % per_half + 1) * n_rows] for e in range(n_ex)]
        left, right = choose(cuts, ex), choose(halves, sub)
        lefts += [left, pltpu.roll(left, own, 0)]
        rights += [right, right]
    left = jnp.concatenate(lefts, axis=0).astype(BF16)
    right = jnp.concatenate(rights, axis=0).astype(BF16)
    copies = []
    step = n_rows // gram_buf.shape[0]
    for at in range(gram_buf.shape[0]):
        rows = slice(at * step, (at + 1) * step)
        gram = lax.dot_general(left[:, rows], right, FIRST, preferred_element_type=F32)
        gram_buf[at] = gram * (1.0 / (own * n_ex))
        copies.append(pltpu.make_async_copy(gram_buf.at[at], gram_ref.at[0, rows, :], sems.at[at]))
        copies[-1].start()

    layers = [halves_of(block) for block in layers]
    blocks = {}
    for block, behind, core, column, fits in units:
        grads = [choose([halves[h] for halves in layers], behind) for h in range(n_sub)]
        part = 0.0
        for h in range(n_sub):
            turned = choose(grads, lax.rem(core + h + n_sub - 1, n_sub)).astype(BF16)
            part += lax.dot_general(turned, all_ref[block + h], LAST, preferred_element_type=F32)
        part = part[:own] + part[own:]
        part = part if fits is None else jnp.where(fits, part, 0.0)
        blocks[column] = blocks.get(column, 0.0) + part
    blocks = [blocks[column] for column in sorted(blocks)]
    scores_buf[...] = blocks[0] if len(blocks) == 1 else jnp.concatenate(blocks, axis=1)
    copies.append(pltpu.make_async_copy(scores_buf, scores_ref, sems.at[len(copies)]))
    copies[-1].start()
    for copy in copies:
        copy.wait()


def solution(mesh):
    n_ex, n_lay, n_sub = mesh.shape["ex"], mesh.shape["lay"], mesh.shape["sub"]
    group, per_blk = n_ex // n_lay, n_ex // (n_lay * n_sub)

    def flat(ex, lay, sub):
        return (ex * n_lay + lay) * n_sub + sub

    devices = [(ex, lay, sub) for ex in range(n_ex) for lay in range(n_lay) for sub in range(n_sub)]

    query_pairs = [
        (
            flat(ex, lay, sub),
            flat(ex % group * n_lay + (lay + n_lay - 1) % n_lay, ex // group, (sub + 1) % n_sub),
        )
        for ex, lay, sub in devices
    ]

    moves = [("lay", 1), ("ex", n_ex - 1), ("ex", n_ex // 2), ("ex", 1)]
    moves += [("ex", k) for k in range(2, n_ex - 1) if k != n_ex // 2] + [("lay", k) for k in range(2, n_lay)]
    rounds = -(-len(moves) // n_sub)

    def sender_of(at, sub):
        return (sub + (at == 1)) % n_sub

    def turned(ex, lay):
        return (ex // (n_ex // 2) + lay) % 2 == 0

    def source_of(at, ex, lay, sub):
        sender = sender_of(at, sub)
        if sub == 0 and at < 2 and turned(ex, lay):
            at = 1 - at
        axis, k = moves[min(at * n_sub + sub, len(moves) - 1)]
        return flat((ex + k) % n_ex, lay, sender) if axis == "ex" else flat(ex, (lay + k) % n_lay, sender)

    compact = (n_ex, n_lay, n_sub) == (4, 2, 2)

    def lacked(ex, lay, sub):
        return jnp.where(sub == 0, jnp.where(turned(ex, lay), 0, 1), 1 - (ex + ex // 2) % 2)

    def compact_plan(ex, lay, sub):
        across = lacked(ex, lay, 0)
        beside = lacked(ex, lay, 1)

        def grads_at(core, turn):
            return jnp.where(sub == core, 3 + 3 * turn, 9 + turn)

        slots = [0, grads_at(0, across), grads_at(1, 0), grads_at(1, 1)]
        layers = [0, grads_at(0, 1 - across)]
        same = jnp.where(ex // 2 == sub, 1, jnp.where(sub == 0, 4 + 3 * across, 11))
        other = jnp.where(sub == 0, 11, 4 + 3 * (1 - beside))
        near = jnp.where(ex // 2 == sub, sub, across)
        far = jnp.where(sub == 0, 1 - beside, beside)
        units = [(same, (ex + 1 + lay) % 2, near, 0, None), (other, (ex + lay) % 2, far, 0, None)]
        return slots, layers, units

    def general_plan(ex, lay, sub):
        size = 1 + n_sub
        slots, layers, sources = [0], [0], [(ex, sub)]
        for at, (axis, k) in enumerate(moves):
            core, turn = at % n_sub, at // n_sub
            if core == 0 and turn < 2:
                turn = jnp.where(turned(ex, lay), 1 - turn, turn)
            block = (1 + (core - sub + n_sub) % n_sub * rounds + turn) * size
            if axis == "ex":
                slots.append(block)
                sources.append(((ex + k) % n_ex, sender_of(turn, core)))
            else:
                layers.append(block)
        units = []
        for block, (source, core) in zip(slots, sources):
            behind, row = (source % n_lay + 1 - lay + n_lay) % n_lay, source // n_lay
            for column in range(per_blk):
                units.append((block + 1, behind, core, column, row == sub * per_blk + column))
        return slots, layers, units

    def rotate(value, k):
        return lax.ppermute(value, "sub", [((i + k) % n_sub, i) for i in range(n_sub)])

    def body(layer_inputs, output_grads, basis_in, basis_out, queries):
        _, tokens, depth = layer_inputs.shape
        basis = basis_in.shape[1]
        own = tokens // LEN
        width = basis * basis
        rows, half = queries.shape[1:]

        chunk = lax.ppermute(queries[0], AXES, query_pairs)
        pick_x, pick_g = pl.pallas_call(
            functools.partial(picks_kernel, basis),
            out_shape=(
                jax.ShapeDtypeStruct((8 * basis, 4 * basis), BF16),
                jax.ShapeDtypeStruct((8 * basis, width), BF16),
            ),
            out_specs=(VMEM,) * 2,
            compiler_params=PARAMS,
            cost_estimate=pl.CostEstimate(flops=3 * 10**8, bytes_accessed=0, transcendentals=0),
            name="picks",
        )()
        basis_in, basis_out, pick_x = lax.optimization_barrier((basis_in, basis_out, pick_x))
        proj_x = lax.dot_general(basis_in[0], layer_inputs[0], LAST, preferred_element_type=F32)
        proj_g = lax.dot_general(basis_out[0], output_grads[0], LAST, preferred_element_type=F32)
        proj = jnp.concatenate([proj_x, proj_g])
        parts = [proj] + [rotate(proj, k) for k in range(1, n_sub)]
        chunk = pl.pallas_call(
            chunk_kernel,
            out_shape=jax.ShapeDtypeStruct((rows, half), BF16),
            in_specs=[VMEM],
            out_specs=VMEM,
            compiler_params=PARAMS,
            cost_estimate=pl.CostEstimate(flops=10**11, bytes_accessed=10**9, transcendentals=0),
            name="chunk",
        )(chunk)
        chunks = [chunk] + [rotate(chunk, k) for k in range(1, n_sub)]

        grads = pl.pallas_call(
            functools.partial(grads_kernel, n_sub),
            out_shape=jax.ShapeDtypeStruct((2 * own * n_sub, half), BF16),
            in_specs=[VMEM] * (n_sub + 2),
            out_specs=VMEM,
            compiler_params=PARAMS,
            name="grads",
        )(*parts, pick_x, pick_g)

        mine = jnp.stack([grads] + chunks)
        received = []
        for at in range(rounds):
            pairs = [(source_of(at, *device), flat(*device)) for device in devices]
            received.append(lax.ppermute(mine, AXES, pairs))
        if compact:
            swapped = pl.pallas_call(
                functools.partial(swap_kernel, lacked),
                out_shape=jax.ShapeDtypeStruct((4, rows, half), BF16),
                in_specs=[VMEM] * 2,
                out_specs=VMEM,
                compiler_params=PARAMS,
                name="swap",
            )(*received)
            blocks = [mine] + received + [rotate(swapped, 1)]
        else:
            both = jnp.concatenate(received)
            blocks = [mine, both] + [rotate(both, k) for k in range(1, n_sub)]

        pieces = 2 if width // n_ex % 256 == 0 else 1
        return pl.pallas_call(
            functools.partial(final_kernel, compact_plan if compact else general_plan, n_ex, n_sub, own),
            out_shape=(
                jax.ShapeDtypeStruct((1, width // n_ex, half), F32),
                jax.ShapeDtypeStruct((own, rows * per_blk), F32),
            ),
            in_specs=[VMEM] * len(blocks),
            out_specs=(ANY, ANY),
            scratch_shapes=[
                pltpu.VMEM((sum(block.shape[0] for block in blocks), rows, half), BF16),
                pltpu.VMEM((pieces, width // n_ex // pieces, half), F32),
                pltpu.VMEM((own, rows * per_blk), F32),
                pltpu.SemaphoreType.DMA((pieces + 1,)),
            ],
            compiler_params=PARAMS,
            name="gram_and_scores",
        )(*blocks)

    in_specs = (
        P("lay", ("grp", "ex"), "sub"),
        P("lay", ("grp", "ex"), "sub"),
        P("lay", None, "sub"),
        P("lay", None, "sub"),
        P("lay", "ex", "sub"),
    )
    out_specs = (P(("grp", "lay"), "ex", "sub"), P(("grp", "ex"), ("lay", "sub")))
    return jax.shard_map(body, mesh=mesh, in_specs=in_specs, out_specs=out_specs, check_vma=False)
```

```python
import functools

import jax
import jax.numpy as jnp
from jax import lax
from jax.experimental import pallas as pl
from jax.experimental.pallas import tpu as pltpu
from jax.sharding import PartitionSpec as P

LEN = 64
AXES = ("ex", "lay", "sub")
F32, BF16 = jnp.float32, jnp.bfloat16
VMEM = pl.BlockSpec(memory_space=pltpu.VMEM)
ANY = pl.BlockSpec(memory_space=pl.ANY)
LAST = (((1,), (1,)), ((), ()))
FIRST = (((0,), (0,)), ((), ()))
DEAL = (
    (5, 7, 1, 3),
    (0, 5, 7, 3),
    (4, 6, 0, 3),
    (2, 4, 7, 0),
    (2, 5, 6, 1),
    (5, 6, 3, 0),
    (0, 5, 6, 2),
    (4, 6, 1, 3),
)
PARAMS = pltpu.CompilerParams(vmem_limit_bytes=16 * 1024 * 1024)


def picks_kernel(basis, pick_x_ref, pick_g_ref):
    rows, width = pick_g_ref.shape
    lanes, pair = pick_x_ref.shape[1], 2 * basis
    row = lax.broadcasted_iota(jnp.int32, (rows, lanes), 0) % pair
    col = lax.broadcasted_iota(jnp.int32, (rows, lanes), 1)
    pick_x_ref[...] = jnp.where(row == col % basis, 1.0, 0.0).astype(BF16)
    gap = row - basis - col // basis
    for j in range(width // lanes):
        pick_g_ref[:, j * lanes : (j + 1) * lanes] = jnp.where(gap == j * (lanes // basis), 1.0, 0.0).astype(BF16)


def chunk_kernel(in_ref, out_ref):
    out_ref[...] = in_ref[...]


def grads_kernel(n_sub, *refs):
    parts, (pick_x_ref, pick_g_ref, out_ref) = refs[:n_sub], refs[n_sub:]
    total = parts[0][...]
    for part in parts[1:]:
        total += part[...]
    high = total.astype(BF16).astype(F32)
    rest = total - high
    mid = rest.astype(BF16).astype(F32)
    low = rest - mid
    pieces = [jnp.concatenate([high, mid]).T, jnp.concatenate([low, jnp.zeros_like(low)]).T]
    pieces = jnp.concatenate(pieces, axis=1).astype(BF16)
    own = pieces.shape[0] // LEN
    lanes, width = pick_x_ref.shape[1], pick_g_ref.shape[1]
    tiled_x = jnp.dot(pieces, pick_x_ref[...], preferred_element_type=F32)
    tiles = []
    wide = 2 * lanes if width % (2 * lanes) == 0 else lanes
    tiled_x = jnp.concatenate([tiled_x] * (wide // lanes), axis=1)
    for j in range(width // wide):
        pick_g = pick_g_ref[:, j * wide : (j + 1) * wide]
        product = jnp.dot(pieces, pick_g, preferred_element_type=F32) * tiled_x
        tiles.append(product.reshape(own, LEN, wide).sum(axis=1))
    grads = jnp.concatenate(tiles, axis=1)
    high = grads.astype(BF16).astype(F32)
    low = grads - high
    half = width // n_sub
    rows = []
    for h in range(n_sub):
        cols = slice(h * half, (h + 1) * half)
        rows += [high[:, cols], low[:, cols]]
    out_ref[...] = jnp.concatenate(rows, axis=0).astype(BF16)


def swap_kernel(lacked, first_ref, second_ref, out_ref):
    second = lacked(lax.axis_index("ex"), lax.axis_index("lay"), lax.axis_index("sub")) == 1
    out_ref[0] = first_ref[0]
    out_ref[1] = second_ref[0]

    @pl.when(second)
    def _():
        out_ref[2:] = second_ref[1:]

    @pl.when(jnp.logical_not(second))
    def _():
        out_ref[2:] = first_ref[1:]


def final_kernel(plan, n_ex, n_sub, own, *refs):
    parts, (gram_ref, scores_ref, all_ref, gram_buf, scores_buf, sems) = refs[:-6], refs[-6:]
    start = 0
    for part in parts:
        all_ref[start : start + part.shape[0]] = part[...]
        start += part.shape[0]
    ex, lay, sub = lax.axis_index("ex"), lax.axis_index("lay"), lax.axis_index("sub")
    slots, layers, units = plan(ex, lay, sub)
    half = all_ref.shape[2]
    n_rows, per_half = half * n_sub // n_ex, n_ex // n_sub

    def halves_of(block):
        pieces = all_ref[block].astype(F32)
        return [pieces[h * 2 * own : (h + 1) * 2 * own] for h in range(n_sub)]

    def choose(values, index):
        result = values[0]
        for i in range(1, len(values)):
            result = jnp.where(index == i, values[i], result)
        return result

    lefts, rights = [], []
    for block in slots:
        halves = halves_of(block)
        cuts = [halves[e // per_half][:, e % per_half * n_rows : (e % per_half + 1) * n_rows] for e in range(n_ex)]
        left, right = choose(cuts, ex), choose(halves, sub)
        lefts += [left, pltpu.roll(left, own, 0)]
        rights += [right, right]
    left = jnp.concatenate(lefts, axis=0).astype(BF16)
    right = jnp.concatenate(rights, axis=0).astype(BF16)
    copies = []
    step = n_rows // gram_buf.shape[0]
    for at in range(gram_buf.shape[0]):
        rows = slice(at * step, (at + 1) * step)
        gram = lax.dot_general(left[:, rows], right, FIRST, preferred_element_type=F32)
        gram_buf[at] = gram * (1.0 / (own * n_ex))
        copies.append(pltpu.make_async_copy(gram_buf.at[at], gram_ref.at[0, rows, :], sems.at[at]))
        copies[-1].start()

    layers = [halves_of(block) for block in layers]
    blocks = {}
    for block, behind, core, column, fits in units:
        grads = [choose([halves[h] for halves in layers], behind) for h in range(n_sub)]
        part = 0.0
        for h in range(n_sub):
            turned = choose(grads, lax.rem(core + h + n_sub - 1, n_sub)).astype(BF16)
            part += lax.dot_general(turned, all_ref[block + h], LAST, preferred_element_type=F32)
        part = part[:own] + part[own:]
        part = part if fits is None else jnp.where(fits, part, 0.0)
        blocks[column] = blocks.get(column, 0.0) + part
    blocks = [blocks[column] for column in sorted(blocks)]
    scores_buf[...] = blocks[0] if len(blocks) == 1 else jnp.concatenate(blocks, axis=1)
    copies.append(pltpu.make_async_copy(scores_buf, scores_ref, sems.at[len(copies)]))
    copies[-1].start()
    for copy in copies:
        copy.wait()


def solution(mesh):
    n_ex, n_lay, n_sub = mesh.shape["ex"], mesh.shape["lay"], mesh.shape["sub"]
    group, per_blk = n_ex // n_lay, n_ex // (n_lay * n_sub)

    def flat(ex, lay, sub):
        return (ex * n_lay + lay) * n_sub + sub

    devices = [(ex, lay, sub) for ex in range(n_ex) for lay in range(n_lay) for sub in range(n_sub)]

    query_pairs = [
        (
            flat(ex, lay, sub),
            flat(ex % group * n_lay + (lay + n_lay - 1) % n_lay, ex // group, (sub + 1) % n_sub),
        )
        for ex, lay, sub in devices
    ]

    compact = (n_ex, n_lay, n_sub) == (4, 2, 2)
    moves = [("ex", k) for k in range(1, n_ex)] + [("lay", k) for k in range(1, n_lay)]
    rounds = -(-len(moves) // n_sub)

    def source_of(at, ex, lay, sub):
        if compact:
            row = DEAL[ex * n_lay + lay]
            kind = [value // 2 for value in row].index(2 * at + sub)
            sender = row[kind] % 2
            (axis, k) = ("ex", kind) if kind else ("lay", 1)
        else:
            sender = sub
            axis, k = moves[min(at * n_sub + sub, len(moves) - 1)]
        return flat((ex + k) % n_ex, lay, sender) if axis == "ex" else flat(ex, (lay + k) % n_lay, sender)

    def dealt(kind, ex, lay):
        values = [row[kind] for row in DEAL]
        result = values[0]
        for chip in range(1, len(values)):
            result = jnp.where(ex * n_lay + lay == chip, values[chip], result)
        return result // 4, result // 2 % 2, result % 2

    def unit_kinds(ex, lay):
        up, down = dealt(1, ex, lay), dealt(3, ex, lay)
        odd = ex % 2 == 1
        beside = [jnp.where(odd, b, a) for a, b in zip(up, down)]
        beyond = [jnp.where(odd, a, b) for a, b in zip(up, down)]
        return beside, dealt(2, ex, lay), beyond

    def lacked(ex, lay, sub):
        beside, across, beyond = unit_kinds(ex, lay)
        later = jnp.where(across[1] == sub, across[0], beyond[0])
        return jnp.where(ex // 2 == sub, later, beside[0])

    def compact_plan(ex, lay, sub):
        def grads_at(kind):
            turn, core, _ = dealt(kind, ex, lay)
            return jnp.where(sub == core, 3 + 3 * turn, 9 + turn)

        def unit_at(kind):
            turn, core, _ = kind
            return jnp.where(sub == core, 4 + 3 * turn, 11)

        slots = [0, grads_at(1), grads_at(2), grads_at(3)]
        layers = [0, grads_at(0)]
        beside, across, beyond = unit_kinds(ex, lay)
        mine = ex // 2 == sub
        first, first_core = jnp.where(mine, 1, unit_at(across)), jnp.where(mine, sub, across[2])
        second = jnp.where(mine, unit_at(beside), unit_at(beyond))
        second_core = jnp.where(mine, beside[2], beyond[2])
        units = [(first, (ex + 1 + lay) % 2, first_core, 0, None), (second, (ex + lay) % 2, second_core, 0, None)]
        return slots, layers, units

    def general_plan(ex, lay, sub):
        size = 1 + n_sub
        slots, layers, sources = [0], [0], [(ex, sub)]
        for at, (axis, k) in enumerate(moves):
            core, turn = at % n_sub, at // n_sub
            block = (1 + (core - sub + n_sub) % n_sub * rounds + turn) * size
            if axis == "ex":
                slots.append(block)
                sources.append(((ex + k) % n_ex, core))
            else:
                layers.append(block)
        units = []
        for block, (source, core) in zip(slots, sources):
            behind, row = (source % n_lay + 1 - lay + n_lay) % n_lay, source // n_lay
            for column in range(per_blk):
                units.append((block + 1, behind, core, column, row == sub * per_blk + column))
        return slots, layers, units

    def rotate(value, k):
        return lax.ppermute(value, "sub", [((i + k) % n_sub, i) for i in range(n_sub)])

    def body(layer_inputs, output_grads, basis_in, basis_out, queries):
        _, tokens, depth = layer_inputs.shape
        basis = basis_in.shape[1]
        own = tokens // LEN
        width = basis * basis
        rows, half = queries.shape[1:]

        chunk = lax.ppermute(queries[0], AXES, query_pairs)
        pick_x, pick_g = pl.pallas_call(
            functools.partial(picks_kernel, basis),
            out_shape=(
                jax.ShapeDtypeStruct((8 * basis, 4 * basis), BF16),
                jax.ShapeDtypeStruct((8 * basis, width), BF16),
            ),
            out_specs=(VMEM,) * 2,
            compiler_params=PARAMS,
            cost_estimate=pl.CostEstimate(flops=3 * 10**8, bytes_accessed=0, transcendentals=0),
            name="picks",
        )()
        basis_in, basis_out, pick_x = lax.optimization_barrier((basis_in, basis_out, pick_x))
        proj_x = lax.dot_general(basis_in[0], layer_inputs[0], LAST, preferred_element_type=F32)
        proj_g = lax.dot_general(basis_out[0], output_grads[0], LAST, preferred_element_type=F32)
        proj = jnp.concatenate([proj_x, proj_g])
        parts = [proj] + [rotate(proj, k) for k in range(1, n_sub)]
        chunk = pl.pallas_call(
            chunk_kernel,
            out_shape=jax.ShapeDtypeStruct((rows, half), BF16),
            in_specs=[VMEM],
            out_specs=VMEM,
            compiler_params=PARAMS,
            cost_estimate=pl.CostEstimate(flops=10**11, bytes_accessed=10**9, transcendentals=0),
            name="chunk",
        )(chunk)
        chunks = [chunk] + [rotate(chunk, k) for k in range(1, n_sub)]

        grads = pl.pallas_call(
            functools.partial(grads_kernel, n_sub),
            out_shape=jax.ShapeDtypeStruct((2 * own * n_sub, half), BF16),
            in_specs=[VMEM] * (n_sub + 2),
            out_specs=VMEM,
            compiler_params=PARAMS,
            name="grads",
        )(*parts, pick_x, pick_g)

        mine = jnp.stack([grads] + chunks)
        received = []
        for at in range(rounds):
            pairs = [(source_of(at, *device), flat(*device)) for device in devices]
            received.append(lax.ppermute(mine, AXES, pairs))
        if compact:
            swapped = pl.pallas_call(
                functools.partial(swap_kernel, lacked),
                out_shape=jax.ShapeDtypeStruct((4, rows, half), BF16),
                in_specs=[VMEM] * 2,
                out_specs=VMEM,
                compiler_params=PARAMS,
                name="swap",
            )(*received)
            blocks = [mine] + received + [rotate(swapped, 1)]
        else:
            both = jnp.concatenate(received)
            blocks = [mine, both] + [rotate(both, k) for k in range(1, n_sub)]

        pieces = 2 if width // n_ex % 256 == 0 else 1
        return pl.pallas_call(
            functools.partial(final_kernel, compact_plan if compact else general_plan, n_ex, n_sub, own),
            out_shape=(
                jax.ShapeDtypeStruct((1, width // n_ex, half), F32),
                jax.ShapeDtypeStruct((own, rows * per_blk), F32),
            ),
            in_specs=[VMEM] * len(blocks),
            out_specs=(ANY, ANY),
            scratch_shapes=[
                pltpu.VMEM((sum(block.shape[0] for block in blocks), rows, half), BF16),
                pltpu.VMEM((pieces, width // n_ex // pieces, half), F32),
                pltpu.VMEM((own, rows * per_blk), F32),
                pltpu.SemaphoreType.DMA((pieces + 1,)),
            ],
            compiler_params=PARAMS,
            name="gram_and_scores",
        )(*blocks)

    in_specs = (
        P("lay", ("grp", "ex"), "sub"),
        P("lay", ("grp", "ex"), "sub"),
        P("lay", None, "sub"),
        P("lay", None, "sub"),
        P("lay", "ex", "sub"),
    )
    out_specs = (P(("grp", "lay"), "ex", "sub"), P(("grp", "ex"), ("lay", "sub")))
    return jax.shard_map(body, mesh=mesh, in_specs=in_specs, out_specs=out_specs, check_vma=False)
```

```python
import functools

import jax
import jax.numpy as jnp
from jax import lax
from jax.experimental import pallas as pl
from jax.experimental.pallas import tpu as pltpu
from jax.sharding import PartitionSpec as P

LEN = 64
AXES = ("ex", "lay", "sub")
F32, BF16 = jnp.float32, jnp.bfloat16
VMEM = pl.BlockSpec(memory_space=pltpu.VMEM)
ANY = pl.BlockSpec(memory_space=pl.ANY)
LAST = (((1,), (1,)), ((), ()))
FIRST = (((0,), (0,)), ((), ()))
DEAL = (
    (5, 7, 1, 3),
    (0, 5, 7, 3),
    (4, 6, 0, 3),
    (2, 4, 7, 0),
    (2, 5, 6, 1),
    (5, 6, 3, 0),
    (0, 5, 6, 2),
    (4, 6, 1, 3),
)
PARAMS = pltpu.CompilerParams(vmem_limit_bytes=16 * 1024 * 1024)


def picks_kernel(basis, pick_x_ref, pick_g_ref):
    rows, width = pick_g_ref.shape
    lanes, pair = pick_x_ref.shape[1], 2 * basis
    row = lax.broadcasted_iota(jnp.int32, (rows, lanes), 0) % pair
    col = lax.broadcasted_iota(jnp.int32, (rows, lanes), 1)
    pick_x_ref[...] = jnp.where(row == col % basis, 1.0, 0.0).astype(BF16)
    gap = row - basis - col // basis
    for j in range(width // lanes):
        pick_g_ref[:, j * lanes : (j + 1) * lanes] = jnp.where(gap == j * (lanes // basis), 1.0, 0.0).astype(BF16)


def chunk_kernel(in_ref, out_ref):
    out_ref[...] = in_ref[...]


def grads_kernel(n_sub, *refs):
    parts, (pick_x_ref, pick_g_ref, out_ref) = refs[:n_sub], refs[n_sub:]
    total = parts[0][...]
    for part in parts[1:]:
        total += part[...]
    high = total.astype(BF16).astype(F32)
    rest = total - high
    mid = rest.astype(BF16).astype(F32)
    low = rest - mid
    pieces = [jnp.concatenate([high, mid]).T, jnp.concatenate([low, jnp.zeros_like(low)]).T]
    pieces = jnp.concatenate(pieces, axis=1).astype(BF16)
    own = pieces.shape[0] // LEN
    lanes, width = pick_x_ref.shape[1], pick_g_ref.shape[1]
    tiled_x = jnp.dot(pieces, pick_x_ref[...], preferred_element_type=F32)
    tiles = []
    wide = 2 * lanes if width % (2 * lanes) == 0 else lanes
    tiled_x = jnp.concatenate([tiled_x] * (wide // lanes), axis=1)
    for j in range(width // wide):
        pick_g = pick_g_ref[:, j * wide : (j + 1) * wide]
        product = jnp.dot(pieces, pick_g, preferred_element_type=F32) * tiled_x
        tiles.append(product.reshape(own, LEN, wide).sum(axis=1))
    grads = jnp.concatenate(tiles, axis=1)
    high = grads.astype(BF16).astype(F32)
    low = grads - high
    half = width // n_sub
    rows = []
    for h in range(n_sub):
        cols = slice(h * half, (h + 1) * half)
        rows += [high[:, cols], low[:, cols]]
    out_ref[...] = jnp.concatenate(rows, axis=0).astype(BF16)


def swap_kernel(lacked, first_ref, second_ref, out_ref):
    second = lacked(lax.axis_index("ex"), lax.axis_index("lay"), lax.axis_index("sub")) == 1
    out_ref[0] = first_ref[0]
    out_ref[1] = second_ref[0]

    @pl.when(second)
    def _():
        out_ref[2:] = second_ref[1:]

    @pl.when(jnp.logical_not(second))
    def _():
        out_ref[2:] = first_ref[1:]


def final_kernel(plan, n_ex, n_sub, own, *refs):
    parts, (gram_ref, scores_ref, all_ref, gram_buf, scores_buf, sems) = refs[:-6], refs[-6:]
    start = 0
    for part in parts:
        all_ref[start : start + part.shape[0]] = part[...]
        start += part.shape[0]
    ex, lay, sub = lax.axis_index("ex"), lax.axis_index("lay"), lax.axis_index("sub")
    slots, layers, units = plan(ex, lay, sub)
    half = all_ref.shape[2]
    n_rows, per_half = half * n_sub // n_ex, n_ex // n_sub

    def halves_of(block):
        pieces = all_ref[block].astype(F32)
        return [pieces[h * 2 * own : (h + 1) * 2 * own] for h in range(n_sub)]

    def choose(values, index):
        result = values[0]
        for i in range(1, len(values)):
            result = jnp.where(index == i, values[i], result)
        return result

    lefts, rights = [], []
    for block in slots:
        halves = halves_of(block)
        cuts = [halves[e // per_half][:, e % per_half * n_rows : (e % per_half + 1) * n_rows] for e in range(n_ex)]
        left, right = choose(cuts, ex), choose(halves, sub)
        lefts += [left, pltpu.roll(left, own, 0)]
        rights += [right, right]
    left = jnp.concatenate(lefts, axis=0).astype(BF16)
    right = jnp.concatenate(rights, axis=0).astype(BF16)
    copies = []
    _, tall, wide = gram_buf.shape
    for at in range(gram_buf.shape[0]):
        row, col = at // (half // wide) * tall, at % (half // wide) * wide
        gram = lax.dot_general(left[:, row : row + tall], right[:, col : col + wide], FIRST, preferred_element_type=F32)
        gram_buf[at] = gram * (1.0 / (own * n_ex))
        target = gram_ref.at[0, pl.ds(row, tall), pl.ds(col, wide)]
        copies.append(pltpu.make_async_copy(gram_buf.at[at], target, sems.at[at]))
        copies[-1].start()

    layers = [halves_of(block) for block in layers]
    blocks = {}
    for block, behind, core, column, fits in units:
        grads = [choose([halves[h] for halves in layers], behind) for h in range(n_sub)]
        part = 0.0
        for h in range(n_sub):
            turned = choose(grads, lax.rem(core + h + n_sub - 1, n_sub)).astype(BF16)
            part += lax.dot_general(turned, all_ref[block + h], LAST, preferred_element_type=F32)
        part = part[:own] + part[own:]
        part = part if fits is None else jnp.where(fits, part, 0.0)
        blocks[column] = blocks.get(column, 0.0) + part
    blocks = [blocks[column] for column in sorted(blocks)]
    scores_buf[...] = blocks[0] if len(blocks) == 1 else jnp.concatenate(blocks, axis=1)
    copies.append(pltpu.make_async_copy(scores_buf, scores_ref, sems.at[len(copies)]))
    copies[-1].start()
    for copy in copies:
        copy.wait()


def solution(mesh):
    n_ex, n_lay, n_sub = mesh.shape["ex"], mesh.shape["lay"], mesh.shape["sub"]
    group, per_blk = n_ex // n_lay, n_ex // (n_lay * n_sub)

    def flat(ex, lay, sub):
        return (ex * n_lay + lay) * n_sub + sub

    devices = [(ex, lay, sub) for ex in range(n_ex) for lay in range(n_lay) for sub in range(n_sub)]

    query_pairs = [
        (
            flat(ex, lay, sub),
            flat(ex % group * n_lay + (lay + n_lay - 1) % n_lay, ex // group, (sub + 1) % n_sub),
        )
        for ex, lay, sub in devices
    ]

    compact = (n_ex, n_lay, n_sub) == (4, 2, 2)
    moves = [("ex", k) for k in range(1, n_ex)] + [("lay", k) for k in range(1, n_lay)]
    rounds = -(-len(moves) // n_sub)

    def source_of(at, ex, lay, sub):
        if compact:
            row = DEAL[ex * n_lay + lay]
            kind = [value // 2 for value in row].index(2 * at + sub)
            sender = row[kind] % 2
            (axis, k) = ("ex", kind) if kind else ("lay", 1)
        else:
            sender = sub
            axis, k = moves[min(at * n_sub + sub, len(moves) - 1)]
        return flat((ex + k) % n_ex, lay, sender) if axis == "ex" else flat(ex, (lay + k) % n_lay, sender)

    def dealt(kind, ex, lay):
        values = [row[kind] for row in DEAL]
        result = values[0]
        for chip in range(1, len(values)):
            result = jnp.where(ex * n_lay + lay == chip, values[chip], result)
        return result // 4, result // 2 % 2, result % 2

    def unit_kinds(ex, lay):
        up, down = dealt(1, ex, lay), dealt(3, ex, lay)
        odd = ex % 2 == 1
        beside = [jnp.where(odd, b, a) for a, b in zip(up, down)]
        beyond = [jnp.where(odd, a, b) for a, b in zip(up, down)]
        return beside, dealt(2, ex, lay), beyond

    def lacked(ex, lay, sub):
        beside, across, beyond = unit_kinds(ex, lay)
        later = jnp.where(across[1] == sub, across[0], beyond[0])
        return jnp.where(ex // 2 == sub, later, beside[0])

    def compact_plan(ex, lay, sub):
        def grads_at(kind):
            turn, core, _ = dealt(kind, ex, lay)
            return jnp.where(sub == core, 3 + 3 * turn, 9 + turn)

        def unit_at(kind):
            turn, core, _ = kind
            return jnp.where(sub == core, 4 + 3 * turn, 11)

        slots = [0, grads_at(1), grads_at(2), grads_at(3)]
        layers = [0, grads_at(0)]
        beside, across, beyond = unit_kinds(ex, lay)
        mine = ex // 2 == sub
        first, first_core = jnp.where(mine, 1, unit_at(across)), jnp.where(mine, sub, across[2])
        second = jnp.where(mine, unit_at(beside), unit_at(beyond))
        second_core = jnp.where(mine, beside[2], beyond[2])
        units = [(first, (ex + 1 + lay) % 2, first_core, 0, None), (second, (ex + lay) % 2, second_core, 0, None)]
        return slots, layers, units

    def general_plan(ex, lay, sub):
        size = 1 + n_sub
        slots, layers, sources = [0], [0], [(ex, sub)]
        for at, (axis, k) in enumerate(moves):
            core, turn = at % n_sub, at // n_sub
            block = (1 + (core - sub + n_sub) % n_sub * rounds + turn) * size
            if axis == "ex":
                slots.append(block)
                sources.append(((ex + k) % n_ex, core))
            else:
                layers.append(block)
        units = []
        for block, (source, core) in zip(slots, sources):
            behind, row = (source % n_lay + 1 - lay + n_lay) % n_lay, source // n_lay
            for column in range(per_blk):
                units.append((block + 1, behind, core, column, row == sub * per_blk + column))
        return slots, layers, units

    def rotate(value, k):
        return lax.ppermute(value, "sub", [((i + k) % n_sub, i) for i in range(n_sub)])

    def body(layer_inputs, output_grads, basis_in, basis_out, queries):
        _, tokens, depth = layer_inputs.shape
        basis = basis_in.shape[1]
        own = tokens // LEN
        width = basis * basis
        rows, half = queries.shape[1:]

        chunk = lax.ppermute(queries[0], AXES, query_pairs)
        pick_x, pick_g = pl.pallas_call(
            functools.partial(picks_kernel, basis),
            out_shape=(
                jax.ShapeDtypeStruct((8 * basis, 4 * basis), BF16),
                jax.ShapeDtypeStruct((8 * basis, width), BF16),
            ),
            out_specs=(VMEM,) * 2,
            compiler_params=PARAMS,
            cost_estimate=pl.CostEstimate(flops=3 * 10**8, bytes_accessed=0, transcendentals=0),
            name="picks",
        )()
        basis_in, basis_out, pick_x = lax.optimization_barrier((basis_in, basis_out, pick_x))
        proj_x = lax.dot_general(basis_in[0], layer_inputs[0], LAST, preferred_element_type=F32)
        proj_g = lax.dot_general(basis_out[0], output_grads[0], LAST, preferred_element_type=F32)
        proj = jnp.concatenate([proj_x, proj_g])
        parts = [proj] + [rotate(proj, k) for k in range(1, n_sub)]
        chunk = pl.pallas_call(
            chunk_kernel,
            out_shape=jax.ShapeDtypeStruct((rows, half), BF16),
            in_specs=[VMEM],
            out_specs=VMEM,
            compiler_params=PARAMS,
            cost_estimate=pl.CostEstimate(flops=10**11, bytes_accessed=10**9, transcendentals=0),
            name="chunk",
        )(chunk)
        chunks = [chunk] + [rotate(chunk, k) for k in range(1, n_sub)]

        grads = pl.pallas_call(
            functools.partial(grads_kernel, n_sub),
            out_shape=jax.ShapeDtypeStruct((2 * own * n_sub, half), BF16),
            in_specs=[VMEM] * (n_sub + 2),
            out_specs=VMEM,
            compiler_params=PARAMS,
            name="grads",
        )(*parts, pick_x, pick_g)

        mine = jnp.stack([grads] + chunks)
        received = []
        for at in range(rounds):
            pairs = [(source_of(at, *device), flat(*device)) for device in devices]
            received.append(lax.ppermute(mine, AXES, pairs))
        if compact:
            swapped = pl.pallas_call(
                functools.partial(swap_kernel, lacked),
                out_shape=jax.ShapeDtypeStruct((4, rows, half), BF16),
                in_specs=[VMEM] * 2,
                out_specs=VMEM,
                compiler_params=PARAMS,
                name="swap",
            )(*received)
            blocks = [mine] + received + [rotate(swapped, 1)]
        else:
            both = jnp.concatenate(received)
            blocks = [mine, both] + [rotate(both, k) for k in range(1, n_sub)]

        tall = 128 if width // n_ex % 128 == 0 else width // n_ex
        wide = 256 if half % 256 == 0 else half
        pieces = width // n_ex // tall * (half // wide)
        return pl.pallas_call(
            functools.partial(final_kernel, compact_plan if compact else general_plan, n_ex, n_sub, own),
            out_shape=(
                jax.ShapeDtypeStruct((1, width // n_ex, half), F32),
                jax.ShapeDtypeStruct((own, rows * per_blk), F32),
            ),
            in_specs=[VMEM] * len(blocks),
            out_specs=(ANY, ANY),
            scratch_shapes=[
                pltpu.VMEM((sum(block.shape[0] for block in blocks), rows, half), BF16),
                pltpu.VMEM((pieces, tall, wide), F32),
                pltpu.VMEM((own, rows * per_blk), F32),
                pltpu.SemaphoreType.DMA((pieces + 1,)),
            ],
            compiler_params=PARAMS,
            name="gram_and_scores",
        )(*blocks)

    in_specs = (
        P("lay", ("grp", "ex"), "sub"),
        P("lay", ("grp", "ex"), "sub"),
        P("lay", None, "sub"),
        P("lay", None, "sub"),
        P("lay", "ex", "sub"),
    )
    out_specs = (P(("grp", "lay"), "ex", "sub"), P(("grp", "ex"), ("lay", "sub")))
    return jax.shard_map(body, mesh=mesh, in_specs=in_specs, out_specs=out_specs, check_vma=False)
```

```python
import functools

import jax
import jax.numpy as jnp
from jax import lax
from jax.experimental import pallas as pl
from jax.experimental.pallas import tpu as pltpu
from jax.sharding import PartitionSpec as P

LEN = 64
AXES = ("ex", "lay", "sub")
F32, BF16 = jnp.float32, jnp.bfloat16
VMEM = pl.BlockSpec(memory_space=pltpu.VMEM)
ANY = pl.BlockSpec(memory_space=pl.ANY)
LAST = (((1,), (1,)), ((), ()))
FIRST = (((0,), (0,)), ((), ()))
DEAL = (
    (5, 7, 1, 3),
    (0, 5, 7, 3),
    (3, 5, 7, 1),
    (1, 6, 4, 2),
    (2, 4, 6, 0),
    (4, 7, 3, 0),
    (2, 7, 4, 0),
    (2, 6, 4, 1),
)
PARAMS = pltpu.CompilerParams(vmem_limit_bytes=16 * 1024 * 1024)


def picks_kernel(basis, pick_x_ref, pick_g_ref):
    rows, width = pick_g_ref.shape
    lanes, pair = pick_x_ref.shape[1], 2 * basis
    row = lax.broadcasted_iota(jnp.int32, (rows, lanes), 0) % pair
    col = lax.broadcasted_iota(jnp.int32, (rows, lanes), 1)
    pick_x_ref[...] = jnp.where(row == col % basis, 1.0, 0.0).astype(BF16)
    gap = row - basis - col // basis
    for j in range(width // lanes):
        pick_g_ref[:, j * lanes : (j + 1) * lanes] = jnp.where(gap == j * (lanes // basis), 1.0, 0.0).astype(BF16)


def chunk_kernel(in_ref, out_ref):
    out_ref[...] = in_ref[...]


def grads_kernel(n_sub, *refs):
    parts, (pick_x_ref, pick_g_ref, out_ref) = refs[:n_sub], refs[n_sub:]
    total = parts[0][...]
    for part in parts[1:]:
        total += part[...]
    high = total.astype(BF16).astype(F32)
    rest = total - high
    mid = rest.astype(BF16).astype(F32)
    low = rest - mid
    pieces = [jnp.concatenate([high, mid]).T, jnp.concatenate([low, jnp.zeros_like(low)]).T]
    pieces = jnp.concatenate(pieces, axis=1).astype(BF16)
    own = pieces.shape[0] // LEN
    lanes, width = pick_x_ref.shape[1], pick_g_ref.shape[1]
    tiled_x = jnp.dot(pieces, pick_x_ref[...], preferred_element_type=F32)
    tiles = []
    wide = 2 * lanes if width % (2 * lanes) == 0 else lanes
    tiled_x = jnp.concatenate([tiled_x] * (wide // lanes), axis=1)
    for j in range(width // wide):
        pick_g = pick_g_ref[:, j * wide : (j + 1) * wide]
        product = jnp.dot(pieces, pick_g, preferred_element_type=F32) * tiled_x
        tiles.append(product.reshape(own, LEN, wide).sum(axis=1))
    grads = jnp.concatenate(tiles, axis=1)
    high = grads.astype(BF16).astype(F32)
    low = grads - high
    half = width // n_sub
    rows = []
    for h in range(n_sub):
        cols = slice(h * half, (h + 1) * half)
        rows += [high[:, cols], low[:, cols]]
    out_ref[...] = jnp.concatenate(rows, axis=0).astype(BF16)


def swap_kernel(lacked, first_ref, second_ref, out_ref):
    second = lacked(lax.axis_index("ex"), lax.axis_index("lay"), lax.axis_index("sub")) == 1
    out_ref[0] = first_ref[0]
    out_ref[1] = second_ref[0]

    @pl.when(second)
    def _():
        out_ref[2:] = second_ref[1:]

    @pl.when(jnp.logical_not(second))
    def _():
        out_ref[2:] = first_ref[1:]


def final_kernel(plan, n_ex, n_sub, own, *refs):
    parts, (gram_ref, scores_ref, all_ref, gram_buf, scores_buf, sems) = refs[:-6], refs[-6:]
    start = 0
    for part in parts:
        all_ref[start : start + part.shape[0]] = part[...]
        start += part.shape[0]
    ex, lay, sub = lax.axis_index("ex"), lax.axis_index("lay"), lax.axis_index("sub")
    slots, layers, units = plan(ex, lay, sub)
    half = all_ref.shape[2]
    n_rows, per_half = half * n_sub // n_ex, n_ex // n_sub

    def halves_of(block):
        pieces = all_ref[block].astype(F32)
        return [pieces[h * 2 * own : (h + 1) * 2 * own] for h in range(n_sub)]

    def choose(values, index):
        result = values[0]
        for i in range(1, len(values)):
            result = jnp.where(index == i, values[i], result)
        return result

    lefts, rights = [], []
    for block in slots:
        halves = halves_of(block)
        cuts = [halves[e // per_half][:, e % per_half * n_rows : (e % per_half + 1) * n_rows] for e in range(n_ex)]
        left, right = choose(cuts, ex), choose(halves, sub)
        lefts += [left, pltpu.roll(left, own, 0)]
        rights += [right, right]
    left = jnp.concatenate(lefts, axis=0).astype(BF16)
    right = jnp.concatenate(rights, axis=0).astype(BF16)
    copies = []
    step = n_rows // gram_buf.shape[0]
    for at in range(gram_buf.shape[0]):
        rows = slice(at * step, (at + 1) * step)
        gram = lax.dot_general(left[:, rows], right, FIRST, preferred_element_type=F32)
        gram_buf[at] = gram * (1.0 / (own * n_ex))
        copies.append(pltpu.make_async_copy(gram_buf.at[at], gram_ref.at[0, rows, :], sems.at[at]))
        copies[-1].start()

    layers = [halves_of(block) for block in layers]
    blocks = {}
    for block, behind, core, column, fits in units:
        grads = [choose([halves[h] for halves in layers], behind) for h in range(n_sub)]
        part = 0.0
        for h in range(n_sub):
            turned = choose(grads, lax.rem(core + h + n_sub - 1, n_sub)).astype(BF16)
            part += lax.dot_general(turned, all_ref[block + h], LAST, preferred_element_type=F32)
        part = part[:own] + part[own:]
        part = part if fits is None else jnp.where(fits, part, 0.0)
        blocks[column] = blocks.get(column, 0.0) + part
    blocks = [blocks[column] for column in sorted(blocks)]
    scores_buf[...] = blocks[0] if len(blocks) == 1 else jnp.concatenate(blocks, axis=1)
    copies.append(pltpu.make_async_copy(scores_buf, scores_ref, sems.at[len(copies)]))
    copies[-1].start()
    for copy in copies:
        copy.wait()


def solution(mesh):
    n_ex, n_lay, n_sub = mesh.shape["ex"], mesh.shape["lay"], mesh.shape["sub"]
    group, per_blk = n_ex // n_lay, n_ex // (n_lay * n_sub)

    def flat(ex, lay, sub):
        return (ex * n_lay + lay) * n_sub + sub

    devices = [(ex, lay, sub) for ex in range(n_ex) for lay in range(n_lay) for sub in range(n_sub)]

    query_pairs = [
        (
            flat(ex, lay, sub),
            flat(ex % group * n_lay + (lay + n_lay - 1) % n_lay, ex // group, (sub + 1) % n_sub),
        )
        for ex, lay, sub in devices
    ]

    compact = (n_ex, n_lay, n_sub) == (4, 2, 2)
    moves = [("ex", k) for k in range(1, n_ex)] + [("lay", k) for k in range(1, n_lay)]
    rounds = -(-len(moves) // n_sub)

    def source_of(at, ex, lay, sub):
        if compact:
            row = DEAL[ex * n_lay + lay]
            kind = [value // 2 for value in row].index(2 * at + sub)
            sender = row[kind] % 2
            (axis, k) = ("ex", kind) if kind else ("lay", 1)
        else:
            sender = sub
            axis, k = moves[min(at * n_sub + sub, len(moves) - 1)]
        return flat((ex + k) % n_ex, lay, sender) if axis == "ex" else flat(ex, (lay + k) % n_lay, sender)

    def dealt(kind, ex, lay):
        values = [row[kind] for row in DEAL]
        result = values[0]
        for chip in range(1, len(values)):
            result = jnp.where(ex * n_lay + lay == chip, values[chip], result)
        return result // 4, result // 2 % 2, result % 2

    def unit_kinds(ex, lay):
        up, down = dealt(1, ex, lay), dealt(3, ex, lay)
        odd = ex % 2 == 1
        beside = [jnp.where(odd, b, a) for a, b in zip(up, down)]
        beyond = [jnp.where(odd, a, b) for a, b in zip(up, down)]
        return beside, dealt(2, ex, lay), beyond

    def lacked(ex, lay, sub):
        beside, across, beyond = unit_kinds(ex, lay)
        later = jnp.where(across[1] == sub, across[0], beyond[0])
        return jnp.where(ex // 2 == sub, later, beside[0])

    def compact_plan(ex, lay, sub):
        def grads_at(kind):
            turn, core, _ = dealt(kind, ex, lay)
            return jnp.where(sub == core, 3 + 3 * turn, 9 + turn)

        def unit_at(kind):
            turn, core, _ = kind
            return jnp.where(sub == core, 4 + 3 * turn, 11)

        slots = [0, grads_at(1), grads_at(2), grads_at(3)]
        layers = [0, grads_at(0)]
        beside, across, beyond = unit_kinds(ex, lay)
        mine = ex // 2 == sub
        first, first_core = jnp.where(mine, 1, unit_at(across)), jnp.where(mine, sub, across[2])
        second = jnp.where(mine, unit_at(beside), unit_at(beyond))
        second_core = jnp.where(mine, beside[2], beyond[2])
        units = [(first, (ex + 1 + lay) % 2, first_core, 0, None), (second, (ex + lay) % 2, second_core, 0, None)]
        return slots, layers, units

    def general_plan(ex, lay, sub):
        size = 1 + n_sub
        slots, layers, sources = [0], [0], [(ex, sub)]
        for at, (axis, k) in enumerate(moves):
            core, turn = at % n_sub, at // n_sub
            block = (1 + (core - sub + n_sub) % n_sub * rounds + turn) * size
            if axis == "ex":
                slots.append(block)
                sources.append(((ex + k) % n_ex, core))
            else:
                layers.append(block)
        units = []
        for block, (source, core) in zip(slots, sources):
            behind, row = (source % n_lay + 1 - lay + n_lay) % n_lay, source // n_lay
            for column in range(per_blk):
                units.append((block + 1, behind, core, column, row == sub * per_blk + column))
        return slots, layers, units

    def rotate(value, k):
        return lax.ppermute(value, "sub", [((i + k) % n_sub, i) for i in range(n_sub)])

    def body(layer_inputs, output_grads, basis_in, basis_out, queries):
        _, tokens, depth = layer_inputs.shape
        basis = basis_in.shape[1]
        own = tokens // LEN
        width = basis * basis
        rows, half = queries.shape[1:]

        chunk = lax.ppermute(queries[0], AXES, query_pairs)
        pick_x, pick_g = pl.pallas_call(
            functools.partial(picks_kernel, basis),
            out_shape=(
                jax.ShapeDtypeStruct((8 * basis, 4 * basis), BF16),
                jax.ShapeDtypeStruct((8 * basis, width), BF16),
            ),
            out_specs=(VMEM,) * 2,
            compiler_params=PARAMS,
            cost_estimate=pl.CostEstimate(flops=3 * 10**8, bytes_accessed=0, transcendentals=0),
            name="picks",
        )()
        basis_in, basis_out, pick_x = lax.optimization_barrier((basis_in, basis_out, pick_x))
        proj_x = lax.dot_general(basis_in[0], layer_inputs[0], LAST, preferred_element_type=F32)
        proj_g = lax.dot_general(basis_out[0], output_grads[0], LAST, preferred_element_type=F32)
        proj = jnp.concatenate([proj_x, proj_g])
        parts = [proj] + [rotate(proj, k) for k in range(1, n_sub)]
        chunk = pl.pallas_call(
            chunk_kernel,
            out_shape=jax.ShapeDtypeStruct((rows, half), BF16),
            in_specs=[VMEM],
            out_specs=VMEM,
            compiler_params=PARAMS,
            cost_estimate=pl.CostEstimate(flops=10**11, bytes_accessed=10**9, transcendentals=0),
            name="chunk",
        )(chunk)
        chunks = [chunk] + [rotate(chunk, k) for k in range(1, n_sub)]

        grads = pl.pallas_call(
            functools.partial(grads_kernel, n_sub),
            out_shape=jax.ShapeDtypeStruct((2 * own * n_sub, half), BF16),
            in_specs=[VMEM] * (n_sub + 2),
            out_specs=VMEM,
            compiler_params=PARAMS,
            name="grads",
        )(*parts, pick_x, pick_g)

        mine = jnp.stack([grads] + chunks)
        received = []
        for at in range(rounds):
            pairs = [(source_of(at, *device), flat(*device)) for device in devices]
            received.append(lax.ppermute(mine, AXES, pairs))
        if compact:
            swapped = pl.pallas_call(
                functools.partial(swap_kernel, lacked),
                out_shape=jax.ShapeDtypeStruct((4, rows, half), BF16),
                in_specs=[VMEM] * 2,
                out_specs=VMEM,
                compiler_params=PARAMS,
                name="swap",
            )(*received)
            blocks = [mine] + received + [rotate(swapped, 1)]
        else:
            both = jnp.concatenate(received)
            blocks = [mine, both] + [rotate(both, k) for k in range(1, n_sub)]

        pieces = 2 if width // n_ex % 256 == 0 else 1
        return pl.pallas_call(
            functools.partial(final_kernel, compact_plan if compact else general_plan, n_ex, n_sub, own),
            out_shape=(
                jax.ShapeDtypeStruct((1, width // n_ex, half), F32),
                jax.ShapeDtypeStruct((own, rows * per_blk), F32),
            ),
            in_specs=[VMEM] * len(blocks),
            out_specs=(ANY, ANY),
            scratch_shapes=[
                pltpu.VMEM((sum(block.shape[0] for block in blocks), rows, half), BF16),
                pltpu.VMEM((pieces, width // n_ex // pieces, half), F32),
                pltpu.VMEM((own, rows * per_blk), F32),
                pltpu.SemaphoreType.DMA((pieces + 1,)),
            ],
            compiler_params=PARAMS,
            name="gram_and_scores",
        )(*blocks)

    in_specs = (
        P("lay", ("grp", "ex"), "sub"),
        P("lay", ("grp", "ex"), "sub"),
        P("lay", None, "sub"),
        P("lay", None, "sub"),
        P("lay", "ex", "sub"),
    )
    out_specs = (P(("grp", "lay"), "ex", "sub"), P(("grp", "ex"), ("lay", "sub")))
    return jax.shard_map(body, mesh=mesh, in_specs=in_specs, out_specs=out_specs, check_vma=False)
```

```python
import functools

import jax
import jax.numpy as jnp
from jax import lax
from jax.experimental import pallas as pl
from jax.experimental.pallas import tpu as pltpu
from jax.sharding import PartitionSpec as P

LEN = 64
AXES = ("ex", "lay", "sub")
F32, BF16 = jnp.float32, jnp.bfloat16
VMEM = pl.BlockSpec(memory_space=pltpu.VMEM)
ANY = pl.BlockSpec(memory_space=pl.ANY)
LAST = (((1,), (1,)), ((), ()))
FIRST = (((0,), (0,)), ((), ()))
DEAL = (
    (5, 7, 1, 3),
    (0, 5, 7, 3),
    (1, 5, 7, 3),
    (1, 6, 4, 3),
    (3, 4, 6, 0),
    (4, 7, 2, 0),
    (2, 7, 4, 0),
    (2, 6, 4, 0),
)
PARAMS = pltpu.CompilerParams(vmem_limit_bytes=16 * 1024 * 1024)


def picks_kernel(basis, pick_x_ref, pick_g_ref):
    rows, width = pick_g_ref.shape
    lanes, pair = pick_x_ref.shape[1], 2 * basis
    row = lax.broadcasted_iota(jnp.int32, (rows, lanes), 0) % pair
    col = lax.broadcasted_iota(jnp.int32, (rows, lanes), 1)
    pick_x_ref[...] = jnp.where(row == col % basis, 1.0, 0.0).astype(BF16)
    gap = row - basis - col // basis
    for j in range(width // lanes):
        pick_g_ref[:, j * lanes : (j + 1) * lanes] = jnp.where(gap == j * (lanes // basis), 1.0, 0.0).astype(BF16)


def chunk_kernel(in_ref, out_ref):
    out_ref[...] = in_ref[...]


def grads_kernel(n_sub, *refs):
    parts, (pick_x_ref, pick_g_ref, out_ref) = refs[:n_sub], refs[n_sub:]
    total = parts[0][...]
    for part in parts[1:]:
        total += part[...]
    high = total.astype(BF16).astype(F32)
    rest = total - high
    mid = rest.astype(BF16).astype(F32)
    low = rest - mid
    pieces = [jnp.concatenate([high, mid]).T, jnp.concatenate([low, jnp.zeros_like(low)]).T]
    pieces = jnp.concatenate(pieces, axis=1).astype(BF16)
    own = pieces.shape[0] // LEN
    lanes, width = pick_x_ref.shape[1], pick_g_ref.shape[1]
    tiled_x = jnp.dot(pieces, pick_x_ref[...], preferred_element_type=F32)
    tiles = []
    wide = 2 * lanes if width % (2 * lanes) == 0 else lanes
    tiled_x = jnp.concatenate([tiled_x] * (wide // lanes), axis=1)
    for j in range(width // wide):
        pick_g = pick_g_ref[:, j * wide : (j + 1) * wide]
        product = jnp.dot(pieces, pick_g, preferred_element_type=F32) * tiled_x
        tiles.append(product.reshape(own, LEN, wide).sum(axis=1))
    grads = jnp.concatenate(tiles, axis=1)
    high = grads.astype(BF16).astype(F32)
    low = grads - high
    half = width // n_sub
    rows = []
    for h in range(n_sub):
        cols = slice(h * half, (h + 1) * half)
        rows += [high[:, cols], low[:, cols]]
    out_ref[...] = jnp.concatenate(rows, axis=0).astype(BF16)


def swap_kernel(lacked, first_ref, second_ref, out_ref):
    second = lacked(lax.axis_index("ex"), lax.axis_index("lay"), lax.axis_index("sub")) == 1
    out_ref[0] = first_ref[0]
    out_ref[1] = second_ref[0]

    @pl.when(second)
    def _():
        out_ref[2:] = second_ref[1:]

    @pl.when(jnp.logical_not(second))
    def _():
        out_ref[2:] = first_ref[1:]


def final_kernel(plan, n_ex, n_sub, own, *refs):
    parts, (gram_ref, scores_ref, all_ref, gram_buf, scores_buf, sems) = refs[:-6], refs[-6:]
    start = 0
    for part in parts:
        all_ref[start : start + part.shape[0]] = part[...]
        start += part.shape[0]
    ex, lay, sub = lax.axis_index("ex"), lax.axis_index("lay"), lax.axis_index("sub")
    slots, layers, units = plan(ex, lay, sub)
    half = all_ref.shape[2]
    n_rows, per_half = half * n_sub // n_ex, n_ex // n_sub

    def halves_of(block):
        pieces = all_ref[block].astype(F32)
        return [pieces[h * 2 * own : (h + 1) * 2 * own] for h in range(n_sub)]

    def choose(values, index):
        result = values[0]
        for i in range(1, len(values)):
            result = jnp.where(index == i, values[i], result)
        return result

    lefts, rights = [], []
    for block in slots:
        halves = halves_of(block)
        cuts = [halves[e // per_half][:, e % per_half * n_rows : (e % per_half + 1) * n_rows] for e in range(n_ex)]
        left, right = choose(cuts, ex), choose(halves, sub)
        lefts += [left, pltpu.roll(left, own, 0)]
        rights += [right, right]
    left = jnp.concatenate(lefts, axis=0).astype(BF16)
    right = jnp.concatenate(rights, axis=0).astype(BF16)
    copies = []
    step = n_rows // gram_buf.shape[0]
    for at in range(gram_buf.shape[0]):
        rows = slice(at * step, (at + 1) * step)
        gram = lax.dot_general(left[:, rows], right, FIRST, preferred_element_type=F32)
        gram_buf[at] = gram * (1.0 / (own * n_ex))
        copies.append(pltpu.make_async_copy(gram_buf.at[at], gram_ref.at[0, rows, :], sems.at[at]))
        copies[-1].start()

    layers = [halves_of(block) for block in layers]
    blocks = {}
    for block, behind, core, column, fits in units:
        grads = [choose([halves[h] for halves in layers], behind) for h in range(n_sub)]
        part = 0.0
        for h in range(n_sub):
            turned = choose(grads, lax.rem(core + h + n_sub - 1, n_sub)).astype(BF16)
            part += lax.dot_general(turned, all_ref[block + h], LAST, preferred_element_type=F32)
        part = part[:own] + part[own:]
        part = part if fits is None else jnp.where(fits, part, 0.0)
        blocks[column] = blocks.get(column, 0.0) + part
    blocks = [blocks[column] for column in sorted(blocks)]
    scores_buf[...] = blocks[0] if len(blocks) == 1 else jnp.concatenate(blocks, axis=1)
    copies.append(pltpu.make_async_copy(scores_buf, scores_ref, sems.at[len(copies)]))
    copies[-1].start()
    for copy in copies:
        copy.wait()


def solution(mesh):
    n_ex, n_lay, n_sub = mesh.shape["ex"], mesh.shape["lay"], mesh.shape["sub"]
    group, per_blk = n_ex // n_lay, n_ex // (n_lay * n_sub)

    def flat(ex, lay, sub):
        return (ex * n_lay + lay) * n_sub + sub

    devices = [(ex, lay, sub) for ex in range(n_ex) for lay in range(n_lay) for sub in range(n_sub)]

    query_pairs = [
        (
            flat(ex, lay, sub),
            flat(ex % group * n_lay + (lay + n_lay - 1) % n_lay, ex // group, (sub + 1) % n_sub),
        )
        for ex, lay, sub in devices
    ]

    compact = (n_ex, n_lay, n_sub) == (4, 2, 2)
    moves = [("ex", k) for k in range(1, n_ex)] + [("lay", k) for k in range(1, n_lay)]
    rounds = -(-len(moves) // n_sub)

    def source_of(at, ex, lay, sub):
        if compact:
            row = DEAL[ex * n_lay + lay]
            kind = [value // 2 for value in row].index(2 * at + sub)
            sender = row[kind] % 2
            (axis, k) = ("ex", kind) if kind else ("lay", 1)
        else:
            sender = sub
            axis, k = moves[min(at * n_sub + sub, len(moves) - 1)]
        return flat((ex + k) % n_ex, lay, sender) if axis == "ex" else flat(ex, (lay + k) % n_lay, sender)

    def dealt(kind, ex, lay):
        values = [row[kind] for row in DEAL]
        result = values[0]
        for chip in range(1, len(values)):
            result = jnp.where(ex * n_lay + lay == chip, values[chip], result)
        return result // 4, result // 2 % 2, result % 2

    def unit_kinds(ex, lay):
        up, down = dealt(1, ex, lay), dealt(3, ex, lay)
        odd = ex % 2 == 1
        beside = [jnp.where(odd, b, a) for a, b in zip(up, down)]
        beyond = [jnp.where(odd, a, b) for a, b in zip(up, down)]
        return beside, dealt(2, ex, lay), beyond

    def lacked(ex, lay, sub):
        beside, across, beyond = unit_kinds(ex, lay)
        later = jnp.where(across[1] == sub, across[0], beyond[0])
        return jnp.where(ex // 2 == sub, later, beside[0])

    def compact_plan(ex, lay, sub):
        def grads_at(kind):
            turn, core, _ = dealt(kind, ex, lay)
            return jnp.where(sub == core, 3 + 3 * turn, 9 + turn)

        def unit_at(kind):
            turn, core, _ = kind
            return jnp.where(sub == core, 4 + 3 * turn, 11)

        slots = [0, grads_at(1), grads_at(2), grads_at(3)]
        layers = [0, grads_at(0)]
        beside, across, beyond = unit_kinds(ex, lay)
        mine = ex // 2 == sub
        first, first_core = jnp.where(mine, 1, unit_at(across)), jnp.where(mine, sub, across[2])
        second = jnp.where(mine, unit_at(beside), unit_at(beyond))
        second_core = jnp.where(mine, beside[2], beyond[2])
        units = [(first, (ex + 1 + lay) % 2, first_core, 0, None), (second, (ex + lay) % 2, second_core, 0, None)]
        return slots, layers, units

    def general_plan(ex, lay, sub):
        size = 1 + n_sub
        slots, layers, sources = [0], [0], [(ex, sub)]
        for at, (axis, k) in enumerate(moves):
            core, turn = at % n_sub, at // n_sub
            block = (1 + (core - sub + n_sub) % n_sub * rounds + turn) * size
            if axis == "ex":
                slots.append(block)
                sources.append(((ex + k) % n_ex, core))
            else:
                layers.append(block)
        units = []
        for block, (source, core) in zip(slots, sources):
            behind, row = (source % n_lay + 1 - lay + n_lay) % n_lay, source // n_lay
            for column in range(per_blk):
                units.append((block + 1, behind, core, column, row == sub * per_blk + column))
        return slots, layers, units

    def rotate(value, k):
        return lax.ppermute(value, "sub", [((i + k) % n_sub, i) for i in range(n_sub)])

    def body(layer_inputs, output_grads, basis_in, basis_out, queries):
        _, tokens, depth = layer_inputs.shape
        basis = basis_in.shape[1]
        own = tokens // LEN
        width = basis * basis
        rows, half = queries.shape[1:]

        chunk = lax.ppermute(queries[0], AXES, query_pairs)
        pick_x, pick_g = pl.pallas_call(
            functools.partial(picks_kernel, basis),
            out_shape=(
                jax.ShapeDtypeStruct((8 * basis, 4 * basis), BF16),
                jax.ShapeDtypeStruct((8 * basis, width), BF16),
            ),
            out_specs=(VMEM,) * 2,
            compiler_params=PARAMS,
            cost_estimate=pl.CostEstimate(flops=3 * 10**8, bytes_accessed=0, transcendentals=0),
            name="picks",
        )()
        basis_in, basis_out, pick_x = lax.optimization_barrier((basis_in, basis_out, pick_x))
        proj_x = lax.dot_general(basis_in[0], layer_inputs[0], LAST, preferred_element_type=F32)
        proj_g = lax.dot_general(basis_out[0], output_grads[0], LAST, preferred_element_type=F32)
        proj = jnp.concatenate([proj_x, proj_g])
        parts = [proj] + [rotate(proj, k) for k in range(1, n_sub)]
        chunk = pl.pallas_call(
            chunk_kernel,
            out_shape=jax.ShapeDtypeStruct((rows, half), BF16),
            in_specs=[VMEM],
            out_specs=VMEM,
            compiler_params=PARAMS,
            cost_estimate=pl.CostEstimate(flops=10**11, bytes_accessed=10**9, transcendentals=0),
            name="chunk",
        )(chunk)
        chunks = [chunk] + [rotate(chunk, k) for k in range(1, n_sub)]

        grads = pl.pallas_call(
            functools.partial(grads_kernel, n_sub),
            out_shape=jax.ShapeDtypeStruct((2 * own * n_sub, half), BF16),
            in_specs=[VMEM] * (n_sub + 2),
            out_specs=VMEM,
            compiler_params=PARAMS,
            name="grads",
        )(*parts, pick_x, pick_g)

        mine = jnp.stack([grads] + chunks)
        received = []
        for at in range(rounds):
            pairs = [(source_of(at, *device), flat(*device)) for device in devices]
            received.append(lax.ppermute(mine, AXES, pairs))
        if compact:
            swapped = pl.pallas_call(
                functools.partial(swap_kernel, lacked),
                out_shape=jax.ShapeDtypeStruct((4, rows, half), BF16),
                in_specs=[VMEM] * 2,
                out_specs=VMEM,
                compiler_params=PARAMS,
                name="swap",
            )(*received)
            blocks = [mine] + received + [rotate(swapped, 1)]
        else:
            both = jnp.concatenate(received)
            blocks = [mine, both] + [rotate(both, k) for k in range(1, n_sub)]

        pieces = 2 if width // n_ex % 256 == 0 else 1
        return pl.pallas_call(
            functools.partial(final_kernel, compact_plan if compact else general_plan, n_ex, n_sub, own),
            out_shape=(
                jax.ShapeDtypeStruct((1, width // n_ex, half), F32),
                jax.ShapeDtypeStruct((own, rows * per_blk), F32),
            ),
            in_specs=[VMEM] * len(blocks),
            out_specs=(ANY, ANY),
            scratch_shapes=[
                pltpu.VMEM((sum(block.shape[0] for block in blocks), rows, half), BF16),
                pltpu.VMEM((pieces, width // n_ex // pieces, half), F32),
                pltpu.VMEM((own, rows * per_blk), F32),
                pltpu.SemaphoreType.DMA((pieces + 1,)),
            ],
            compiler_params=PARAMS,
            name="gram_and_scores",
        )(*blocks)

    in_specs = (
        P("lay", ("grp", "ex"), "sub"),
        P("lay", ("grp", "ex"), "sub"),
        P("lay", None, "sub"),
        P("lay", None, "sub"),
        P("lay", "ex", "sub"),
    )
    out_specs = (P(("grp", "lay"), "ex", "sub"), P(("grp", "ex"), ("lay", "sub")))
    return jax.shard_map(body, mesh=mesh, in_specs=in_specs, out_specs=out_specs, check_vma=False)
```
